128 devices in a mesh: dp: 8 (over z, y_hi), seq: 16 (over y_lo, x, core).
Axes of the slice: x: 4, y: 4 (y_hi: 2, y_lo: 2; y = y_hi * 2 + y_lo), z: 4, core: 2. Of those that a mesh axis runs over, the one named last changes fastest.
Arguments:
- latents: bfloat16 [8, 16, 512, 1152], P('dp', 'seq'), may hold values from -6 to 6
- modulation: float32 [8, 2, 3, 1152], P('dp'), may hold values from -3 to 3
- spatial_qkv: bfloat16 [1152, 1728], replicated, may hold values from -2.5 to 2.5
- spatial_out: bfloat16 [576, 1152], replicated, may hold values from -0.25 to 0.25
- temporal_qkv: bfloat16 [1152, 1728], replicated, may hold values from -2.5 to 2.5
- temporal_out: bfloat16 [576, 1152], replicated, may hold values from -0.25 to 0.25
- cotangent: bfloat16 [8, 16, 512, 1152], P('dp', None, 'seq'), may hold values from -6 to 6
Outputs:
- block_output: bfloat16 [8, 16, 512, 1152], P('dp', None, 'seq')
- latent_grad: bfloat16 [8, 16, 512, 1152], P('dp', 'seq')
- grad_spatial_qkv: float32 [1152, 1728], P(('dp', 'seq'))
- grad_spatial_out: float32 [576, 1152], P(None, ('dp', 'seq'))
- grad_temporal_qkv: float32 [1152, 1728], P(('dp', 'seq'))
- grad_temporal_out: float32 [576, 1152], P(None, ('dp', 'seq'))
The draws below stay inside these ranges and needn't reach their ends.
All inputs are finite; a program needn't handle non-finite values.
Results may differ from the reference program's by a relative error of at most 0.015.
Values may be sent and summed in bfloat16 or wider, within the bound.
A program may use at most 192 MiB of HBM per device.

```python
import jax
import jax.numpy as jnp
from jax import lax

D = 1152
HEADS = 8
HEAD = 72
HD = 576
FRAMES = 16
POS = 512
VIDEOS = 8


def projection_draw(key):
    base = jnp.clip(jax.random.normal(key, (D, 3 * HD), jnp.float32), -6.0, 6.0) * D ** (-0.5)
    return base.astype(jnp.bfloat16)


def draw_spatial_qkv(key, part):
    key = jax.random.fold_in(key, 5)
    return projection_draw(key)


def draw_temporal_qkv(key, part):
    key = jax.random.fold_in(key, 7)
    return projection_draw(key)


def block_levels(stream_key, extent, shards, least, top_value):
    loudness = 1.0
    for position, blocks in shards:
        heights = jax.random.uniform(jax.random.fold_in(jax.random.fold_in(stream_key, 6), position), (blocks,), jnp.float32, least / len(shards), top_value / len(shards))
        loudness = loudness * jnp.repeat(jnp.exp(heights), extent[position] // blocks).reshape((-1,) + (1,) * (len(extent) - 1 - position))
    return loudness


def bell_draw(own_key, extent, scale, reach, shards=(), kind=jnp.bfloat16):
    entries = jax.random.normal(own_key, extent, jnp.float32) * scale
    if len(shards) > 0:
        entries = block_levels(own_key, extent, shards, -0.22, 0.18) * entries
    return jnp.clip(entries, min=-reach, max=reach).astype(kind)


def setup_inputs(seed: int = 0) -> dict:
    key_of = jax.random.split(jax.random.key(seed), 8)
    return {
        "latents": bell_draw(key_of[0], (VIDEOS, FRAMES, POS, D), 1.0, 6.0, ((0, 8), (1, 16))),
        "modulation": bell_draw(key_of[1], (VIDEOS, 2, 3, D), 0.5, 3.0, ((0, 8),), jnp.float32),
        "spatial_qkv": draw_spatial_qkv(jax.random.fold_in(key_of[7], 71), 0),
        "spatial_out": bell_draw(key_of[3], (HD, D), HD ** -0.5, 0.25),
        "temporal_qkv": draw_temporal_qkv(jax.random.fold_in(key_of[7], 71), 0),
        "temporal_out": bell_draw(key_of[5], (HD, D), HD ** -0.5, 0.25),
        "cotangent": bell_draw(key_of[6], (VIDEOS, FRAMES, POS, D), 1.0, 6.0, ((0, 8), (2, 16))),
    }


def modulate(stream, shift, scale):
    centre = lax.optimization_barrier(jnp.mean(stream, -1, keepdims=True))
    centred = stream - centre
    spread = lax.optimization_barrier(jnp.mean(centred * centred, -1, keepdims=True))
    return centred * lax.rsqrt(spread + 1e-06) * (1.0 + scale) + shift

def attend(qkv, seq_first):
    first_len = qkv.shape[0]
    second_len = qkv.shape[1]
    pieces = qkv.reshape(first_len, second_len, 3, HEADS, HEAD).astype(jnp.float32)
    queries = pieces[:, :, 0]
    key_rows = pieces[:, :, 1]
    values = pieces[:, :, 2]
    if seq_first:
        score_form = 'lbhe,mbhe->bhlm'
        mix_form = 'bhlm,mbhe->lbhe'
    else:
        score_form = 'blhe,bmhe->bhlm'
        mix_form = 'bhlm,bmhe->blhe'
    scores = jnp.einsum(score_form, queries, key_rows) * HEAD ** (-0.5)
    largest = lax.optimization_barrier(jnp.max(scores, -1, keepdims=True))
    expo = jnp.exp(scores - largest)
    attn_probs = (expo / lax.optimization_barrier(jnp.sum(expo, -1, keepdims=True))).astype(jnp.bfloat16)
    attended = jnp.einsum(mix_form, attn_probs.astype(jnp.float32), values)
    return attended.reshape(first_len, second_len, HD).astype(jnp.bfloat16)

def forward_block(stream, styles, qkv_weight, out_weight, seq_first):
    widened = stream.astype(jnp.float32)
    normed = modulate(widened, styles[0], styles[1]).astype(jnp.bfloat16)
    qkv = jnp.dot(normed, qkv_weight, preferred_element_type=jnp.float32).astype(jnp.bfloat16)
    attended = attend(qkv, seq_first)
    projected = jnp.dot(attended, out_weight, preferred_element_type=jnp.float32)
    result = (widened + styles[2] * projected).astype(jnp.bfloat16)
    return (result, (normed, qkv, attended))

def backward_block(stream, styles, qkv_weight, out_weight, seq_first, stored, grad_result):
    normed, qkv, attended = stored
    wide_grad = grad_result.astype(jnp.float32)
    proj_grad = (styles[2] * wide_grad).astype(jnp.bfloat16)
    width = proj_grad.shape[-1]
    out_grad = lax.dot_general(attended.reshape(-1, attended.shape[-1]), proj_grad.reshape(-1, width), (((0,), (0,)), ((), ())), preferred_element_type=jnp.float32)
    attended_grad = lax.dot_general(proj_grad, out_weight, (((2,), (1,)), ((), ())), preferred_element_type=jnp.float32).astype(jnp.bfloat16)
    _, pull_back = jax.vjp(lambda operand: attend(operand, seq_first), qkv)
    qkv_grad = pull_back(attended_grad)[0]
    qkv_wgrad = lax.dot_general(normed.reshape(-1, width), qkv_grad.reshape(-1, qkv_grad.shape[-1]), (((0,), (0,)), ((), ())), preferred_element_type=jnp.float32)
    normed_grad = lax.dot_general(qkv_grad, qkv_weight, (((2,), (1,)), ((), ())), preferred_element_type=jnp.float32)
    _, pull_norm = jax.vjp(lambda operand: modulate(operand, styles[0], styles[1]), stream.astype(jnp.float32))
    input_grad = (pull_norm(normed_grad)[0] + wide_grad).astype(jnp.bfloat16)
    return (input_grad, qkv_wgrad, out_grad)

def reference(latents, modulation, spatial_qkv, spatial_out, temporal_qkv, temporal_out, cotangent):

    def one_video(totals, inputs):
        frames, styles, grad_mixed = inputs
        space_result, space_stored = forward_block(frames, styles[0], spatial_qkv, spatial_out, False)
        time_result, time_stored = forward_block(space_result, styles[1], temporal_qkv, temporal_out, True)
        space_grad, time_qkv, time_outg = backward_block(space_result, styles[1], temporal_qkv, temporal_out, True, time_stored, grad_mixed)
        frame_grad, space_qkv, space_outg = backward_block(frames, styles[0], spatial_qkv, spatial_out, False, space_stored, space_grad)
        totals = (totals[0] + space_qkv, totals[1] + space_outg, totals[2] + time_qkv, totals[3] + time_outg)
        return (totals, (time_result, frame_grad))
    one_video = jax.checkpoint(one_video)
    start = (jnp.zeros((D, 3 * HD), jnp.float32), jnp.zeros((HD, D), jnp.float32), jnp.zeros((D, 3 * HD), jnp.float32), jnp.zeros((HD, D), jnp.float32))
    totals, outputs = lax.scan(one_video, start, (latents, modulation, cotangent))
    return (outputs[0], outputs[1], totals[0], totals[1], totals[2], totals[3])
```

```python
import functools
import math

import jax
import jax.numpy as jnp
from jax import lax
from jax.experimental import pallas as pl
from jax.experimental.pallas import tpu as pltpu
from jax.sharding import PartitionSpec as P

D = 1152
HEADS = 8
HEAD = 72
HD = 576
QKV = 3 * HD
FRAMES = 16
POS = 512
SPAN = 32
TOK = 512
SCALE = HEAD ** (-0.5)
EXP2 = SCALE / math.log(2.0)
MESH = pl.DeviceIdType.MESH
BF = jnp.bfloat16
F32 = jnp.float32
PIECES = 6
WIDE = 384

NN = (((1,), (0,)), ((), ()))
NT = (((1,), (1,)), ((), ()))
TN = (((0,), (0,)), ((), ()))


def mm(a, b, form=NN):
    return lax.dot_general(a, b, form, preferred_element_type=F32)


def vmem_spec():
    return pl.BlockSpec(memory_space=pltpu.VMEM)


def any_spec():
    return pl.BlockSpec(memory_space=pl.ANY)


def standardise(x):
    centre = jnp.mean(x, -1, keepdims=True)
    centred = x - centre
    spread = jnp.mean(centred * centred, -1, keepdims=True)
    rstd = lax.rsqrt(spread + 1e-06)
    return centred * rstd, rstd


def norm_backward(x, dnormed, scale):
    xhat, rstd = standardise(x)
    dxhat = dnormed * (1.0 + scale)
    first = jnp.mean(dxhat, -1, keepdims=True)
    second = jnp.mean(dxhat * xhat, -1, keepdims=True)
    return rstd * (dxhat - first - xhat * second)


def softmax(scores, mask=None):
    if mask is not None:
        scores = jnp.where(mask, scores, -1e30)
    largest = jnp.max(scores, -1, keepdims=True)
    expo = jnp.exp2((scores - largest) * EXP2)
    return expo * (1.0 / jnp.sum(expo, -1, keepdims=True))


def head(ref_or_val, part, h):
    lo = part * HD + h * HEAD
    return ref_or_val[:, lo : lo + HEAD]


def score_backward(p, dp):
    wide = p.astype(F32)
    delta = jnp.sum(dp * wide, -1, keepdims=True)
    return (wide * (dp - delta) * SCALE).astype(BF)


def weight_grads(normed, dqkv, dproj, att, g):
    for lo in range(0, D, 384):
        rows = slice(lo, lo + 384)
        left = normed[:, rows]
        for n in (0, 2):
            both = mm(left, dqkv[:, n * WIDE : (n + 2) * WIDE], TN)
            g[n, rows, :] = both[:, :WIDE].astype(BF)
            g[n + 1, rows, :] = both[:, WIDE:].astype(BF)
        last = mm(left, dqkv[:, 4 * WIDE :], TN)
        outs = mm(dproj[:, rows], att[...], TN)
        g[4, rows, :192] = last.astype(BF)
        g[4, rows, 192:] = outs[:, :192].astype(BF)
        g[5, rows, :] = outs[:, 192:].astype(BF)


def spatial_forward(lat, mod, wq, normed, qkv, probs, att):
    shift, scale = mod[0, 0:1, :], mod[0, 1:2, :]
    for lo in range(0, TOK, 256):
        rows = slice(lo, lo + 256)
        xhat, _ = standardise(lat[rows, :].astype(F32))
        n = (xhat * (1.0 + scale) + shift).astype(BF)
        normed[rows, :] = n
        qkv[rows, :] = mm(n, wq[...]).astype(BF)


def spatial_head(h, qkv, probs, att):
    keys, values = head(qkv, 1, h), head(qkv, 2, h)
    for lo in range(0, TOK, 256):
        rows = slice(lo, lo + 256)
        q = qkv[rows, h * HEAD : (h + 1) * HEAD]
        p = softmax(mm(q, keys, NT)).astype(BF)
        probs[h, rows, :] = p
        att[rows, h * HEAD : (h + 1) * HEAD] = mm(p, values).astype(BF)


def spatial_backward(lat, mod, normed, qkv, probs, att, wq, wo, dmid, lat_grad, g, dproj, datt, dqkv, ds):
    scale, gate = mod[0, 1:2, :], mod[0, 2:3, :]
    for lo in range(0, TOK, 256):
        rows = slice(lo, lo + 256)
        dpr = (dmid[rows, :].astype(F32) * gate).astype(BF)
        dproj[rows, :] = dpr
        datt[rows, :] = mm(dpr, wo[...], NT).astype(BF)
    for h in range(HEADS):
        cols = slice(h * HEAD, (h + 1) * HEAD)
        q, k, v, do = head(qkv, 0, h), head(qkv, 1, h), head(qkv, 2, h), datt[:, cols]
        for lo in range(0, TOK, 256):
            rows = slice(lo, lo + 256)
            p = probs[h, rows, :]
            d = score_backward(p, mm(do[rows], v, NT))
            ds[rows, :] = d
            dqkv[rows, cols] = mm(d, k).astype(BF)
        dk = mm(q, ds[...], TN)
        dv = mm(do, probs[h], TN)
        dqkv[:, HD + h * HEAD : HD + (h + 1) * HEAD] = dk.T.astype(BF)
        dqkv[:, 2 * HD + h * HEAD : 2 * HD + (h + 1) * HEAD] = dv.T.astype(BF)
    for lo in range(0, TOK, 256):
        rows = slice(lo, lo + 256)
        dnormed = mm(dqkv[rows, :], wq[...], NT)
        dx = norm_backward(lat[rows, :].astype(F32), dnormed, scale)
        lat_grad[rows, :] = (dx + dmid[rows, :].astype(F32)).astype(BF)
    weight_grads(normed, dqkv, dproj, att, g)


def temporal_half(h2, lat_t, att_t, cot, mod, wo_s, wq, wo, mid, normed, qkv, att, dproj, dqkv, dmid):
    rows = slice(h2 * 256, (h2 + 1) * 256)
    part = slice(h2 * 16, (h2 + 1) * 16)
    gate_s = mod[0, 2:3, :]
    shift, scale, gate = mod[1, 0:1, :], mod[1, 1:2, :], mod[1, 2:3, :]
    x = lat_t[:, part, :].reshape(256, D).astype(F32)
    m = (x + gate_s * mm(att_t[:, part, :].reshape(256, HD), wo_s[...])).astype(BF)
    mid[rows, :] = m
    xhat, _ = standardise(m.astype(F32))
    n = (xhat * (1.0 + scale) + shift).astype(BF)
    normed[rows, :] = n
    qkv[rows, :] = mm(n, wq[...]).astype(BF)
    row_id = lax.broadcasted_iota(jnp.int32, (256, 256), 0)
    col_id = lax.broadcasted_iota(jnp.int32, (256, 256), 1)
    mask = (row_id & 15) == (col_id & 15)
    c = cot[:, part, :].reshape(256, D).astype(F32)
    dpr = (c * gate).astype(BF)
    dproj[rows, :] = dpr
    datt = mm(dpr, wo[...], NT).astype(BF)
    for h in range(HEADS):
        cols = slice(h * HEAD, (h + 1) * HEAD)
        q = qkv[rows, cols]
        k = qkv[rows, HD + h * HEAD : HD + (h + 1) * HEAD]
        v = qkv[rows, 2 * HD + h * HEAD : 2 * HD + (h + 1) * HEAD]
        p = softmax(mm(q, k, NT), mask).astype(BF)
        att[rows, cols] = mm(p, v).astype(BF)
        do = datt[:, cols]
        d = score_backward(p, mm(do, v, NT))
        dqkv[rows, cols] = mm(d, k).astype(BF)
        dqkv[rows, HD + h * HEAD : HD + (h + 1) * HEAD] = mm(q, d, TN).T.astype(BF)
        dqkv[rows, 2 * HD + h * HEAD : 2 * HD + (h + 1) * HEAD] = mm(do, p, TN).T.astype(BF)
    dnormed = mm(dqkv[rows, :], wq[...], NT)
    dx = norm_backward(mid[rows, :].astype(F32), dnormed, scale)
    dmid[:, part, :] = (dx + c).astype(BF).reshape(FRAMES, 16, D)


def temporal_output(h2, mod, wo, mid, att, block_out):
    rows = slice(h2 * 256, (h2 + 1) * 256)
    part = slice(h2 * 16, (h2 + 1) * 16)
    gate = mod[1, 2:3, :]
    y = mid[rows, :].astype(F32) + gate * mm(att[rows, :], wo[...])
    block_out[:, part, :] = y.astype(BF).reshape(FRAMES, 16, D)


def greet_seq(me):
    barrier = pltpu.get_barrier_semaphore()

    @pl.loop(1, FRAMES)
    def _(i):
        pl.semaphore_signal(
            barrier, inc=1, device_id={"seq": lax.rem(me + i, FRAMES)}, device_id_type=MESH
        )

    pl.semaphore_wait(barrier, FRAMES - 1)


def exchange(me, n, src_of, dst_of, send, recv, local):
    def copy(t, slot):
        return pltpu.make_async_remote_copy(
            src_ref=src_of(t),
            dst_ref=dst_of(slot),
            send_sem=send.at[n, t],
            recv_sem=recv.at[n, slot],
            device_id={"seq": t},
            device_id_type=MESH,
        )

    def own():
        return pltpu.make_async_copy(src_of(me), dst_of(me), local.at[n])

    def start():
        @pl.loop(1, FRAMES)
        def _(i):
            copy(lax.rem(me + i, FRAMES), me).start()

        own().start()

    def finish():
        @pl.loop(1, FRAMES)
        def _(i):
            t = lax.rem(me + i, FRAMES)
            c = copy(t, t)
            c.wait_send()
            c.wait_recv()

        own().wait()

    return start, finish


def spatial_forward_kernel(lat, mod, wq, normed, qkv, probs, att, lat_t, att_t, send, recv, local):
    me = lax.axis_index("seq")
    greet_seq(me)

    def span(t):
        return pl.ds(pl.multiple_of(t * SPAN, SPAN), SPAN)

    lat_go, lat_end = exchange(
        me, 0, lambda t: lat.at[span(t)], lambda s: lat_t.at[s], send, recv, local
    )
    lat_go()
    spatial_forward(lat, mod, wq, normed, qkv, probs, att)
    ends = [lat_end]
    for n, (heads, lanes) in enumerate(((range(0, 4), slice(0, 256)), (range(4, 8), slice(256, HD)))):
        for h in heads:
            spatial_head(h, qkv, probs, att)
        lo, width = lanes.start, lanes.stop - lanes.start
        go, end = exchange(
            me,
            1 + n,
            lambda t, lo=lo, width=width: att.at[span(t), pl.ds(lo, width)],
            lambda s, lo=lo, width=width: att_t.at[s, :, pl.ds(lo, width)],
            send,
            recv,
            local,
        )
        go()
        ends.append(end)
    for end in ends:
        end()


def temporal_kernel(
    lat_t, att_t, cot, mod, wo_s, wq, wo,
    block_out, dmid_in, g,
    mid, normed, qkv, att, dproj, dqkv, dmid, send, recv, local,
):
    me = lax.axis_index("seq")
    greet_seq(me)
    ends = []
    for h2 in range(2):
        temporal_half(
            h2, lat_t, att_t, cot, mod, wo_s, wq, wo, mid, normed, qkv, att, dproj, dqkv, dmid
        )
        part = pl.ds(h2 * 16, 16)
        go, end = exchange(
            me,
            h2,
            lambda t, part=part: dmid.at[t, part],
            lambda s, part=part: dmid_in.at[s, part],
            send,
            recv,
            local,
        )
        go()
        ends.append(end)
    for h2 in range(2):
        temporal_output(h2, mod, wo, mid, att, block_out)
    weight_grads(normed, dqkv, dproj, att, g)
    for end in ends:
        end()


def spatial_backward_kernel(
    lat, mod, normed, qkv, probs, att, wq, wo, dmid, lat_grad, g, dproj, datt, dqkv, ds
):
    spatial_backward(lat, mod, normed, qkv, probs, att, wq, wo, dmid, lat_grad, g, dproj, datt, dqkv, ds)


def spot(z, y, x, c):
    return {
        "dp": z * 2 + lax.div(y, 2),
        "seq": lax.rem(y, 2) * 8 + x * 2 + c,
    }


class Place:
    def __init__(self):
        dp, seq = lax.axis_index("dp"), lax.axis_index("seq")
        self.z = lax.div(dp, 2)
        self.y = lax.rem(dp, 2) * 2 + lax.div(seq, 8)
        self.x = lax.rem(lax.div(seq, 2), 4)
        self.c = lax.rem(seq, 2)
        self.at = (self.z, self.y, self.x)

    def moved(self, axis, j):
        return spot(*[j if i == axis else v for i, v in enumerate(self.at)], self.c)

    def partner(self):
        return spot(*self.at, 1 - self.c)


ORDERS = ((0, 1, 2), (1, 2, 0), (2, 0, 1))
CHUNK = 288
HALF = 144
BLOCK = 72
SLOT = 80


def odd_even(j):
    return j + 1 - 2 * lax.rem(j, 2)


def send_to(src, dst, send_sem, recv_sem, device):
    return pltpu.make_async_remote_copy(
        src_ref=src, dst_ref=dst, send_sem=send_sem, recv_sem=recv_sem, device_id=device, device_id_type=MESH
    )


class Reducer:
    def __init__(self, place, m, g, out, buf, sem):
        self.p, self.m, self.g, self.out, self.b, self.s = place, m, g, out, buf, sem

    def go0(self, k):
        return send_to(
            self.g.at[(1 - self.p.c) * 3 + k], self.b["r0"].at[self.m, k],
            self.s["s0"].at[self.m, k], self.s["v0"].at[self.m, k], self.p.partner(),
        )

    def chunk(self, j, half):
        return pl.ds(pl.multiple_of(j * CHUNK + half * HALF, 16), HALF)

    def ring(self, k, half):
        axis = ORDERS[k][0]
        j = self.p.at[axis]
        pair = (odd_even(j), 3 - j)
        return axis, j, pair[half], pair[1 - half]

    def go1(self, k, half, slot):
        axis, j, first, second = self.ring(k, half)
        other = 3 - first if half == 0 else odd_even(first)
        rows = self.chunk(first if slot == 0 else other, half)
        return send_to(
            self.b["r0"].at[self.m, k, rows], self.b["ra"].at[self.m, k, half, slot],
            self.s["sa"].at[self.m, k, half, slot], self.s["va"].at[self.m, k, half, slot],
            self.p.moved(axis, first),
        )

    def go2(self, k, half):
        axis, j, first, second = self.ring(k, half)
        return send_to(
            self.b["tb"].at[self.m, k, half], self.b["rb"].at[self.m, k, half],
            self.s["sb"].at[self.m, k, half], self.s["vb"].at[self.m, k, half],
            self.p.moved(axis, second),
        )

    def go3(self, k, to, slot):
        axis = ORDERS[k][1]
        return send_to(
            self.b["t2"].at[self.m, k, to], self.b["r2"].at[self.m, k, slot],
            self.s["s2"].at[self.m, k, to], self.s["v2"].at[self.m, k, slot],
            self.p.moved(axis, to),
        )

    def go4(self, k, x, c, s, e):
        a, b, _ = ORDERS[k]
        return send_to(
            self.b["t3"].at[self.m, k, x, c], self.b["r3"].at[self.m, k, s, e],
            self.s["s3"].at[self.m, k, x, c], self.s["v3"].at[self.m, k, s, e],
            spot(self.p.at[a], self.p.at[b], x, c),
        )

    def own4(self, k, x, c):
        s = self.p.at[ORDERS[k][2]]
        return pltpu.make_async_copy(
            self.b["t3"].at[self.m, k, x, c], self.b["r3"].at[self.m, k, s, self.p.c],
            self.s["v3"].at[self.m, k, s, self.p.c],
        )

    def to_self(self, k, x, c):
        p = self.p
        a, b, _ = ORDERS[k]
        return (p.at[a] == p.z) & (p.at[b] == p.y) & (x == p.x) & (c == p.c)


    def phase0(self):
        for k in range(3):
            self.go0(k).start()

    def phase1(self, k):
        self.go0(k).wait_recv()
        r0 = self.b["r0"]
        n = self.p.c * 3 + k

        @pl.loop(0, D // HALF)
        def _(i):
            rows = pl.ds(pl.multiple_of(i * HALF, 16), HALF)
            r0[self.m, k, rows] = (
                r0[self.m, k, rows].astype(F32) + self.g[n, rows].astype(F32)
            ).astype(BF)

        for slot in (1, 0):
            for half in range(2):
                self.go1(k, half, slot).start()

    def phase2(self, k):
        for half in range(2):
            axis, j, first, second = self.ring(k, half)
            self.go1(k, half, 1).wait_recv()
            rows = self.chunk(second, half)
            self.b["tb"][self.m, k, half] = (
                self.b["r0"][self.m, k, rows].astype(F32) + self.b["ra"][self.m, k, half, 1].astype(F32)
            ).astype(BF)
            self.go2(k, half).start()

    def phase3(self, k):
        axis = ORDERS[k][1]
        me = self.p.at[axis]
        for half in range(2):
            _, j, _, _ = self.ring(k, half)
            self.go1(k, half, 0).wait_recv()
            self.go2(k, half).wait_recv()
            rows = self.chunk(j, half)
            total = (
                self.b["r0"][self.m, k, rows].astype(F32)
                + self.b["ra"][self.m, k, half, 0].astype(F32)
                + self.b["rb"][self.m, k, half].astype(F32)
            )
            for i in range(2):
                self.b["t2"][self.m, k, 2 * half + i, :BLOCK] = total[i * BLOCK : (i + 1) * BLOCK].astype(BF)
                self.b["t2"][self.m, k, 2 * half + i, BLOCK:] = jnp.zeros((SLOT - BLOCK, WIDE), BF)

        @pl.loop(1, 4)
        def _(i):
            self.go3(k, lax.rem(me + i, 4), me).start()

    def phase4(self, k):
        axis = ORDERS[k][1]
        me = self.p.at[axis]
        total = self.b["t2"][self.m, k, me].astype(F32)
        for i in range(1, 4):
            t = lax.rem(me + i, 4)
            self.go3(k, t, t).wait_recv()
            total = total + self.b["r2"][self.m, k, t].astype(F32)
        row = lax.broadcasted_iota(jnp.int32, (128, SLOT), 0)
        col = lax.broadcasted_iota(jnp.int32, (128, SLOT), 1)
        pick = ((row & 15) < 9) & (col == lax.shift_right_logical(row, 4) * 9 + (row & 15))
        spread = mm(jnp.where(pick, 1.0, 0.0).astype(BF), total.astype(BF)).astype(BF)
        for x in range(4):
            for c in range(2):
                lo = (x * 2 + c) * 16
                self.b["t3"][self.m, k, x, c] = spread[lo : lo + 16]
        s = self.p.at[ORDERS[k][2]]

        @pl.loop(0, 8)
        def _(i):
            x, c = lax.div(i, 2), lax.rem(i, 2)
            mine = self.to_self(k, x, c)

            @pl.when(mine)
            def _():
                self.own4(k, x, c).start()

            @pl.when(jnp.logical_not(mine))
            def _():
                self.go4(k, x, c, s, self.p.c).start()

    def phase5(self, k):
        p = self.p
        own = self.to_self(k, p.x, p.c)
        own_s = p.at[ORDERS[k][2]]

        @pl.loop(0, 8)
        def _(i):
            s, e = lax.div(i, 2), lax.rem(i, 2)
            mine = own & (s == own_s) & (e == p.c)

            @pl.when(mine)
            def _():
                self.own4(k, p.x, p.c).wait()

            @pl.when(jnp.logical_not(mine))
            def _():
                self.go4(k, s, e, s, e).wait_recv()

        for e in range(2):
            total = self.b["r3"][self.m, k, 0, e].astype(F32)
            for s in range(1, 4):
                total = total + self.b["r3"][self.m, k, s, e].astype(F32)
            self.out[:, (e * 3 + k) * WIDE : (e * 3 + k + 1) * WIDE] = total

    def drain(self):
        for k in range(3):
            self.go0(k).wait_send()
            me = self.p.at[ORDERS[k][1]]
            for half in range(2):
                self.go1(k, half, 0).wait_send()
                self.go1(k, half, 1).wait_send()
                self.go2(k, half).wait_send()

            @pl.loop(1, 4)
            def _(i):
                t = lax.rem(me + i, 4)
                self.go3(k, t, t).wait_send()

            @pl.loop(0, 8)
            def _(i):
                x, c = lax.div(i, 2), lax.rem(i, 2)

                @pl.when(jnp.logical_not(self.to_self(k, x, c)))
                def _():
                    self.go4(k, x, c, 0, 0).wait_send()


def greet_all(p):
    barrier = pltpu.get_barrier_semaphore()

    def hail(device):
        pl.semaphore_signal(barrier, inc=1, device_id=device, device_id_type=MESH)

    hail(p.partner())
    for axis in range(3):
        for i in range(1, 4):
            hail(p.moved(axis, lax.rem(p.at[axis] + i, 4)))
    selves = 0
    for k in range(3):
        a, b, c = ORDERS[k]

        @pl.loop(0, 8)
        def _(i):
            s, e = lax.div(i, 2), lax.rem(i, 2)
            where = [None] * 3
            where[a], where[b], where[c] = p.z, p.y, s
            same = (where[0] == p.z) & (where[1] == p.y) & (where[2] == p.x) & (e == p.c)

            @pl.when(jnp.logical_not(same))
            def _():
                hail(spot(*where, e))

        own = (p.at[a] == p.z) & (p.at[b] == p.y)
        selves = selves + jnp.where(own & (p.at[c] == p.x), 1, 0)
    pl.semaphore_wait(barrier, 10 + 24 - selves)


def reduce_buffers(count):
    dma = pltpu.SemaphoreType.DMA
    bufs = dict(
        r0=pltpu.VMEM((count, 3, D, WIDE), BF),
        ra=pltpu.VMEM((count, 3, 2, 2, HALF, WIDE), BF),
        tb=pltpu.VMEM((count, 3, 2, HALF, WIDE), BF),
        rb=pltpu.VMEM((count, 3, 2, HALF, WIDE), BF),
        t2=pltpu.VMEM((count, 3, 4, SLOT, WIDE), BF),
        r2=pltpu.VMEM((count, 3, 4, SLOT, WIDE), BF),
        t3=pltpu.VMEM((count, 3, 4, 2, 16, WIDE), BF),
        r3=pltpu.VMEM((count, 3, 4, 2, 16, WIDE), BF),
    )
    sems = {}
    for end in "sv":
        sems[end + "0"] = dma((count, 3))
        sems[end + "a"] = dma((count, 3, 2, 2))
        sems[end + "b"] = dma((count, 3, 2))
        sems[end + "2"] = dma((count, 3, 4))
        sems[end + "3"] = dma((count, 3, 4, 2))
    return bufs, sems


def reduce_kernel(g_t, g_s, out_t, out_s, buf, sem):
    p = Place()
    greet_all(p)
    both = [Reducer(p, 0, g_t, out_t, buf, sem), Reducer(p, 1, g_s, out_s, buf, sem)]
    for r in both:
        r.phase0()
    for name in ("phase1", "phase2", "phase3", "phase4", "phase5"):
        for r in both:
            for k in range(3):
                getattr(r, name)(k)
    for r in both:
        r.drain()


def params(collective_id=None):
    if collective_id is None:
        return pltpu.CompilerParams(vmem_limit_bytes=56 * 1024 * 1024)
    return pltpu.CompilerParams(
        vmem_limit_bytes=56 * 1024 * 1024, collective_id=collective_id, has_side_effects=True
    )


def shape(dims, kind=BF):
    return jax.ShapeDtypeStruct(dims, kind)


def exchange_sems(count):
    return [
        pltpu.SemaphoreType.DMA((count, FRAMES)),
        pltpu.SemaphoreType.DMA((count, FRAMES)),
        pltpu.SemaphoreType.DMA((count,)),
    ]


def run_spatial_forward(lat, mod, wq):
    return pl.pallas_call(
        spatial_forward_kernel,
        out_shape=(
            shape((TOK, D)), shape((TOK, QKV)), shape((HEADS, TOK, TOK)), shape((TOK, HD)),
            shape((FRAMES, SPAN, D)), shape((FRAMES, SPAN, HD)),
        ),
        in_specs=[vmem_spec()] * 3,
        out_specs=[vmem_spec()] * 4 + [any_spec()] * 2,
        scratch_shapes=exchange_sems(3),
        compiler_params=params(0),
        name="spatial_forward",
    )(lat, mod, wq)


def run_temporal(lat_t, att_t, cot, mod, wo_s, wq, wo):
    return pl.pallas_call(
        temporal_kernel,
        out_shape=(shape((FRAMES, SPAN, D)), shape((FRAMES, SPAN, D)), shape((PIECES, D, WIDE))),
        in_specs=[vmem_spec()] * 7,
        out_specs=[vmem_spec(), any_spec(), vmem_spec()],
        scratch_shapes=[
            pltpu.VMEM((TOK, D), BF),
            pltpu.VMEM((TOK, D), BF),
            pltpu.VMEM((TOK, QKV), BF),
            pltpu.VMEM((TOK, HD), BF),
            pltpu.VMEM((TOK, D), BF),
            pltpu.VMEM((TOK, QKV), BF),
            pltpu.VMEM((FRAMES, SPAN, D), BF),
        ] + exchange_sems(2),
        compiler_params=params(1),
        name="temporal",
    )(lat_t, att_t, cot, mod, wo_s, wq, wo)


def run_spatial_backward(lat, mod, normed, qkv, probs, att, wq, wo, dmid):
    return pl.pallas_call(
        spatial_backward_kernel,
        out_shape=(shape((TOK, D)), shape((PIECES, D, WIDE))),
        in_specs=[vmem_spec()] * 9,
        out_specs=[vmem_spec()] * 2,
        scratch_shapes=[
            pltpu.VMEM((TOK, D), BF),
            pltpu.VMEM((TOK, HD), BF),
            pltpu.VMEM((TOK, QKV), BF),
            pltpu.VMEM((TOK, TOK), BF),
        ],
        compiler_params=params(),
        name="spatial_backward",
    )(lat, mod, normed, qkv, probs, att, wq, wo, dmid)


def run_reduce(g_t, g_s):
    bufs, sems = reduce_buffers(2)
    names, keys = list(bufs), list(sems)

    def kernel(g_t, g_s, out_t, out_s, *rest):
        buf = dict(zip(names, rest[: len(names)]))
        sem = dict(zip(keys, rest[len(names) :]))
        reduce_kernel(g_t, g_s, out_t, out_s, buf, sem)

    return pl.pallas_call(
        kernel,
        out_shape=(shape((16, PIECES * WIDE), F32),) * 2,
        in_specs=[vmem_spec()] * 2,
        out_specs=[vmem_spec()] * 2,
        scratch_shapes=list(bufs.values()) + list(sems.values()),
        compiler_params=params(2),
        name="reduce_gradients",
    )(g_t, g_s)


def body(latents, modulation, spatial_qkv, spatial_out, temporal_qkv, temporal_out, cotangent):
    lat, mod, cot = latents[0, 0], modulation[0], cotangent[0]
    normed, qkv, probs, att, lat_t, att_t = run_spatial_forward(lat, mod, spatial_qkv)
    block_out, dmid, g_t = run_temporal(lat_t, att_t, cot, mod, spatial_out, temporal_qkv, temporal_out)
    lat_grad, g_s = run_spatial_backward(
        lat, mod, normed, qkv, probs, att, spatial_qkv, spatial_out, dmid.reshape(TOK, D)
    )
    sum_t, sum_s = run_reduce(g_t, g_s)
    return (
        block_out[None],
        lat_grad[None, None],
        sum_s[:9, :QKV],
        sum_s[:9, QKV:].T,
        sum_t[:9, :QKV],
        sum_t[:9, QKV:].T,
    )


def solution(mesh):
    return jax.shard_map(
        body,
        mesh=mesh,
        in_specs=(
            P("dp", "seq", None, None),
            P("dp", None, None, None),
            P(),
            P(),
            P(),
            P(),
            P("dp", None, "seq", None),
        ),
        out_specs=(
            P("dp", None, "seq", None),
            P("dp", "seq", None, None),
            P(("dp", "seq"), None),
            P(None, ("dp", "seq")),
            P(("dp", "seq"), None),
            P(None, ("dp", "seq")),
        ),
        check_vma=False,
    )
```

```python
import functools
import math

import jax
import jax.numpy as jnp
from jax import lax
from jax.experimental import pallas as pl
from jax.experimental.pallas import tpu as pltpu
from jax.sharding import PartitionSpec as P

D = 1152
HEADS = 8
HEAD = 72
HD = 576
QKV = 3 * HD
FRAMES = 16
POS = 512
SPAN = 32
TOK = 512
SCALE = HEAD ** (-0.5)
EXP2 = SCALE / math.log(2.0)
MESH = pl.DeviceIdType.MESH
BF = jnp.bfloat16
F32 = jnp.float32
PIECES = 6
WIDE = 384

NN = (((1,), (0,)), ((), ()))
NT = (((1,), (1,)), ((), ()))
TN = (((0,), (0,)), ((), ()))


def mm(a, b, form=NN):
    return lax.dot_general(a, b, form, preferred_element_type=F32)


def vmem_spec():
    return pl.BlockSpec(memory_space=pltpu.VMEM)


def any_spec():
    return pl.BlockSpec(memory_space=pl.ANY)


def standardise(x):
    centre = jnp.mean(x, -1, keepdims=True)
    centred = x - centre
    spread = jnp.mean(centred * centred, -1, keepdims=True)
    rstd = lax.rsqrt(spread + 1e-06)
    return centred * rstd, rstd


def norm_backward(x, dnormed, scale):
    xhat, rstd = standardise(x)
    dxhat = dnormed * (1.0 + scale)
    first = jnp.mean(dxhat, -1, keepdims=True)
    second = jnp.mean(dxhat * xhat, -1, keepdims=True)
    return rstd * (dxhat - first - xhat * second)


def softmax(scores, mask=None):
    if mask is not None:
        scores = jnp.where(mask, scores, -1e30)
    largest = jnp.max(scores, -1, keepdims=True)
    expo = jnp.exp2((scores - largest) * EXP2)
    return expo * (1.0 / jnp.sum(expo, -1, keepdims=True))


def head(ref_or_val, part, h):
    lo = part * HD + h * HEAD
    return ref_or_val[:, lo : lo + HEAD]


def score_backward(p, dp):
    wide = p.astype(F32)
    delta = jnp.sum(dp * wide, -1, keepdims=True)
    return (wide * (dp - delta) * SCALE).astype(BF)


def weight_grads(group, normed, dqkv, dproj, att, g):
    n = 2 * group
    for lo in range(0, D, 384):
        rows = slice(lo, lo + 384)
        if group < 2:
            both = mm(normed[:, rows], dqkv[:, n * WIDE : (n + 2) * WIDE], TN)
            g[n, rows, :] = both[:, :WIDE].astype(BF)
            g[n + 1, rows, :] = both[:, WIDE:].astype(BF)
        else:
            last = mm(normed[:, rows], dqkv[:, n * WIDE :], TN)
            outs = mm(dproj[:, rows], att[...], TN)
            g[n, rows, :192] = last.astype(BF)
            g[n, rows, 192:] = outs[:, :192].astype(BF)
            g[n + 1, rows, :] = outs[:, 192:].astype(BF)


def spatial_norm(lat, mod, normed):
    shift, scale = mod[0, 0:1, :], mod[1, 0:1, :]
    for lo in range(0, TOK, 128):
        rows = slice(lo, lo + 128)
        xhat, _ = standardise(lat[rows, :].astype(F32))
        normed[rows, :] = (xhat * (1.0 + scale) + shift).astype(BF)


def spatial_project(normed, wq, qkv):
    for lo in range(0, TOK, 256):
        rows = slice(lo, lo + 256)
        qkv[rows, :] = mm(normed[rows, :], wq[...], NT).astype(BF)


def spatial_head(h, qkv, probs, att):
    keys, values = head(qkv, 1, h), head(qkv, 2, h)
    for lo in range(0, TOK, 256):
        rows = slice(lo, lo + 256)
        q = qkv[rows, h * HEAD : (h + 1) * HEAD]
        p = softmax(mm(q, keys, NT)).astype(BF)
        probs[h, rows, :] = p
        att[rows, h * HEAD : (h + 1) * HEAD] = mm(p, values).astype(BF)


def spatial_back_open(mod, wo, dmid, dproj, datt):
    gate = mod[2, 0:1, :]
    for lo in range(0, TOK, 256):
        rows = slice(lo, lo + 256)
        dpr = (dmid[rows, :].astype(F32) * gate).astype(BF)
        dproj[rows, :] = dpr
        datt[rows, :] = mm(dpr, wo[...], NT).astype(BF)


def spatial_back_head(h, qkv, probs, datt, dqkv, ds):
    cols = slice(h * HEAD, (h + 1) * HEAD)
    q, k, v, do = head(qkv, 0, h), head(qkv, 1, h), head(qkv, 2, h), datt[:, cols]
    for lo in range(0, TOK, 256):
        rows = slice(lo, lo + 256)
        p = probs[h, rows, :]
        d = score_backward(p, mm(do[rows], v, NT))
        ds[rows, :] = d
        dqkv[rows, cols] = mm(d, k).astype(BF)
    dk = mm(q, ds[...], TN)
    dv = mm(do, probs[h], TN)
    dqkv[:, HD + h * HEAD : HD + (h + 1) * HEAD] = dk.T.astype(BF)
    dqkv[:, 2 * HD + h * HEAD : 2 * HD + (h + 1) * HEAD] = dv.T.astype(BF)


def spatial_back_close(rows, lat, mod, wq, dmid, dqkv, lat_grad):
    dnormed = mm(dqkv[rows, :], wq[...])
    dx = norm_backward(lat[rows, :].astype(F32), dnormed, mod[1, 0:1, :])
    lat_grad[rows, :] = (dx + dmid[rows, :].astype(F32)).astype(BF)


def temporal_open(h2, cot, mod, wo, dproj, datt):
    rows = slice(h2 * 256, (h2 + 1) * 256)
    part = slice(h2 * 16, (h2 + 1) * 16)
    dpr = (cot[:, part, :].reshape(256, D).astype(F32) * mod[2, 1:2, :]).astype(BF)
    dproj[rows, :] = dpr
    datt[rows, :] = mm(dpr, wo[...], NT).astype(BF)


def temporal_half(h2, lat_t, att_t, cot, mod, wo_s, wq, mid, normed, qkv, att, datt, dqkv, dmid):
    rows = slice(h2 * 256, (h2 + 1) * 256)
    part = slice(h2 * 16, (h2 + 1) * 16)
    gate_s = mod[2, 0:1, :]
    shift, scale = mod[0, 1:2, :], mod[1, 1:2, :]
    x = lat_t[:, part, :].reshape(256, D).astype(F32)
    m = (x + gate_s * mm(att_t[:, part, :].reshape(256, HD), wo_s[...])).astype(BF)
    mid[rows, :] = m
    xhat, _ = standardise(m.astype(F32))
    n = (xhat * (1.0 + scale) + shift).astype(BF)
    normed[rows, :] = n
    qkv[rows, :] = mm(n, wq[...], NT).astype(BF)
    row_id = lax.broadcasted_iota(jnp.int32, (256, 256), 0)
    col_id = lax.broadcasted_iota(jnp.int32, (256, 256), 1)
    mask = (row_id & 15) == (col_id & 15)
    for h in range(HEADS):
        cols = slice(h * HEAD, (h + 1) * HEAD)
        q = qkv[rows, cols]
        k = qkv[rows, HD + h * HEAD : HD + (h + 1) * HEAD]
        v = qkv[rows, 2 * HD + h * HEAD : 2 * HD + (h + 1) * HEAD]
        p = softmax(mm(q, k, NT), mask).astype(BF)
        att[rows, cols] = mm(p, v).astype(BF)
        do = datt[rows, cols]
        d = score_backward(p, mm(do, v, NT))
        dqkv[rows, cols] = mm(d, k).astype(BF)
        dqkv[rows, HD + h * HEAD : HD + (h + 1) * HEAD] = mm(q, d, TN).T.astype(BF)
        dqkv[rows, 2 * HD + h * HEAD : 2 * HD + (h + 1) * HEAD] = mm(do, p, TN).T.astype(BF)
    dnormed = mm(dqkv[rows, :], wq[...])
    dx = norm_backward(mid[rows, :].astype(F32), dnormed, scale)
    c = cot[:, part, :].reshape(256, D).astype(F32)
    dmid[:, part, :] = (dx + c).astype(BF).reshape(FRAMES, 16, D)


def temporal_output(h2, mod, wo, mid, att, block_out):
    rows = slice(h2 * 256, (h2 + 1) * 256)
    part = slice(h2 * 16, (h2 + 1) * 16)
    gate = mod[2, 1:2, :]
    y = mid[rows, :].astype(F32) + gate * mm(att[rows, :], wo[...])
    block_out[:, part, :] = y.astype(BF).reshape(FRAMES, 16, D)


class Exchange:
    def __init__(self, me, n, src_of, dst_of, send, recv, local):
        self.me, self.n, self.src_of, self.dst_of = me, n, src_of, dst_of
        self.send, self.recv, self.local = send, recv, local

    def copy(self, t, slot):
        return pltpu.make_async_remote_copy(
            src_ref=self.src_of(t),
            dst_ref=self.dst_of(slot),
            send_sem=self.send.at[self.n, t],
            recv_sem=self.recv.at[self.n, slot],
            device_id={"seq": t},
            device_id_type=MESH,
        )

    def own(self):
        return pltpu.make_async_copy(self.src_of(self.me), self.dst_of(self.me), self.local.at[self.n])

    def others(self, step):
        @pl.loop(1, FRAMES)
        def _(i):
            step(lax.rem(self.me + i, FRAMES))

    def start(self):
        self.others(lambda t: self.copy(t, self.me).start())
        self.own().start()

    def arrive(self):
        self.others(lambda t: self.copy(t, t).wait_recv())
        self.own().wait()

    def drain(self):
        self.others(lambda t: self.copy(t, t).wait_send())


def spot(z, y, x, c):
    return {
        "dp": z * 2 + lax.div(y, 2),
        "seq": lax.rem(y, 2) * 8 + x * 2 + c,
    }


class Place:
    def __init__(self):
        dp, seq = lax.axis_index("dp"), lax.axis_index("seq")
        self.z = lax.div(dp, 2)
        self.y = lax.rem(dp, 2) * 2 + lax.div(seq, 8)
        self.x = lax.rem(lax.div(seq, 2), 4)
        self.c = lax.rem(seq, 2)
        self.at = (self.z, self.y, self.x)

    def moved(self, axis, j):
        return spot(*[j if i == axis else v for i, v in enumerate(self.at)], self.c)

    def partner(self):
        return spot(*self.at, 1 - self.c)


ORDERS = ((0, 1, 2), (1, 2, 0), (2, 0, 1))
CHUNK = 288
HALF = 144
BLOCK = 72
SLOT = 80


def odd_even(j):
    return j + 1 - 2 * lax.rem(j, 2)


def send_to(src, dst, send_sem, recv_sem, device):
    return pltpu.make_async_remote_copy(
        src_ref=src, dst_ref=dst, send_sem=send_sem, recv_sem=recv_sem, device_id=device, device_id_type=MESH
    )


class Reducer:
    def __init__(self, place, m, g, out, buf, sem):
        self.p, self.m, self.g, self.out, self.b, self.s = place, m, g, out, buf, sem

    def go0(self, k):
        return send_to(
            self.g.at[(1 - self.p.c) * 3 + k], self.b["r0"].at[self.m, k],
            self.s["s0"].at[self.m, k], self.s["v0"].at[self.m, k], self.p.partner(),
        )

    def chunk(self, j, half):
        return pl.ds(pl.multiple_of(j * CHUNK + half * HALF, 16), HALF)

    def ring(self, k, half):
        axis = ORDERS[k][0]
        j = self.p.at[axis]
        pair = (odd_even(j), 3 - j)
        return axis, j, pair[half], pair[1 - half]

    def go1(self, k, half, slot):
        axis, j, first, second = self.ring(k, half)
        other = 3 - first if half == 0 else odd_even(first)
        rows = self.chunk(first if slot == 0 else other, half)
        return send_to(
            self.b["r0"].at[self.m, k, rows], self.b["ra"].at[self.m, k, half, slot],
            self.s["sa"].at[self.m, k, half, slot], self.s["va"].at[self.m, k, half, slot],
            self.p.moved(axis, first),
        )

    def go2(self, k, half):
        axis, j, first, second = self.ring(k, half)
        return send_to(
            self.b["tb"].at[self.m, k, half], self.b["rb"].at[self.m, k, half],
            self.s["sb"].at[self.m, k, half], self.s["vb"].at[self.m, k, half],
            self.p.moved(axis, second),
        )

    def go3(self, k, to, slot):
        axis = ORDERS[k][1]
        return send_to(
            self.b["t2"].at[self.m, k, to], self.b["r2"].at[self.m, k, slot],
            self.s["s2"].at[self.m, k, to], self.s["v2"].at[self.m, k, slot],
            self.p.moved(axis, to),
        )

    def go4(self, k, x, c, s, e):
        a, b, _ = ORDERS[k]
        return send_to(
            self.b["t3"].at[self.m, k, x, c], self.b["r3"].at[self.m, k, s, e],
            self.s["s3"].at[self.m, k, x, c], self.s["v3"].at[self.m, k, s, e],
            spot(self.p.at[a], self.p.at[b], x, c),
        )

    def own4(self, k, x, c):
        s = self.p.at[ORDERS[k][2]]
        return pltpu.make_async_copy(
            self.b["t3"].at[self.m, k, x, c], self.b["r3"].at[self.m, k, s, self.p.c],
            self.s["v3"].at[self.m, k, s, self.p.c],
        )

    def to_self(self, k, x, c):
        p = self.p
        a, b, _ = ORDERS[k]
        return (p.at[a] == p.z) & (p.at[b] == p.y) & (x == p.x) & (c == p.c)


    def phase0(self, k):
        self.go0(k).start()

    def sent0(self):
        for k in range(3):
            self.go0(k).wait_send()

    def phase1(self, k):
        self.go0(k).wait_recv()
        r0 = self.b["r0"]
        n = self.p.c * 3 + k

        @pl.loop(0, D // HALF)
        def _(i):
            rows = pl.ds(pl.multiple_of(i * HALF, 16), HALF)
            r0[self.m, k, rows] = (
                r0[self.m, k, rows].astype(F32) + self.g[n, rows].astype(F32)
            ).astype(BF)

        for slot in (1, 0):
            for half in range(2):
                self.go1(k, half, slot).start()

    def phase2(self, k):
        for half in range(2):
            axis, j, first, second = self.ring(k, half)
            self.go1(k, half, 1).wait_recv()
            rows = self.chunk(second, half)
            self.b["tb"][self.m, k, half] = (
                self.b["r0"][self.m, k, rows].astype(F32) + self.b["ra"][self.m, k, half, 1].astype(F32)
            ).astype(BF)
            self.go2(k, half).start()

    def phase3(self, k):
        axis = ORDERS[k][1]
        me = self.p.at[axis]
        for half in range(2):
            _, j, _, _ = self.ring(k, half)
            self.go1(k, half, 0).wait_recv()
            self.go2(k, half).wait_recv()
            rows = self.chunk(j, half)
            total = (
                self.b["r0"][self.m, k, rows].astype(F32)
                + self.b["ra"][self.m, k, half, 0].astype(F32)
                + self.b["rb"][self.m, k, half].astype(F32)
            )
            for i in range(2):
                self.b["t2"][self.m, k, 2 * half + i, :BLOCK] = total[i * BLOCK : (i + 1) * BLOCK].astype(BF)
                self.b["t2"][self.m, k, 2 * half + i, BLOCK:] = jnp.zeros((SLOT - BLOCK, WIDE), BF)

        @pl.loop(1, 4)
        def _(i):
            self.go3(k, lax.rem(me + i, 4), me).start()

    def phase4(self, k):
        axis = ORDERS[k][1]
        me = self.p.at[axis]
        total = self.b["t2"][self.m, k, me].astype(F32)
        for i in range(1, 4):
            t = lax.rem(me + i, 4)
            self.go3(k, t, t).wait_recv()
            total = total + self.b["r2"][self.m, k, t].astype(F32)
        row = lax.broadcasted_iota(jnp.int32, (128, SLOT), 0)
        col = lax.broadcasted_iota(jnp.int32, (128, SLOT), 1)
        pick = ((row & 15) < 9) & (col == lax.shift_right_logical(row, 4) * 9 + (row & 15))
        spread = mm(jnp.where(pick, 1.0, 0.0).astype(BF), total.astype(BF)).astype(BF)
        for x in range(4):
            for c in range(2):
                lo = (x * 2 + c) * 16
                self.b["t3"][self.m, k, x, c] = spread[lo : lo + 16]
        s = self.p.at[ORDERS[k][2]]

        @pl.loop(0, 8)
        def _(i):
            x, c = lax.div(i, 2), lax.rem(i, 2)
            mine = self.to_self(k, x, c)

            @pl.when(mine)
            def _():
                self.own4(k, x, c).start()

            @pl.when(jnp.logical_not(mine))
            def _():
                self.go4(k, x, c, s, self.p.c).start()

    def phase5(self, k):
        p = self.p
        own = self.to_self(k, p.x, p.c)
        own_s = p.at[ORDERS[k][2]]

        @pl.loop(0, 8)
        def _(i):
            s, e = lax.div(i, 2), lax.rem(i, 2)
            mine = own & (s == own_s) & (e == p.c)

            @pl.when(mine)
            def _():
                self.own4(k, p.x, p.c).wait()

            @pl.when(jnp.logical_not(mine))
            def _():
                self.go4(k, s, e, s, e).wait_recv()

        for e in range(2):
            total = self.b["r3"][self.m, k, 0, e].astype(F32)
            for s in range(1, 4):
                total = total + self.b["r3"][self.m, k, s, e].astype(F32)
            n = e * 3 + k
            if n < 4:
                self.out[0][:, n * WIDE : (n + 1) * WIDE] = total[:9]
            elif n == 4:
                self.out[0][:, n * WIDE :] = total[:9, :192]
                self.out[1][:, :192] = total[:9, 192:]
            else:
                self.out[1][:, 192:] = total[:9]

    def drain(self):
        for k in range(3):
            me = self.p.at[ORDERS[k][1]]
            for half in range(2):
                self.go1(k, half, 0).wait_send()
                self.go1(k, half, 1).wait_send()
                self.go2(k, half).wait_send()

            @pl.loop(1, 4)
            def _(i):
                t = lax.rem(me + i, 4)
                self.go3(k, t, t).wait_send()

            @pl.loop(0, 8)
            def _(i):
                x, c = lax.div(i, 2), lax.rem(i, 2)

                @pl.when(jnp.logical_not(self.to_self(k, x, c)))
                def _():
                    self.go4(k, x, c, 0, 0).wait_send()


def greet(p, me):
    barrier = pltpu.get_barrier_semaphore()

    def hail(device):
        pl.semaphore_signal(barrier, inc=1, device_id=device, device_id_type=MESH)

    @pl.loop(1, FRAMES)
    def _(i):
        hail({"seq": lax.rem(me + i, FRAMES)})

    hail(p.partner())
    for axis in range(3):
        for i in range(1, 4):
            hail(p.moved(axis, lax.rem(p.at[axis] + i, 4)))
    selves = 0
    for k in range(3):
        a, b, c = ORDERS[k]

        @pl.loop(0, 8)
        def _(i):
            s, e = lax.div(i, 2), lax.rem(i, 2)
            where = [None] * 3
            where[a], where[b], where[c] = p.z, p.y, s
            same = (where[0] == p.z) & (where[1] == p.y) & (where[2] == p.x) & (e == p.c)

            @pl.when(jnp.logical_not(same))
            def _():
                hail(spot(*where, e))

        own = (p.at[a] == p.z) & (p.at[b] == p.y)
        selves = selves + jnp.where(own & (p.at[c] == p.x), 1, 0)
    return FRAMES - 1 + 10 + 24 - selves


def reduce_buffers(count):
    dma = pltpu.SemaphoreType.DMA
    bufs = dict(
        r0=pltpu.VMEM((count, 3, D, WIDE), BF),
        ra=pltpu.VMEM((count, 3, 2, 2, HALF, WIDE), BF),
        tb=pltpu.VMEM((count, 3, 2, HALF, WIDE), BF),
        rb=pltpu.VMEM((count, 3, 2, HALF, WIDE), BF),
        t2=pltpu.VMEM((count, 3, 4, SLOT, WIDE), BF),
        r2=pltpu.VMEM((count, 3, 4, SLOT, WIDE), BF),
        t3=pltpu.VMEM((count, 3, 4, 2, 16, WIDE), BF),
        r3=pltpu.VMEM((count, 3, 4, 2, 16, WIDE), BF),
    )
    sems = {}
    for end in "sv":
        sems[end + "0"] = dma((count, 3))
        sems[end + "a"] = dma((count, 3, 2, 2))
        sems[end + "b"] = dma((count, 3, 2))
        sems[end + "2"] = dma((count, 3, 4))
        sems[end + "3"] = dma((count, 3, 4, 2))
    return bufs, sems


def kernel(ins, outs, v, sem, buf, rsem):
    me = lax.axis_index("seq")
    p = Place()
    mod = ins["mod"]
    lat, cot = v["lat"], v["cot"]

    names = ("lat", "wq_s", "cot", "wo_t", "wo_s", "wq_t")
    loads = {k: pltpu.make_async_copy(ins[k], v[k], sem["load"].at[i]) for i, k in enumerate(names)}
    for k in names:
        loads[k].start()
    expected = greet(p, me)

    def exchange(n, src_of, dst_of):
        return Exchange(me, n, src_of, dst_of, sem["send"], sem["recv"], sem["local"])

    def frame_rows(t, h2):
        return pl.ds(pl.multiple_of(t * SPAN + h2 * 16, 16), 16)

    lat_x, att_x, dmid_x = [], [], []
    for h2 in range(2):
        part = pl.ds(h2 * 16, 16)
        lat_x.append(exchange(
            h2, lambda t, h2=h2: lat.at[frame_rows(t, h2)], lambda s, part=part: v["lat_t"].at[s, part]
        ))
        att_x.append(exchange(
            2 + h2, lambda t, h2=h2: v["att_s"].at[frame_rows(t, h2)], lambda s, part=part: v["att_in"].at[s, part]
        ))
        dmid_x.append(exchange(
            4 + h2, lambda t, part=part: v["dmid_t"].at[t, part],
            lambda s, h2=h2: v["dmid"].at[frame_rows(s, h2)],
        ))

    red_t = Reducer(p, 0, v["g"], (outs["qkv_t"], outs["out_t"]), buf, rsem)
    red_s = Reducer(p, 1, v["g"], (outs["qkv_s"], outs["out_s"]), buf, rsem)

    loads["lat"].wait()
    spatial_norm(lat, mod, v["normed_s"])
    pl.semaphore_wait(pltpu.get_barrier_semaphore(), expected)
    lat_x[0].start()
    loads["wq_s"].wait()
    spatial_project(v["normed_s"], v["wq_s"], v["qkv_s"])
    for h in range(HEADS):
        spatial_head(h, v["qkv_s"], v["probs"], v["att_s"])
    att_x[0].start()
    lat_x[1].start()
    att_x[1].start()

    for k in names[2:]:
        loads[k].wait()
    for h2 in range(2):
        temporal_open(h2, cot, mod, v["wo_t"], v["dproj"], v["datt"])
    for h2 in range(2):
        lat_x[h2].arrive()
        att_x[h2].arrive()
        temporal_half(
            h2, v["lat_t"], v["att_in"], cot, mod, v["wo_s"], v["wq_t"], v["mid"], v["normed_t"],
            v["qkv_t"], v["att_t"], v["datt"], v["dqkv"], v["dmid_t"],
        )
        dmid_x[h2].start()
    for h2 in range(2):
        temporal_output(h2, mod, v["wo_t"], v["mid"], v["att_t"], v["block_out"])
    store_out = pltpu.make_async_copy(v["block_out"], outs["block_out"], sem["store"].at[0])
    store_out.start()
    for group in range(3):
        weight_grads(group, v["normed_t"], v["dqkv"], v["dproj"], v["att_t"], v["g"])
    for k in range(3):
        red_t.phase0(k)

    for h2 in range(2):
        dmid_x[h2].arrive()
    spatial_back_open(mod, v["wo_s"], v["dmid"], v["dproj"], v["datt"])
    steps = {0: "phase1", 2: "phase2", 4: "phase3", 6: "phase4"}
    for h in range(HEADS):
        if h in steps:
            for k in range(3):
                getattr(red_t, steps[h])(k)
        spatial_back_head(h, v["qkv_s"], v["probs"], v["datt"], v["dqkv"], v["ds"])
    red_t.sent0()
    for group, ready in ((2, ()), (0, (1,)), (1, (0, 2))):
        weight_grads(group, v["normed_s"], v["dqkv"], v["dproj"], v["att_s"], v["g"])
        for k in ready:
            red_s.phase0(k)
    for lo in (0, 256):
        spatial_back_close(slice(lo, lo + 256), lat, mod, v["wq_s"], v["dmid"], v["dqkv"], v["lat_grad"])
    store_grad = pltpu.make_async_copy(v["lat_grad"], outs["lat_grad"], sem["store"].at[1])
    store_grad.start()
    for k in range(3):
        red_t.phase5(k)

    for name in ("phase1", "phase2", "phase3", "phase4", "phase5"):
        for k in (1, 0, 2):
            getattr(red_s, name)(k)

    store_out.wait()
    store_grad.wait()
    for x in lat_x + att_x + dmid_x:
        x.drain()
    red_s.sent0()
    red_t.drain()
    red_s.drain()


def shape(dims, kind=BF):
    return jax.ShapeDtypeStruct(dims, kind)


def params(collective_id=None):
    if collective_id is None:
        return pltpu.CompilerParams(vmem_limit_bytes=VMEM_LIMIT)
    return pltpu.CompilerParams(
        vmem_limit_bytes=VMEM_LIMIT, collective_id=collective_id, has_side_effects=True
    )


VMEM_LIMIT = 62 * 1024 * 1024
INPUTS = ("lat", "mod", "wq_s", "wo_s", "wq_t", "wo_t", "cot")
OUTPUTS = {
    "block_out": shape((FRAMES, SPAN, D)),
    "lat_grad": shape((TOK, D)),
    "qkv_s": shape((9, QKV), F32),
    "out_s": shape((9, HD), F32),
    "qkv_t": shape((9, QKV), F32),
    "out_t": shape((9, HD), F32),
}
VALUES = {
    "lat": (TOK, D), "cot": (FRAMES, SPAN, D),
    "wq_s": (QKV, D), "wo_s": (HD, D), "wq_t": (QKV, D), "wo_t": (HD, D),
    "normed_s": (TOK, D), "qkv_s": (TOK, QKV), "probs": (HEADS, TOK, TOK), "att_s": (TOK, HD),
    "lat_t": (FRAMES, SPAN, D), "att_in": (FRAMES, SPAN, HD),
    "mid": (TOK, D), "normed_t": (TOK, D), "qkv_t": (TOK, QKV), "att_t": (TOK, HD),
    "dproj": (TOK, D), "datt": (TOK, HD), "dqkv": (TOK, QKV), "ds": (TOK, TOK),
    "dmid_t": (FRAMES, SPAN, D), "dmid": (TOK, D),
    "block_out": (FRAMES, SPAN, D), "lat_grad": (TOK, D),
    "g": (PIECES, D, WIDE),
}


def run(*args):
    dma = pltpu.SemaphoreType.DMA
    bufs, rsems = reduce_buffers(2)
    sems = {
        "load": dma((6,)), "store": dma((2,)),
        "send": dma((6, FRAMES)), "recv": dma((6, FRAMES)), "local": dma((6,)),
    }
    values = {k: pltpu.VMEM(d, BF) for k, d in VALUES.items()}
    groups = (values, sems, bufs, rsems)

    def unpack(*refs):
        refs = list(refs)

        def take(names):
            got = dict(zip(names, refs))
            del refs[: len(got)]
            return got

        kernel(take(INPUTS), take(OUTPUTS), *[take(g) for g in groups])

    return pl.pallas_call(
        unpack,
        out_shape=tuple(OUTPUTS.values()),
        in_specs=[vmem_spec() if k == "mod" else any_spec() for k in INPUTS],
        out_specs=[any_spec()] * 2 + [vmem_spec()] * 4,
        scratch_shapes=[x for g in groups for x in g.values()],
        compiler_params=params(0),
        name="attention_blocks",
    )(*args)


def body(latents, modulation, spatial_qkv, spatial_out, temporal_qkv, temporal_out, cotangent):
    block_out, lat_grad, qkv_s, out_s, qkv_t, out_t = run(
        latents[0, 0], modulation[0].transpose(1, 0, 2), spatial_qkv.T, spatial_out,
        temporal_qkv.T, temporal_out, cotangent[0],
    )
    return block_out[None], lat_grad[None, None], qkv_s, out_s.T, qkv_t, out_t.T


def solution(mesh):
    return jax.shard_map(
        body,
        mesh=mesh,
        in_specs=(
            P("dp", "seq", None, None),
            P("dp", None, None, None),
            P(),
            P(),
            P(),
            P(),
            P("dp", None, "seq", None),
        ),
        out_specs=(
            P("dp", None, "seq", None),
            P("dp", "seq", None, None),
            P(("dp", "seq"), None),
            P(None, ("dp", "seq")),
            P(("dp", "seq"), None),
            P(None, ("dp", "seq")),
        ),
        check_vma=False,
    )
```

```python
import functools
import math

import jax
import jax.numpy as jnp
from jax import lax
from jax.experimental import pallas as pl
from jax.experimental.pallas import tpu as pltpu
from jax.sharding import PartitionSpec as P

D = 1152
HEADS = 8
HEAD = 72
HD = 576
QKV = 3 * HD
FRAMES = 16
POS = 512
SPAN = 32
TOK = 512
SCALE = HEAD ** (-0.5)
EXP2 = SCALE / math.log(2.0)
MESH = pl.DeviceIdType.MESH
BF = jnp.bfloat16
F32 = jnp.float32
PIECES = 6
WIDE = 384

NN = (((1,), (0,)), ((), ()))
NT = (((1,), (1,)), ((), ()))
TN = (((0,), (0,)), ((), ()))


def mm(a, b, form=NN):
    return lax.dot_general(a, b, form, preferred_element_type=F32)


def vmem_spec():
    return pl.BlockSpec(memory_space=pltpu.VMEM)


def any_spec():
    return pl.BlockSpec(memory_space=pl.ANY)


def standardise(x):
    centre = jnp.mean(x, -1, keepdims=True)
    centred = x - centre
    spread = jnp.mean(centred * centred, -1, keepdims=True)
    rstd = lax.rsqrt(spread + 1e-06)
    return centred * rstd, rstd


def norm_backward(x, dnormed, scale):
    xhat, rstd = standardise(x)
    dxhat = dnormed * (1.0 + scale)
    first = jnp.mean(dxhat, -1, keepdims=True)
    second = jnp.mean(dxhat * xhat, -1, keepdims=True)
    return rstd * (dxhat - first - xhat * second)


def softmax(scores, mask=None):
    if mask is not None:
        scores = jnp.where(mask, scores, -1e30)
    largest = jnp.max(scores, 0, keepdims=True)
    expo = jnp.exp2((scores - largest) * EXP2)
    return expo * (1.0 / jnp.sum(expo, 0, keepdims=True))


def cols_of(part, h):
    return slice(part * HD + h * HEAD, part * HD + (h + 1) * HEAD)


def rows_of(h):
    return slice(h * HEAD, (h + 1) * HEAD)


def score_backward(p, dp):
    wide = p.astype(F32)
    return (wide * (dp - jnp.sum(dp * wide, 0, keepdims=True))).astype(BF)


def weight_grads(group, normed, dqkv, dproj, att, g):
    n = 2 * group
    for lo in range(0, D, 384):
        rows = slice(lo, lo + 384)
        if group < 2:
            both = mm(normed[:, rows], dqkv[:, n * WIDE : (n + 2) * WIDE], TN)
            g[n, rows, :] = both[:, :WIDE].astype(BF)
            g[n + 1, rows, :] = both[:, WIDE:].astype(BF)
        else:
            last = mm(normed[:, rows], dqkv[:, n * WIDE :], TN)
            outs = mm(dproj[:, rows], att[...], TN)
            g[n, rows, :192] = last.astype(BF)
            g[n, rows, 192:] = outs[:, :192].astype(BF)
            g[n + 1, rows, :] = outs[:, 192:].astype(BF)


def span_of(h2):
    return slice(h2 * 256, (h2 + 1) * 256)


def flat(ref, h2):
    return ref[h2].reshape(256, ref.shape[-1])


def spatial_norm(lat, mod, normed):
    shift, scale = mod[0, 0:1, :], mod[1, 0:1, :]
    for h2 in range(2):
        for lo in (0, 8):
            xhat, _ = standardise(lat[h2, lo : lo + 8].reshape(128, D).astype(F32))
            rows = slice(h2 * 256 + lo * 16, h2 * 256 + lo * 16 + 128)
            normed[rows, :] = (xhat * (1.0 + scale) + shift).astype(BF)


def project(normed, wq, qkv, spans):
    for h2 in spans:
        qkv[span_of(h2), :] = mm(normed[span_of(h2), :], wq[...], NT).astype(BF)


def spatial_heads(pair, qkv, probs, sb, turn):
    heads = [(pair * 2 + i, i) for i in range(2)]
    for h, i in heads:
        sb[i] = mm(qkv[:, cols_of(1, h)], qkv[:, cols_of(0, h)], NT)
    for h, i in heads:
        probs[h] = softmax(sb[i]).astype(BF)
    for h, i in heads:
        turn[rows_of(h), :] = mm(qkv[:, cols_of(2, h)], probs[h], TN).astype(BF)


def block_result(h2, x, mod, block, wo, att):
    gate = mod[2, block : block + 1, :]
    return (x + gate * mm(att, wo[...])).astype(BF)


def spatial_back_open(h2, mod, wo, dmid, dproj, datt):
    rows = span_of(h2)
    dpr = (flat(dmid, h2).astype(F32) * mod[2, 0:1, :]).astype(BF)
    dproj[rows, :] = dpr
    datt[rows, :] = mm(dpr, wo[...], NT).astype(BF)


def spatial_back_heads(pair, qkv, probs, datt, dqkv, sb, ds, turn):
    heads = [(pair * 2 + i, i) for i in range(2)]
    for h, i in heads:
        sb[i] = mm(qkv[:, cols_of(2, h)], datt[:, cols_of(0, h)], NT)
    for h, i in heads:
        ds[i] = score_backward(probs[h], sb[i])
    for h, i in heads:
        dqkv[:, cols_of(2, h)] = mm(probs[h], datt[:, cols_of(0, h)]).astype(BF)
    for h, i in heads:
        dqkv[:, cols_of(1, h)] = (mm(ds[i], qkv[:, cols_of(0, h)]) * SCALE).astype(BF)
    for h, i in heads:
        turn[rows_of(h), :] = (mm(qkv[:, cols_of(1, h)], ds[i], TN) * SCALE).astype(BF)


def block_gradient(h2, x, mod, block, wq, dy, dqkv):
    dnormed = mm(dqkv[span_of(h2), :], wq[...])
    dx = norm_backward(x.astype(F32), dnormed, mod[1, block : block + 1, :])
    return (dx + dy.astype(F32)).astype(BF).reshape(FRAMES, 16, D)


def temporal_open(h2, cot, mod, wo, dproj, datt):
    rows = span_of(h2)
    dpr = (flat(cot, h2).astype(F32) * mod[2, 1:2, :]).astype(BF)
    dproj[rows, :] = dpr
    datt[rows, :] = mm(dpr, wo[...], NT).astype(BF)


def temporal_norm(h2, mod, mid, normed):
    xhat, _ = standardise(flat(mid, h2).astype(F32))
    normed[span_of(h2), :] = (xhat * (1.0 + mod[1, 1:2, :]) + mod[0, 1:2, :]).astype(BF)


def tile_of(h):
    return h // 4, slice(h % 4 // 2 * 256, h % 4 // 2 * 256 + 256), slice(h % 2 * 256, h % 2 * 256 + 256)


def temporal_heads(h2, qkv, datt, dqkv, sb, pt, ds, turn):
    rows = span_of(h2)
    row_id = lax.broadcasted_iota(jnp.int32, (256, 256), 0)
    col_id = lax.broadcasted_iota(jnp.int32, (256, 256), 1)
    mask = (row_id & 15) == (col_id & 15)
    heads = [(h, tile_of(h)) for h in range(HEADS)]
    for h, at in heads:
        sb[at] = mm(qkv[rows, cols_of(1, h)], qkv[rows, cols_of(0, h)], NT)
    for h, at in heads:
        pt[at] = softmax(sb[at], mask).astype(BF)
    for h, at in heads:
        sb[at] = mm(qkv[rows, cols_of(2, h)], datt[rows, cols_of(0, h)], NT)
    for h, at in heads:
        ds[at] = score_backward(pt[at], sb[at])
    for h, at in heads:
        dqkv[rows, cols_of(2, h)] = mm(pt[at], datt[rows, cols_of(0, h)]).astype(BF)
    for h, at in heads:
        dqkv[rows, cols_of(1, h)] = (mm(ds[at], qkv[rows, cols_of(0, h)]) * SCALE).astype(BF)
    for h, at in heads:
        turn[rows_of(h), rows] = (mm(qkv[rows, cols_of(1, h)], ds[at], TN) * SCALE).astype(BF)
    dqkv[rows, 0:HD] = turn[:, rows].T


def temporal_attended(h2, qkv, pt, turn, att):
    rows = span_of(h2)
    for h in range(HEADS):
        turn[rows_of(h), rows] = mm(qkv[rows, cols_of(2, h)], pt[tile_of(h)], TN).astype(BF)
    att[rows, :] = turn[:, rows].T


class Exchange:
    def __init__(self, me, n, src_of, dst_of, send, recv, local):
        self.me, self.n, self.src_of, self.dst_of = me, n, src_of, dst_of
        self.send, self.recv, self.local = send, recv, local

    def copy(self, t, slot):
        return pltpu.make_async_remote_copy(
            src_ref=self.src_of(t),
            dst_ref=self.dst_of(slot),
            send_sem=self.send.at[self.n, t],
            recv_sem=self.recv.at[self.n, slot],
            device_id={"seq": t},
            device_id_type=MESH,
        )

    def own(self):
        return pltpu.make_async_copy(self.src_of(self.me), self.dst_of(self.me), self.local.at[self.n])

    def others(self, step):
        @pl.loop(1, FRAMES)
        def _(i):
            step(lax.rem(self.me + i, FRAMES))

    def start(self):
        y, x, c = lax.div(self.me, 8), lax.rem(lax.div(self.me, 2), 4), lax.rem(self.me, 2)
        for dc in range(2):
            for dy, dx in ((0, 1), (0, 3), (1, 0), (1, 1), (1, 3), (0, 2), (1, 2), (0, 0))[: 7 + dc]:
                t = lax.rem(y + dy, 2) * 8 + lax.rem(x + dx, 4) * 2 + lax.rem(c + dc, 2)
                self.copy(t, self.me).start()
        self.own().start()

    def arrive(self):
        self.others(lambda t: self.copy(t, t).wait_recv())
        self.own().wait()

    def drain(self):
        self.others(lambda t: self.copy(t, t).wait_send())


def spot(z, y, x, c):
    return {
        "dp": z * 2 + lax.div(y, 2),
        "seq": lax.rem(y, 2) * 8 + x * 2 + c,
    }


class Place:
    def __init__(self):
        dp, seq = lax.axis_index("dp"), lax.axis_index("seq")
        self.z = lax.div(dp, 2)
        self.y = lax.rem(dp, 2) * 2 + lax.div(seq, 8)
        self.x = lax.rem(lax.div(seq, 2), 4)
        self.c = lax.rem(seq, 2)
        self.at = (self.z, self.y, self.x)

    def moved(self, axis, j):
        return spot(*[j if i == axis else v for i, v in enumerate(self.at)], self.c)

    def partner(self):
        return spot(*self.at, 1 - self.c)


ORDERS = ((0, 1, 2), (1, 2, 0), (2, 0, 1))
CHUNK = 288
HALF = 144
BLOCK = 72
SLOT = 80


def odd_even(j):
    return j + 1 - 2 * lax.rem(j, 2)


def send_to(src, dst, send_sem, recv_sem, device):
    return pltpu.make_async_remote_copy(
        src_ref=src, dst_ref=dst, send_sem=send_sem, recv_sem=recv_sem, device_id=device, device_id_type=MESH
    )


class Reducer:
    def __init__(self, place, m, g, out, buf, sem):
        self.p, self.m, self.g, self.out, self.b, self.s = place, m, g, out, buf, sem

    def go0(self, k):
        return send_to(
            self.g.at[(1 - self.p.c) * 3 + k], self.b["r0"].at[self.m, k],
            self.s["s0"].at[self.m, k], self.s["v0"].at[self.m, k], self.p.partner(),
        )

    def chunk(self, j, half):
        return pl.ds(pl.multiple_of(j * CHUNK + half * HALF, 16), HALF)

    def ring(self, k, half):
        axis = ORDERS[k][0]
        j = self.p.at[axis]
        pair = (odd_even(j), 3 - j)
        return axis, j, pair[half], pair[1 - half]

    def go1(self, k, half, slot):
        axis, j, first, second = self.ring(k, half)
        other = 3 - first if half == 0 else odd_even(first)
        rows = self.chunk(first if slot == 0 else other, half)
        return send_to(
            self.b["r0"].at[self.m, k, rows], self.b["ra"].at[self.m, k, half, slot],
            self.s["sa"].at[self.m, k, half, slot], self.s["va"].at[self.m, k, half, slot],
            self.p.moved(axis, first),
        )

    def go2(self, k, half):
        axis, j, first, second = self.ring(k, half)
        return send_to(
            self.b["tb"].at[self.m, k, half], self.b["rb"].at[self.m, k, half],
            self.s["sb"].at[self.m, k, half], self.s["vb"].at[self.m, k, half],
            self.p.moved(axis, second),
        )

    def go3(self, k, to, slot):
        axis = ORDERS[k][1]
        return send_to(
            self.b["t2"].at[self.m, k, to], self.b["r2"].at[self.m, k, slot],
            self.s["s2"].at[self.m, k, to], self.s["v2"].at[self.m, k, slot],
            self.p.moved(axis, to),
        )

    def go4(self, k, x, c, s, e):
        a, b, _ = ORDERS[k]
        return send_to(
            self.b["t3"].at[self.m, k, x, c], self.b["r3"].at[self.m, k, s, e],
            self.s["s3"].at[self.m, k, x, c], self.s["v3"].at[self.m, k, s, e],
            spot(self.p.at[a], self.p.at[b], x, c),
        )

    def own4(self, k, x, c):
        s = self.p.at[ORDERS[k][2]]
        return pltpu.make_async_copy(
            self.b["t3"].at[self.m, k, x, c], self.b["r3"].at[self.m, k, s, self.p.c],
            self.s["v3"].at[self.m, k, s, self.p.c],
        )

    def to_self(self, k, x, c):
        p = self.p
        a, b, _ = ORDERS[k]
        return (p.at[a] == p.z) & (p.at[b] == p.y) & (x == p.x) & (c == p.c)


    def phase0(self, k):
        self.go0(k).start()

    def sent0(self):
        for k in range(3):
            self.go0(k).wait_send()

    def phase1(self, k):
        self.go0(k).wait_recv()
        r0 = self.b["r0"]
        n = self.p.c * 3 + k

        @pl.loop(0, D // HALF)
        def _(i):
            rows = pl.ds(pl.multiple_of(i * HALF, 16), HALF)
            r0[self.m, k, rows] = (
                r0[self.m, k, rows].astype(F32) + self.g[n, rows].astype(F32)
            ).astype(BF)

        for slot in (1, 0):
            for half in range(2):
                self.go1(k, half, slot).start()

    def phase2(self, k):
        for half in range(2):
            axis, j, first, second = self.ring(k, half)
            self.go1(k, half, 1).wait_recv()
            rows = self.chunk(second, half)
            self.b["tb"][self.m, k, half] = (
                self.b["r0"][self.m, k, rows].astype(F32) + self.b["ra"][self.m, k, half, 1].astype(F32)
            ).astype(BF)
            self.go2(k, half).start()

    def phase3(self, k):
        axis = ORDERS[k][1]
        me = self.p.at[axis]
        for half in range(2):
            _, j, _, _ = self.ring(k, half)
            self.go1(k, half, 0).wait_recv()
            self.go2(k, half).wait_recv()
            rows = self.chunk(j, half)
            total = (
                self.b["r0"][self.m, k, rows].astype(F32)
                + self.b["ra"][self.m, k, half, 0].astype(F32)
                + self.b["rb"][self.m, k, half].astype(F32)
            )
            for i in range(2):
                self.b["t2"][self.m, k, 2 * half + i, :BLOCK] = total[i * BLOCK : (i + 1) * BLOCK].astype(BF)
                self.b["t2"][self.m, k, 2 * half + i, BLOCK:] = jnp.zeros((SLOT - BLOCK, WIDE), BF)

        @pl.loop(1, 4)
        def _(i):
            self.go3(k, lax.rem(me + i, 4), me).start()

    def phase4(self, k):
        axis = ORDERS[k][1]
        me = self.p.at[axis]
        total = self.b["t2"][self.m, k, me].astype(F32)
        for i in range(1, 4):
            t = lax.rem(me + i, 4)
            self.go3(k, t, t).wait_recv()
            total = total + self.b["r2"][self.m, k, t].astype(F32)
        row = lax.broadcasted_iota(jnp.int32, (128, SLOT), 0)
        col = lax.broadcasted_iota(jnp.int32, (128, SLOT), 1)
        pick = ((row & 15) < 9) & (col == lax.shift_right_logical(row, 4) * 9 + (row & 15))
        spread = mm(jnp.where(pick, 1.0, 0.0).astype(BF), total.astype(BF)).astype(BF)
        for x in range(4):
            for c in range(2):
                lo = (x * 2 + c) * 16
                self.b["t3"][self.m, k, x, c] = spread[lo : lo + 16]
        s = self.p.at[ORDERS[k][2]]

        @pl.loop(0, 8)
        def _(i):
            x, c = lax.div(i, 2), lax.rem(i, 2)
            mine = self.to_self(k, x, c)

            @pl.when(mine)
            def _():
                self.own4(k, x, c).start()

            @pl.when(jnp.logical_not(mine))
            def _():
                self.go4(k, x, c, s, self.p.c).start()

    def phase5(self, k):
        p = self.p
        own = self.to_self(k, p.x, p.c)
        own_s = p.at[ORDERS[k][2]]

        @pl.loop(0, 8)
        def _(i):
            s, e = lax.div(i, 2), lax.rem(i, 2)
            mine = own & (s == own_s) & (e == p.c)

            @pl.when(mine)
            def _():
                self.own4(k, p.x, p.c).wait()

            @pl.when(jnp.logical_not(mine))
            def _():
                self.go4(k, s, e, s, e).wait_recv()

        for e in range(2):
            total = self.b["r3"][self.m, k, 0, e].astype(F32)
            for s in range(1, 4):
                total = total + self.b["r3"][self.m, k, s, e].astype(F32)
            n = e * 3 + k
            if n < 4:
                self.out[0][:, n * WIDE : (n + 1) * WIDE] = total[:9]
            elif n == 4:
                self.out[0][:, n * WIDE :] = total[:9, :192]
                self.out[1][:, :192] = total[:9, 192:]
            else:
                self.out[1][:, 192:] = total[:9]

    def drain(self):
        for k in range(3):
            me = self.p.at[ORDERS[k][1]]
            for half in range(2):
                self.go1(k, half, 0).wait_send()
                self.go1(k, half, 1).wait_send()
                self.go2(k, half).wait_send()

            @pl.loop(1, 4)
            def _(i):
                t = lax.rem(me + i, 4)
                self.go3(k, t, t).wait_send()

            @pl.loop(0, 8)
            def _(i):
                x, c = lax.div(i, 2), lax.rem(i, 2)

                @pl.when(jnp.logical_not(self.to_self(k, x, c)))
                def _():
                    self.go4(k, x, c, 0, 0).wait_send()


def greet(p, me):
    barrier = pltpu.get_barrier_semaphore()

    def hail(device):
        pl.semaphore_signal(barrier, inc=1, device_id=device, device_id_type=MESH)

    @pl.loop(1, FRAMES)
    def _(i):
        hail({"seq": lax.rem(me + i, FRAMES)})

    hail(p.partner())
    for axis in range(3):
        for i in range(1, 4):
            hail(p.moved(axis, lax.rem(p.at[axis] + i, 4)))
    selves = 0
    for k in range(3):
        a, b, c = ORDERS[k]

        @pl.loop(0, 8)
        def _(i):
            s, e = lax.div(i, 2), lax.rem(i, 2)
            where = [None] * 3
            where[a], where[b], where[c] = p.z, p.y, s
            same = (where[0] == p.z) & (where[1] == p.y) & (where[2] == p.x) & (e == p.c)

            @pl.when(jnp.logical_not(same))
            def _():
                hail(spot(*where, e))

        own = (p.at[a] == p.z) & (p.at[b] == p.y)
        selves = selves + jnp.where(own & (p.at[c] == p.x), 1, 0)
    return FRAMES - 1 + 10 + 24 - selves


def reduce_buffers(count):
    dma = pltpu.SemaphoreType.DMA
    bufs = dict(
        r0=pltpu.VMEM((count, 3, D, WIDE), BF),
        ra=pltpu.VMEM((count, 3, 2, 2, HALF, WIDE), BF),
        tb=pltpu.VMEM((count, 3, 2, HALF, WIDE), BF),
        rb=pltpu.VMEM((count, 3, 2, HALF, WIDE), BF),
        t2=pltpu.VMEM((count, 3, 4, SLOT, WIDE), BF),
        r2=pltpu.VMEM((count, 3, 4, SLOT, WIDE), BF),
        t3=pltpu.VMEM((count, 3, 4, 2, 16, WIDE), BF),
        r3=pltpu.VMEM((count, 3, 4, 2, 16, WIDE), BF),
    )
    sems = {}
    for end in "sv":
        sems[end + "0"] = dma((count, 3))
        sems[end + "a"] = dma((count, 3, 2, 2))
        sems[end + "b"] = dma((count, 3, 2))
        sems[end + "2"] = dma((count, 3, 4))
        sems[end + "3"] = dma((count, 3, 4, 2))
    return bufs, sems


def kernel(ins, outs, v, sem, buf, rsem):
    me = lax.axis_index("seq")
    p = Place()
    mod = ins["mod"]
    lat, cot, mid, dmid, g = v["lat"], v["cot"], v["mid"], v["dmid"], v["g"]

    def load(src, dst, n):
        return pltpu.make_async_copy(src, dst, sem["load"].at[n])

    loads = {}
    for n, (k, h2) in enumerate((("lat", 0), ("lat", 1), ("cot", 0), ("cot", 1))):
        loads[k, h2] = load(ins[k].at[:, h2], v[k].at[h2], n)
    for n, k in enumerate(("wq_s", "wo_s", "wo_t", "wq_t")):
        loads[k] = load(ins[k], v[k], 4 + n)
    order = (("lat", 0), ("lat", 1), "wq_s", "wo_s", ("cot", 0), ("cot", 1), "wo_t", "wq_t")
    for k in order:
        loads[k].start()
    expected = greet(p, me)

    def exchange(n, src_of, dst_of):
        return Exchange(me, n, src_of, dst_of, sem["send"], sem["recv"], sem["local"])

    def frame_rows(t):
        return pl.ds(pl.multiple_of(t * 16, 16), 16)

    lat_x = exchange(0, lambda t: lat.at[0, t], lambda s: v["lat_in"].at[s])
    att_x = exchange(1, lambda t: v["att_s"].at[frame_rows(t)], lambda s: v["att_in"].at[s])
    mid_x = exchange(2, lambda t: v["mid_s"].at[frame_rows(t)], lambda s: mid.at[1, s])
    dmid_x = [
        exchange(3 + h2, lambda t, h2=h2: v["dmid_t"].at[h2, t], lambda s, h2=h2: dmid.at[h2, s])
        for h2 in range(2)
    ]
    red_t = Reducer(p, 0, g, (outs["qkv_t"], outs["out_t"]), buf, rsem)
    red_s = Reducer(p, 1, g, (outs["qkv_s"], outs["out_s"]), buf, rsem)

    def reduce_step(red, name, ks=(1, 0, 2)):
        for k in ks:
            getattr(red, name)(k)

    loads["lat", 0].wait()
    loads["lat", 1].wait()
    spatial_norm(lat, mod, v["normed_s"])
    pl.semaphore_wait(pltpu.get_barrier_semaphore(), expected)
    lat_x.start()
    loads["wq_s"].wait()
    project(v["normed_s"], v["wq_s"], v["qkv_s"], (0, 1))
    for pair in range(4):
        spatial_heads(pair, v["qkv_s"], v["probs"], v["sb"], v["turn"])
    v["att_s"][...] = v["turn"][...].T
    att_x.start()
    loads["wo_s"].wait()
    v["mid_s"][...] = block_result(1, flat(lat, 1).astype(F32), mod, 0, v["wo_s"], v["att_s"][256:, :])
    mid_x.start()

    for k in order[4:]:
        loads[k].wait()
    for h2 in range(2):
        temporal_open(h2, cot, mod, v["wo_t"], v["dproj"], v["datt"])
    for h2 in range(2):
        if h2 == 0:
            lat_x.arrive()
            att_x.arrive()
            x = v["lat_in"][...].reshape(256, D).astype(F32)
            att_in = v["att_in"][...].reshape(256, HD)
            mid[0] = block_result(0, x, mod, 0, v["wo_s"], att_in).reshape(FRAMES, 16, D)
        else:
            mid_x.arrive()
        temporal_norm(h2, mod, mid, v["normed_t"])
        project(v["normed_t"], v["wq_t"], v["qkv_t"], (h2,))
        temporal_heads(h2, v["qkv_t"], v["datt"], v["dqkv"], v["sb"], v["pt"], v["ds"], v["turn"])
        v["dmid_t"][h2] = block_gradient(h2, flat(mid, h2), mod, 1, v["wq_t"], flat(cot, h2), v["dqkv"])
        dmid_x[h2].start()
        temporal_attended(h2, v["qkv_t"], v["pt"], v["turn"], v["att_t"])
    for group, ready in ((2, ()), (0, (1,)), (1, (0, 2))):
        weight_grads(group, v["normed_t"], v["dqkv"], v["dproj"], v["att_t"], g)
        reduce_step(red_t, "phase0", ready)
    store_out = []
    for h2 in range(2):
        y = block_result(h2, flat(mid, h2).astype(F32), mod, 1, v["wo_t"], v["att_t"][span_of(h2), :])
        v["block_out"][h2] = y.reshape(FRAMES, 16, D)
        store_out.append(pltpu.make_async_copy(v["block_out"].at[h2], outs["block_out"].at[:, h2], sem["store"].at[h2]))
        store_out[h2].start()

    for h2 in range(2):
        dmid_x[h2].arrive()
        spatial_back_open(h2, mod, v["wo_s"], dmid, v["dproj"], v["datt"])
    for pair in range(4):
        if pair == 2:
            reduce_step(red_t, "phase1")
        spatial_back_heads(pair, v["qkv_s"], v["probs"], v["datt"], v["dqkv"], v["sb"], v["ds"], v["turn"])
    v["dqkv"][:, 0:HD] = v["turn"][...].T
    red_t.sent0()
    for group, ready in ((2, ()), (0, (1,)), (1, (0, 2))):
        weight_grads(group, v["normed_s"], v["dqkv"], v["dproj"], v["att_s"], g)
        reduce_step(red_s, "phase0", ready)
    reduce_step(red_t, "phase2")
    lat_grad = mid
    store_grad = []
    for h2 in range(2):
        lat_grad[h2] = block_gradient(h2, flat(lat, h2), mod, 0, v["wq_s"], flat(dmid, h2), v["dqkv"])
        store_grad.append(pltpu.make_async_copy(lat_grad.at[h2], outs["lat_grad"].at[:, h2], sem["store"].at[2 + h2]))
        store_grad[h2].start()
        if h2 == 0:
            reduce_step(red_t, "phase3")

    reduce_step(red_s, "phase1")
    reduce_step(red_t, "phase4")
    reduce_step(red_s, "phase2")
    reduce_step(red_t, "phase5")
    reduce_step(red_s, "phase3")
    reduce_step(red_s, "phase4")
    for c in store_out + store_grad:
        c.wait()
    for x in [lat_x, att_x, mid_x] + dmid_x:
        x.drain()
    red_s.sent0()
    red_t.drain()
    reduce_step(red_s, "phase5")
    red_s.drain()


def shape(dims, kind=BF):
    return jax.ShapeDtypeStruct(dims, kind)


def params(collective_id=None):
    if collective_id is None:
        return pltpu.CompilerParams(vmem_limit_bytes=VMEM_LIMIT)
    return pltpu.CompilerParams(
        vmem_limit_bytes=VMEM_LIMIT, collective_id=collective_id, has_side_effects=True
    )


VMEM_LIMIT = 62 * 1024 * 1024
INPUTS = ("lat", "mod", "wq_s", "wo_s", "wq_t", "wo_t", "cot")
OUTPUTS = {
    "block_out": shape((FRAMES, 2, 16, D)),
    "lat_grad": shape((FRAMES, 2, 16, D)),
    "qkv_s": shape((9, QKV), F32),
    "out_s": shape((9, HD), F32),
    "qkv_t": shape((9, QKV), F32),
    "out_t": shape((9, HD), F32),
}
HALVES = (2, FRAMES, 16, D)
VALUES = {
    "lat": HALVES, "cot": HALVES,
    "wq_s": (QKV, D), "wo_s": (HD, D), "wq_t": (QKV, D), "wo_t": (HD, D),
    "normed_s": (TOK, D), "qkv_s": (TOK, QKV), "probs": (HEADS, TOK, TOK), "att_s": (TOK, HD),
    "mid_s": (256, D), "lat_in": HALVES[1:], "att_in": (FRAMES, 16, HD),
    "mid": HALVES, "normed_t": (TOK, D), "qkv_t": (TOK, QKV), "att_t": (TOK, HD),
    "dproj": (TOK, D), "datt": (TOK, HD), "dqkv": (TOK, QKV),
    "sb": (2, TOK, TOK), "pt": (2, TOK, TOK), "ds": (2, TOK, TOK), "turn": (HD, TOK),
    "dmid_t": HALVES, "dmid": HALVES, "block_out": HALVES,
    "g": (PIECES, D, WIDE),
}
KINDS = {"sb": F32}


def run(*args):
    dma = pltpu.SemaphoreType.DMA
    bufs, rsems = reduce_buffers(2)
    sems = {
        "load": dma((8,)), "store": dma((4,)),
        "send": dma((5, FRAMES)), "recv": dma((5, FRAMES)), "local": dma((5,)),
    }
    values = {k: pltpu.VMEM(d, KINDS.get(k, BF)) for k, d in VALUES.items()}
    groups = (values, sems, bufs, rsems)

    def unpack(*refs):
        refs = list(refs)

        def take(names):
            got = dict(zip(names, refs))
            del refs[: len(got)]
            return got

        kernel(take(INPUTS), take(OUTPUTS), *[take(g) for g in groups])

    return pl.pallas_call(
        unpack,
        out_shape=tuple(OUTPUTS.values()),
        in_specs=[vmem_spec() if k == "mod" else any_spec() for k in INPUTS],
        out_specs=[any_spec()] * 2 + [vmem_spec()] * 4,
        scratch_shapes=[x for g in groups for x in g.values()],
        compiler_params=params(0),
        name="attention_blocks",
    )(*args)


def hand_over(*refs):
    n = len(refs) // 2
    sems = refs[-1]
    copies = [pltpu.make_async_copy(refs[i], refs[n + i], sems.at[i]) for i in range(n)]
    for c in copies:
        c.start()
    for c in copies:
        c.wait()


def body(latents, modulation, spatial_qkv, spatial_out, temporal_qkv, temporal_out, cotangent):
    halves = (FRAMES, 2, 16, D)
    results = run(
        latents.reshape(halves), modulation[0].transpose(1, 0, 2), spatial_qkv.T, spatial_out,
        temporal_qkv.T, temporal_out, cotangent.reshape(halves),
    )
    block_out, lat_grad, qkv_s, out_s, qkv_t, out_t = pl.pallas_call(
        hand_over,
        out_shape=tuple(OUTPUTS.values()),
        in_specs=[any_spec()] * 6,
        out_specs=[any_spec()] * 6,
        scratch_shapes=[pltpu.SemaphoreType.DMA((6,))],
        compiler_params=params(),
        name="hand_over",
    )(*results)
    return (
        block_out.reshape(1, FRAMES, SPAN, D), lat_grad.reshape(1, 1, TOK, D),
        qkv_s, out_s.T, qkv_t, out_t.T,
    )


def solution(mesh):
    return jax.shard_map(
        body,
        mesh=mesh,
        in_specs=(
            P("dp", "seq", None, None),
            P("dp", None, None, None),
            P(),
            P(),
            P(),
            P(),
            P("dp", None, "seq", None),
        ),
        out_specs=(
            P("dp", None, "seq", None),
            P("dp", "seq", None, None),
            P(("dp", "seq"), None),
            P(None, ("dp", "seq")),
            P(("dp", "seq"), None),
            P(None, ("dp", "seq")),
        ),
        check_vma=False,
    )
```

```python
import functools
import math

import jax
import jax.numpy as jnp
from jax import lax
from jax.experimental import pallas as pl
from jax.experimental.pallas import tpu as pltpu
from jax.sharding import PartitionSpec as P

D = 1152
HEADS = 8
HEAD = 72
HD = 576
QKV = 3 * HD
FRAMES = 16
POS = 512
SPAN = 32
TOK = 512
SCALE = HEAD ** (-0.5)
EXP2 = SCALE / math.log(2.0)
MESH = pl.DeviceIdType.MESH
BF = jnp.bfloat16
F32 = jnp.float32
PIECES = 6
WIDE = 384

NN = (((1,), (0,)), ((), ()))
NT = (((1,), (1,)), ((), ()))
TN = (((0,), (0,)), ((), ()))


def mm(a, b, form=NN):
    return lax.dot_general(a, b, form, preferred_element_type=F32)


def vmem_spec():
    return pl.BlockSpec(memory_space=pltpu.VMEM)


def any_spec():
    return pl.BlockSpec(memory_space=pl.ANY)


def standardise(x):
    centre = jnp.mean(x, -1, keepdims=True)
    centred = x - centre
    spread = jnp.mean(centred * centred, -1, keepdims=True)
    rstd = lax.rsqrt(spread + 1e-06)
    return centred * rstd, rstd


def norm_backward(x, dnormed, scale):
    xhat, rstd = standardise(x)
    dxhat = dnormed * (1.0 + scale)
    first = jnp.mean(dxhat, -1, keepdims=True)
    second = jnp.mean(dxhat * xhat, -1, keepdims=True)
    return rstd * (dxhat - first - xhat * second)


def softmax(scores, mask=None):
    if mask is not None:
        scores = jnp.where(mask, scores, -1e30)
    largest = jnp.max(scores, 0, keepdims=True)
    expo = jnp.exp2((scores - largest) * EXP2)
    return expo * (1.0 / jnp.sum(expo, 0, keepdims=True))


def cols_of(part, h):
    return slice(part * HD + h * HEAD, part * HD + (h + 1) * HEAD)


def rows_of(h):
    return slice(h * HEAD, (h + 1) * HEAD)


def score_backward(p, dp):
    wide = p.astype(F32)
    return (wide * (dp - jnp.sum(dp * wide, 0, keepdims=True))).astype(BF)


def weight_grads(group, normed, dqkv, dproj, att, g):
    n = 2 * group
    for lo in range(0, D, 384):
        rows = slice(lo, lo + 384)
        if group < 2:
            both = mm(normed[:, rows], dqkv[:, n * WIDE : (n + 2) * WIDE], TN)
            g[n, rows, :] = both[:, :WIDE].astype(BF)
            g[n + 1, rows, :] = both[:, WIDE:].astype(BF)
        else:
            last = mm(normed[:, rows], dqkv[:, n * WIDE :], TN)
            outs = mm(dproj[:, rows], att[...], TN)
            g[n, rows, :192] = last.astype(BF)
            g[n, rows, 192:] = outs[:, :192].astype(BF)
            g[n + 1, rows, :] = outs[:, 192:].astype(BF)


def span_of(h2):
    return slice(h2 * 256, (h2 + 1) * 256)


def flat(ref, h2):
    return ref[h2].reshape(256, ref.shape[-1])


def spatial_norm(lat, mod, normed):
    shift, scale = mod[0, 0:1, :], mod[1, 0:1, :]
    for h2 in range(2):
        for lo in (0, 8):
            xhat, _ = standardise(lat[h2, lo : lo + 8].reshape(128, D).astype(F32))
            rows = slice(h2 * 256 + lo * 16, h2 * 256 + lo * 16 + 128)
            normed[rows, :] = (xhat * (1.0 + scale) + shift).astype(BF)


def project(normed, wq, qkv, spans):
    for h2 in spans:
        qkv[span_of(h2), :] = mm(normed[span_of(h2), :], wq[...], NT).astype(BF)


def spatial_heads(pair, qkv, probs, sb, turn):
    heads = [(pair * 2 + i, i) for i in range(2)]
    for h, i in heads:
        sb[i] = mm(qkv[:, cols_of(1, h)], qkv[:, cols_of(0, h)], NT)
    for h, i in heads:
        probs[h] = softmax(sb[i]).astype(BF)
    for h, i in heads:
        turn[rows_of(h), :] = mm(qkv[:, cols_of(2, h)], probs[h], TN).astype(BF)


def block_result(h2, x, mod, block, wo, att):
    gate = mod[2, block : block + 1, :]
    return (x + gate * mm(att, wo[...])).astype(BF)


def spatial_back_open(h2, mod, wo, dmid, dproj, datt):
    rows = span_of(h2)
    dpr = (flat(dmid, h2).astype(F32) * mod[2, 0:1, :]).astype(BF)
    dproj[rows, :] = dpr
    datt[rows, :] = mm(dpr, wo[...], NT).astype(BF)


def spatial_back_heads(pair, qkv, probs, datt, dqkv, sb, ds, turn):
    heads = [(pair * 2 + i, i) for i in range(2)]
    for h, i in heads:
        sb[i] = mm(qkv[:, cols_of(2, h)], datt[:, cols_of(0, h)], NT)
    for h, i in heads:
        ds[i] = score_backward(probs[h], sb[i])
    for h, i in heads:
        dqkv[:, cols_of(2, h)] = mm(probs[h], datt[:, cols_of(0, h)]).astype(BF)
    for h, i in heads:
        dqkv[:, cols_of(1, h)] = (mm(ds[i], qkv[:, cols_of(0, h)]) * SCALE).astype(BF)
    for h, i in heads:
        turn[rows_of(h), :] = (mm(qkv[:, cols_of(1, h)], ds[i], TN) * SCALE).astype(BF)


def block_gradient(h2, x, mod, block, wq, dy, dqkv):
    dnormed = mm(dqkv[span_of(h2), :], wq[...])
    dx = norm_backward(x.astype(F32), dnormed, mod[1, block : block + 1, :])
    return (dx + dy.astype(F32)).astype(BF).reshape(FRAMES, 16, D)


def temporal_open(h2, cot, mod, wo, dproj, datt):
    rows = span_of(h2)
    dpr = (flat(cot, h2).astype(F32) * mod[2, 1:2, :]).astype(BF)
    dproj[rows, :] = dpr
    datt[rows, :] = mm(dpr, wo[...], NT).astype(BF)


def temporal_norm(h2, mod, mid, normed):
    xhat, _ = standardise(flat(mid, h2).astype(F32))
    normed[span_of(h2), :] = (xhat * (1.0 + mod[1, 1:2, :]) + mod[0, 1:2, :]).astype(BF)


def pair_of(part, pair):
    return slice(part * HD + pair * 2 * HEAD, part * HD + (pair + 1) * 2 * HEAD)


def split_pair(x):
    first = lax.broadcasted_iota(jnp.int32, x.shape, 1) < HEAD
    zero = jnp.zeros_like(x)
    return jnp.concatenate([jnp.where(first, x, zero), jnp.where(first, zero, x)], 0)


def pair_tile(pair):
    return pair // 2, slice(pair % 2 * 256, pair % 2 * 256 + 256), slice(0, 512)


def temporal_heads(h2, qkv, datt, dqkv, sb, pt, ds, turn):
    rows = span_of(h2)
    row_id = lax.broadcasted_iota(jnp.int32, (256, 512), 0)
    col_id = lax.broadcasted_iota(jnp.int32, (256, 512), 1)
    mask = (row_id & 15) == (col_id & 15)
    pairs = [(n, pair_tile(n)) for n in range(HEADS // 2)]
    for n, at in pairs:
        sb[at] = mm(qkv[rows, pair_of(1, n)], split_pair(qkv[rows, pair_of(0, n)]), NT)
    for n, at in pairs:
        pt[at] = softmax(sb[at], mask).astype(BF)
    for n, at in pairs:
        sb[at] = mm(qkv[rows, pair_of(2, n)], split_pair(datt[rows, pair_of(0, n)]), NT)
    for n, at in pairs:
        ds[at] = score_backward(pt[at], sb[at])
    for n, at in pairs:
        dqkv[rows, pair_of(2, n)] = mm(pt[at], split_pair(datt[rows, pair_of(0, n)])).astype(BF)
    for n, at in pairs:
        dqkv[rows, pair_of(1, n)] = (mm(ds[at], split_pair(qkv[rows, pair_of(0, n)])) * SCALE).astype(BF)
    for n, at in pairs:
        both = mm(qkv[rows, pair_of(1, n)], ds[at], TN) * SCALE
        turn[rows_of(2 * n), rows] = both[:HEAD, :256].astype(BF)
        turn[rows_of(2 * n + 1), rows] = both[HEAD:, 256:].astype(BF)
    dqkv[rows, 0:HD] = turn[:, rows].T


def temporal_attended(h2, qkv, pt, turn, att):
    rows = span_of(h2)
    for n in range(HEADS // 2):
        both = mm(qkv[rows, pair_of(2, n)], pt[pair_tile(n)], TN)
        turn[rows_of(2 * n), rows] = both[:HEAD, :256].astype(BF)
        turn[rows_of(2 * n + 1), rows] = both[HEAD:, 256:].astype(BF)
    att[rows, :] = turn[:, rows].T


class Exchange:
    def __init__(self, me, n, src_of, dst_of, send, recv, local):
        self.me, self.n, self.src_of, self.dst_of = me, n, src_of, dst_of
        self.send, self.recv, self.local = send, recv, local

    def copy(self, t, slot):
        return pltpu.make_async_remote_copy(
            src_ref=self.src_of(t),
            dst_ref=self.dst_of(slot),
            send_sem=self.send.at[self.n, t],
            recv_sem=self.recv.at[self.n, slot],
            device_id={"seq": t},
            device_id_type=MESH,
        )

    def own(self):
        return pltpu.make_async_copy(self.src_of(self.me), self.dst_of(self.me), self.local.at[self.n])

    def others(self, step):
        @pl.loop(1, FRAMES)
        def _(i):
            step(lax.rem(self.me + i, FRAMES))

    def start(self):
        y, x, c = lax.div(self.me, 8), lax.rem(lax.div(self.me, 2), 4), lax.rem(self.me, 2)
        for dc in range(2):
            for dy, dx in ((0, 1), (0, 3), (1, 0), (1, 1), (1, 3), (0, 2), (1, 2), (0, 0))[: 7 + dc]:
                t = lax.rem(y + dy, 2) * 8 + lax.rem(x + dx, 4) * 2 + lax.rem(c + dc, 2)
                self.copy(t, self.me).start()
        self.own().start()

    def arrive(self):
        self.others(lambda t: self.copy(t, t).wait_recv())
        self.own().wait()

    def drain(self):
        self.others(lambda t: self.copy(t, t).wait_send())


def spot(z, y, x, c):
    return {
        "dp": z * 2 + lax.div(y, 2),
        "seq": lax.rem(y, 2) * 8 + x * 2 + c,
    }


class Place:
    def __init__(self):
        dp, seq = lax.axis_index("dp"), lax.axis_index("seq")
        self.z = lax.div(dp, 2)
        self.y = lax.rem(dp, 2) * 2 + lax.div(seq, 8)
        self.x = lax.rem(lax.div(seq, 2), 4)
        self.c = lax.rem(seq, 2)
        self.at = (self.z, self.y, self.x)

    def moved(self, axis, j):
        return spot(*[j if i == axis else v for i, v in enumerate(self.at)], self.c)

    def partner(self):
        return spot(*self.at, 1 - self.c)


ORDERS = ((0, 1, 2), (1, 2, 0), (2, 0, 1))
CHUNK = 288
HALF = 144
BLOCK = 72
SLOT = 80


def odd_even(j):
    return j + 1 - 2 * lax.rem(j, 2)


def send_to(src, dst, send_sem, recv_sem, device):
    return pltpu.make_async_remote_copy(
        src_ref=src, dst_ref=dst, send_sem=send_sem, recv_sem=recv_sem, device_id=device, device_id_type=MESH
    )


class Reducer:
    def __init__(self, place, m, g, out, buf, sem):
        self.p, self.m, self.g, self.out, self.b, self.s = place, m, g, out, buf, sem

    def go0(self, k):
        return send_to(
            self.g.at[(1 - self.p.c) * 3 + k], self.b["r0"].at[self.m, k],
            self.s["s0"].at[self.m, k], self.s["v0"].at[self.m, k], self.p.partner(),
        )

    def chunk(self, j, half):
        return pl.ds(pl.multiple_of(j * CHUNK + half * HALF, 16), HALF)

    def ring(self, k, half):
        axis = ORDERS[k][0]
        j = self.p.at[axis]
        pair = (odd_even(j), 3 - j)
        return axis, j, pair[half], pair[1 - half]

    def go1(self, k, half, slot):
        axis, j, first, second = self.ring(k, half)
        other = 3 - first if half == 0 else odd_even(first)
        rows = self.chunk(first if slot == 0 else other, half)
        return send_to(
            self.b["r0"].at[self.m, k, rows], self.b["ra"].at[self.m, k, half, slot],
            self.s["sa"].at[self.m, k, half, slot], self.s["va"].at[self.m, k, half, slot],
            self.p.moved(axis, first),
        )

    def go2(self, k, half):
        axis, j, first, second = self.ring(k, half)
        return send_to(
            self.b["tb"].at[self.m, k, half], self.b["rb"].at[self.m, k, half],
            self.s["sb"].at[self.m, k, half], self.s["vb"].at[self.m, k, half],
            self.p.moved(axis, second),
        )

    def go3(self, k, to, slot):
        axis = ORDERS[k][1]
        return send_to(
            self.b["t2"].at[self.m, k, to], self.b["r2"].at[self.m, k, slot],
            self.s["s2"].at[self.m, k, to], self.s["v2"].at[self.m, k, slot],
            self.p.moved(axis, to),
        )

    def go4(self, k, x, c, s, e):
        a, b, _ = ORDERS[k]
        return send_to(
            self.b["t3"].at[self.m, k, x, c], self.b["r3"].at[self.m, k, s, e],
            self.s["s3"].at[self.m, k, x, c], self.s["v3"].at[self.m, k, s, e],
            spot(self.p.at[a], self.p.at[b], x, c),
        )

    def own4(self, k, x, c):
        s = self.p.at[ORDERS[k][2]]
        return pltpu.make_async_copy(
            self.b["t3"].at[self.m, k, x, c], self.b["r3"].at[self.m, k, s, self.p.c],
            self.s["v3"].at[self.m, k, s, self.p.c],
        )

    def to_self(self, k, x, c):
        p = self.p
        a, b, _ = ORDERS[k]
        return (p.at[a] == p.z) & (p.at[b] == p.y) & (x == p.x) & (c == p.c)


    def phase0(self, k):
        self.go0(k).start()

    def sent0(self):
        for k in range(3):
            self.go0(k).wait_send()

    def phase1(self, k):
        self.go0(k).wait_recv()
        r0 = self.b["r0"]
        n = self.p.c * 3 + k

        @pl.loop(0, D // HALF)
        def _(i):
            rows = pl.ds(pl.multiple_of(i * HALF, 16), HALF)
            r0[self.m, k, rows] = (
                r0[self.m, k, rows].astype(F32) + self.g[n, rows].astype(F32)
            ).astype(BF)

        for slot in (1, 0):
            for half in range(2):
                self.go1(k, half, slot).start()

    def phase2(self, k):
        for half in range(2):
            axis, j, first, second = self.ring(k, half)
            self.go1(k, half, 1).wait_recv()
            rows = self.chunk(second, half)
            self.b["tb"][self.m, k, half] = (
                self.b["r0"][self.m, k, rows].astype(F32) + self.b["ra"][self.m, k, half, 1].astype(F32)
            ).astype(BF)
            self.go2(k, half).start()

    def phase3(self, k):
        axis = ORDERS[k][1]
        me = self.p.at[axis]
        for half in range(2):
            _, j, _, _ = self.ring(k, half)
            self.go1(k, half, 0).wait_recv()
            self.go2(k, half).wait_recv()
            rows = self.chunk(j, half)
            total = (
                self.b["r0"][self.m, k, rows].astype(F32)
                + self.b["ra"][self.m, k, half, 0].astype(F32)
                + self.b["rb"][self.m, k, half].astype(F32)
            )
            for i in range(2):
                self.b["t2"][self.m, k, 2 * half + i, :BLOCK] = total[i * BLOCK : (i + 1) * BLOCK].astype(BF)
                self.b["t2"][self.m, k, 2 * half + i, BLOCK:] = jnp.zeros((SLOT - BLOCK, WIDE), BF)

        @pl.loop(1, 4)
        def _(i):
            self.go3(k, lax.rem(me + i, 4), me).start()

    def phase4(self, k):
        axis = ORDERS[k][1]
        me = self.p.at[axis]
        total = self.b["t2"][self.m, k, me].astype(F32)
        for i in range(1, 4):
            t = lax.rem(me + i, 4)
            self.go3(k, t, t).wait_recv()
            total = total + self.b["r2"][self.m, k, t].astype(F32)
        row = lax.broadcasted_iota(jnp.int32, (128, SLOT), 0)
        col = lax.broadcasted_iota(jnp.int32, (128, SLOT), 1)
        pick = ((row & 15) < 9) & (col == lax.shift_right_logical(row, 4) * 9 + (row & 15))
        spread = mm(jnp.where(pick, 1.0, 0.0).astype(BF), total.astype(BF)).astype(BF)
        for x in range(4):
            for c in range(2):
                lo = (x * 2 + c) * 16
                self.b["t3"][self.m, k, x, c] = spread[lo : lo + 16]
        s = self.p.at[ORDERS[k][2]]

        @pl.loop(0, 8)
        def _(i):
            x, c = lax.div(i, 2), lax.rem(i, 2)
            mine = self.to_self(k, x, c)

            @pl.when(mine)
            def _():
                self.own4(k, x, c).start()

            @pl.when(jnp.logical_not(mine))
            def _():
                self.go4(k, x, c, s, self.p.c).start()

    def phase5(self, k):
        p = self.p
        own = self.to_self(k, p.x, p.c)
        own_s = p.at[ORDERS[k][2]]

        @pl.loop(0, 8)
        def _(i):
            s, e = lax.div(i, 2), lax.rem(i, 2)
            mine = own & (s == own_s) & (e == p.c)

            @pl.when(mine)
            def _():
                self.own4(k, p.x, p.c).wait()

            @pl.when(jnp.logical_not(mine))
            def _():
                self.go4(k, s, e, s, e).wait_recv()

        for e in range(2):
            total = self.b["r3"][self.m, k, 0, e].astype(F32)
            for s in range(1, 4):
                total = total + self.b["r3"][self.m, k, s, e].astype(F32)
            n = e * 3 + k
            if n < 4:
                self.out[0][:, n * WIDE : (n + 1) * WIDE] = total[:9]
            elif n == 4:
                self.out[0][:, n * WIDE :] = total[:9, :192]
                self.out[1][:, :192] = total[:9, 192:]
            else:
                self.out[1][:, 192:] = total[:9]

    def drain(self):
        for k in range(3):
            me = self.p.at[ORDERS[k][1]]
            for half in range(2):
                self.go1(k, half, 0).wait_send()
                self.go1(k, half, 1).wait_send()
                self.go2(k, half).wait_send()

            @pl.loop(1, 4)
            def _(i):
                t = lax.rem(me + i, 4)
                self.go3(k, t, t).wait_send()

            @pl.loop(0, 8)
            def _(i):
                x, c = lax.div(i, 2), lax.rem(i, 2)

                @pl.when(jnp.logical_not(self.to_self(k, x, c)))
                def _():
                    self.go4(k, x, c, 0, 0).wait_send()


def greet(p, me):
    barrier = pltpu.get_barrier_semaphore()

    def hail(device):
        pl.semaphore_signal(barrier, inc=1, device_id=device, device_id_type=MESH)

    @pl.loop(1, FRAMES)
    def _(i):
        hail({"seq": lax.rem(me + i, FRAMES)})

    hail(p.partner())
    for axis in range(3):
        for i in range(1, 4):
            hail(p.moved(axis, lax.rem(p.at[axis] + i, 4)))
    selves = 0
    for k in range(3):
        a, b, c = ORDERS[k]

        @pl.loop(0, 8)
        def _(i):
            s, e = lax.div(i, 2), lax.rem(i, 2)
            where = [None] * 3
            where[a], where[b], where[c] = p.z, p.y, s
            same = (where[0] == p.z) & (where[1] == p.y) & (where[2] == p.x) & (e == p.c)

            @pl.when(jnp.logical_not(same))
            def _():
                hail(spot(*where, e))

        own = (p.at[a] == p.z) & (p.at[b] == p.y)
        selves = selves + jnp.where(own & (p.at[c] == p.x), 1, 0)
    return FRAMES - 1 + 10 + 24 - selves


def reduce_buffers(count):
    dma = pltpu.SemaphoreType.DMA
    bufs = dict(
        r0=pltpu.VMEM((count, 3, D, WIDE), BF),
        ra=pltpu.VMEM((count, 3, 2, 2, HALF, WIDE), BF),
        tb=pltpu.VMEM((count, 3, 2, HALF, WIDE), BF),
        rb=pltpu.VMEM((count, 3, 2, HALF, WIDE), BF),
        t2=pltpu.VMEM((count, 3, 4, SLOT, WIDE), BF),
        r2=pltpu.VMEM((count, 3, 4, SLOT, WIDE), BF),
        t3=pltpu.VMEM((count, 3, 4, 2, 16, WIDE), BF),
        r3=pltpu.VMEM((count, 3, 4, 2, 16, WIDE), BF),
    )
    sems = {}
    for end in "sv":
        sems[end + "0"] = dma((count, 3))
        sems[end + "a"] = dma((count, 3, 2, 2))
        sems[end + "b"] = dma((count, 3, 2))
        sems[end + "2"] = dma((count, 3, 4))
        sems[end + "3"] = dma((count, 3, 4, 2))
    return bufs, sems


def kernel(ins, outs, v, sem, buf, rsem):
    me = lax.axis_index("seq")
    p = Place()
    mod = ins["mod"]
    lat, cot, mid, dmid, g = v["lat"], v["cot"], v["mid"], v["dmid"], v["g"]

    def load(src, dst, n):
        return pltpu.make_async_copy(src, dst, sem["load"].at[n])

    loads = {}
    for n, (k, h2) in enumerate((("lat", 0), ("lat", 1), ("cot", 0), ("cot", 1))):
        loads[k, h2] = load(ins[k].at[:, h2], v[k].at[h2], n)
    for n, k in enumerate(("wq_s", "wo_s", "wo_t", "wq_t")):
        loads[k] = load(ins[k], v[k], 4 + n)
    order = (("lat", 0), ("lat", 1), "wq_s", "wo_s", ("cot", 0), ("cot", 1), "wo_t", "wq_t")
    for k in order:
        loads[k].start()
    expected = greet(p, me)

    def exchange(n, src_of, dst_of):
        return Exchange(me, n, src_of, dst_of, sem["send"], sem["recv"], sem["local"])

    def frame_rows(t):
        return pl.ds(pl.multiple_of(t * 16, 16), 16)

    lat_x = exchange(0, lambda t: lat.at[0, t], lambda s: v["lat_in"].at[s])
    att_x = exchange(1, lambda t: v["att_s"].at[frame_rows(t)], lambda s: v["att_in"].at[s])
    mid_x = exchange(2, lambda t: v["mid_s"].at[frame_rows(t)], lambda s: mid.at[1, s])
    dmid_x = [
        exchange(3 + h2, lambda t, h2=h2: v["dmid_t"].at[h2, t], lambda s, h2=h2: dmid.at[h2, s])
        for h2 in range(2)
    ]
    red_t = Reducer(p, 0, g, (outs["qkv_t"], outs["out_t"]), buf, rsem)
    red_s = Reducer(p, 1, g, (outs["qkv_s"], outs["out_s"]), buf, rsem)

    def reduce_step(red, name, ks=(1, 0, 2)):
        for k in ks:
            getattr(red, name)(k)

    loads["lat", 0].wait()
    loads["lat", 1].wait()
    spatial_norm(lat, mod, v["normed_s"])
    pl.semaphore_wait(pltpu.get_barrier_semaphore(), expected)
    lat_x.start()
    loads["wq_s"].wait()
    project(v["normed_s"], v["wq_s"], v["qkv_s"], (0, 1))
    for pair in range(4):
        spatial_heads(pair, v["qkv_s"], v["probs"], v["sb"], v["turn"])
    v["att_s"][...] = v["turn"][...].T
    att_x.start()
    loads["wo_s"].wait()
    v["mid_s"][...] = block_result(1, flat(lat, 1).astype(F32), mod, 0, v["wo_s"], v["att_s"][256:, :])
    mid_x.start()

    for k in order[4:]:
        loads[k].wait()
    for h2 in range(2):
        temporal_open(h2, cot, mod, v["wo_t"], v["dproj"], v["datt"])
    for h2 in range(2):
        if h2 == 0:
            lat_x.arrive()
            att_x.arrive()
            x = v["lat_in"][...].reshape(256, D).astype(F32)
            att_in = v["att_in"][...].reshape(256, HD)
            mid[0] = block_result(0, x, mod, 0, v["wo_s"], att_in).reshape(FRAMES, 16, D)
        else:
            mid_x.arrive()
        temporal_norm(h2, mod, mid, v["normed_t"])
        project(v["normed_t"], v["wq_t"], v["qkv_t"], (h2,))
        temporal_heads(h2, v["qkv_t"], v["datt"], v["dqkv"], v["sb"], v["pt"], v["ds"], v["turn"])
        v["dmid_t"][h2] = block_gradient(h2, flat(mid, h2), mod, 1, v["wq_t"], flat(cot, h2), v["dqkv"])
        dmid_x[h2].start()
        temporal_attended(h2, v["qkv_t"], v["pt"], v["turn"], v["att_t"])
    for group, ready in ((2, ()), (0, (1,)), (1, (0, 2))):
        weight_grads(group, v["normed_t"], v["dqkv"], v["dproj"], v["att_t"], g)
        reduce_step(red_t, "phase0", ready)
    store_out = []
    for h2 in range(2):
        y = block_result(h2, flat(mid, h2).astype(F32), mod, 1, v["wo_t"], v["att_t"][span_of(h2), :])
        v["block_out"][h2] = y.reshape(FRAMES, 16, D)
        store_out.append(pltpu.make_async_copy(v["block_out"].at[h2], outs["block_out"].at[:, h2], sem["store"].at[h2]))
        store_out[h2].start()

    for h2 in range(2):
        dmid_x[h2].arrive()
        spatial_back_open(h2, mod, v["wo_s"], dmid, v["dproj"], v["datt"])
    for pair in range(4):
        if pair == 2:
            reduce_step(red_t, "phase1")
        spatial_back_heads(pair, v["qkv_s"], v["probs"], v["datt"], v["dqkv"], v["sb"], v["ds"], v["turn"])
    v["dqkv"][:, 0:HD] = v["turn"][...].T
    red_t.sent0()
    for group, ready in ((2, ()), (0, (1,)), (1, (0, 2))):
        weight_grads(group, v["normed_s"], v["dqkv"], v["dproj"], v["att_s"], g)
        reduce_step(red_s, "phase0", ready)
    reduce_step(red_t, "phase2")
    lat_grad = mid
    store_grad = []
    for h2 in range(2):
        lat_grad[h2] = block_gradient(h2, flat(lat, h2), mod, 0, v["wq_s"], flat(dmid, h2), v["dqkv"])
        store_grad.append(pltpu.make_async_copy(lat_grad.at[h2], outs["lat_grad"].at[:, h2], sem["store"].at[2 + h2]))
        store_grad[h2].start()
        if h2 == 0:
            reduce_step(red_t, "phase3")

    reduce_step(red_s, "phase1")
    reduce_step(red_t, "phase4")
    reduce_step(red_s, "phase2")
    reduce_step(red_t, "phase5")
    reduce_step(red_s, "phase3")
    reduce_step(red_s, "phase4")
    for c in store_out + store_grad:
        c.wait()
    for x in [lat_x, att_x, mid_x] + dmid_x:
        x.drain()
    red_s.sent0()
    red_t.drain()
    reduce_step(red_s, "phase5")
    red_s.drain()


def shape(dims, kind=BF):
    return jax.ShapeDtypeStruct(dims, kind)


def params(collective_id=None):
    if collective_id is None:
        return pltpu.CompilerParams(vmem_limit_bytes=VMEM_LIMIT)
    return pltpu.CompilerParams(
        vmem_limit_bytes=VMEM_LIMIT, collective_id=collective_id, has_side_effects=True
    )


VMEM_LIMIT = 62 * 1024 * 1024
INPUTS = ("lat", "mod", "wq_s", "wo_s", "wq_t", "wo_t", "cot")
OUTPUTS = {
    "block_out": shape((FRAMES, 2, 16, D)),
    "lat_grad": shape((FRAMES, 2, 16, D)),
    "qkv_s": shape((9, QKV), F32),
    "out_s": shape((9, HD), F32),
    "qkv_t": shape((9, QKV), F32),
    "out_t": shape((9, HD), F32),
}
HALVES = (2, FRAMES, 16, D)
VALUES = {
    "lat": HALVES, "cot": HALVES,
    "wq_s": (QKV, D), "wo_s": (HD, D), "wq_t": (QKV, D), "wo_t": (HD, D),
    "normed_s": (TOK, D), "qkv_s": (TOK, QKV), "probs": (HEADS, TOK, TOK), "att_s": (TOK, HD),
    "mid_s": (256, D), "lat_in": HALVES[1:], "att_in": (FRAMES, 16, HD),
    "mid": HALVES, "normed_t": (TOK, D), "qkv_t": (TOK, QKV), "att_t": (TOK, HD),
    "dproj": (TOK, D), "datt": (TOK, HD), "dqkv": (TOK, QKV),
    "sb": (2, TOK, TOK), "pt": (2, TOK, TOK), "ds": (2, TOK, TOK), "turn": (HD, TOK),
    "dmid_t": HALVES, "dmid": HALVES, "block_out": HALVES,
    "g": (PIECES, D, WIDE),
}
KINDS = {"sb": F32}


def run(*args):
    dma = pltpu.SemaphoreType.DMA
    bufs, rsems = reduce_buffers(2)
    sems = {
        "load": dma((8,)), "store": dma((4,)),
        "send": dma((5, FRAMES)), "recv": dma((5, FRAMES)), "local": dma((5,)),
    }
    values = {k: pltpu.VMEM(d, KINDS.get(k, BF)) for k, d in VALUES.items()}
    groups = (values, sems, bufs, rsems)

    def unpack(*refs):
        refs = list(refs)

        def take(names):
            got = dict(zip(names, refs))
            del refs[: len(got)]
            return got

        kernel(take(INPUTS), take(OUTPUTS), *[take(g) for g in groups])

    return pl.pallas_call(
        unpack,
        out_shape=tuple(OUTPUTS.values()),
        in_specs=[vmem_spec() if k == "mod" else any_spec() for k in INPUTS],
        out_specs=[any_spec()] * 2 + [vmem_spec()] * 4,
        scratch_shapes=[x for g in groups for x in g.values()],
        compiler_params=params(0),
        name="attention_blocks",
    )(*args)


def hand_over(*refs):
    n = (len(refs) - 2) // 3
    sems = refs[-2:]
    ins = [pltpu.make_async_copy(refs[i], refs[2 * n + i], sems[0].at[i]) for i in range(n)]
    outs = [pltpu.make_async_copy(refs[2 * n + i], refs[n + i], sems[1].at[i]) for i in range(n)]
    for c in ins:
        c.start()
    for i in range(n):
        ins[i].wait()
        outs[i].start()
    for c in outs:
        c.wait()


def body(latents, modulation, spatial_qkv, spatial_out, temporal_qkv, temporal_out, cotangent):
    halves = (FRAMES, 2, 16, D)
    results = run(
        latents.reshape(halves), modulation[0].transpose(1, 0, 2), spatial_qkv.T, spatial_out,
        temporal_qkv.T, temporal_out, cotangent.reshape(halves),
    )
    block_out, lat_grad, qkv_s, out_s, qkv_t, out_t = pl.pallas_call(
        hand_over,
        out_shape=tuple(OUTPUTS.values()),
        in_specs=[any_spec()] * 6,
        out_specs=[any_spec()] * 6,
        scratch_shapes=[pltpu.VMEM(x.shape, x.dtype) for x in OUTPUTS.values()]
        + [pltpu.SemaphoreType.DMA((6,))] * 2,
        compiler_params=params(),
        name="hand_over",
    )(*results)
    return (
        block_out.reshape(1, FRAMES, SPAN, D), lat_grad.reshape(1, 1, TOK, D),
        qkv_s, out_s.T, qkv_t, out_t.T,
    )


def solution(mesh):
    return jax.shard_map(
        body,
        mesh=mesh,
        in_specs=(
            P("dp", "seq", None, None),
            P("dp", None, None, None),
            P(),
            P(),
            P(),
            P(),
            P("dp", None, "seq", None),
        ),
        out_specs=(
            P("dp", None, "seq", None),
            P("dp", "seq", None, None),
            P(("dp", "seq"), None),
            P(None, ("dp", "seq")),
            P(("dp", "seq"), None),
            P(None, ("dp", "seq")),
        ),
        check_vma=False,
    )
```

```python
import functools
import math

import jax
import jax.numpy as jnp
from jax import lax
from jax.experimental import pallas as pl
from jax.experimental.pallas import tpu as pltpu
from jax.sharding import PartitionSpec as P

D = 1152
HEADS = 8
HEAD = 72
HD = 576
QKV = 3 * HD
FRAMES = 16
POS = 512
SPAN = 32
TOK = 512
SCALE = HEAD ** (-0.5)
EXP2 = SCALE / math.log(2.0)
MESH = pl.DeviceIdType.MESH
BF = jnp.bfloat16
F32 = jnp.float32
PIECES = 6
WIDE = 384

NN = (((1,), (0,)), ((), ()))
NT = (((1,), (1,)), ((), ()))
TN = (((0,), (0,)), ((), ()))


def mm(a, b, form=NN):
    return lax.dot_general(a, b, form, preferred_element_type=F32)


def vmem_spec():
    return pl.BlockSpec(memory_space=pltpu.VMEM)


def any_spec():
    return pl.BlockSpec(memory_space=pl.ANY)


def standardise(x):
    centre = jnp.mean(x, -1, keepdims=True)
    centred = x - centre
    spread = jnp.mean(centred * centred, -1, keepdims=True)
    rstd = lax.rsqrt(spread + 1e-06)
    return centred * rstd, rstd


def norm_backward(x, dnormed, scale):
    xhat, rstd = standardise(x)
    dxhat = dnormed * (1.0 + scale)
    first = jnp.mean(dxhat, -1, keepdims=True)
    second = jnp.mean(dxhat * xhat, -1, keepdims=True)
    return rstd * (dxhat - first - xhat * second)


def softmax(scores, mask=None):
    if mask is not None:
        scores = jnp.where(mask, scores, -1e30)
    largest = jnp.max(scores, 0, keepdims=True)
    expo = jnp.exp2((scores - largest) * EXP2)
    return expo * (1.0 / jnp.sum(expo, 0, keepdims=True))


def cols_of(part, h):
    return slice(part * HD + h * HEAD, part * HD + (h + 1) * HEAD)


def rows_of(h):
    return slice(h * HEAD, (h + 1) * HEAD)


def score_backward(p, dp):
    wide = p.astype(F32)
    return (wide * (dp - jnp.sum(dp * wide, 0, keepdims=True))).astype(BF)


SLOTS = (3, 1, 2, 0, 4, 5)


def weight_grads(first, normed, dqkv, dproj, att, g):
    for lo in range(0, D, 384):
        rows = slice(lo, lo + 384)
        left = normed[:, rows]
        if first:
            vals = mm(left, dqkv[:, 2 * HD :], TN)
            outs = mm(dproj[:, rows], att[...], TN)
            g[SLOTS[3], rows, :] = vals[:, :WIDE].astype(BF)
            g[SLOTS[4], rows, :192] = vals[:, WIDE:].astype(BF)
            g[SLOTS[4], rows, 192:] = outs[:, :192].astype(BF)
            g[SLOTS[5], rows, :] = outs[:, 192:].astype(BF)
        else:
            both = mm(left, dqkv[:, : 2 * HD], TN)
            for n in range(3):
                g[SLOTS[n], rows, :] = both[:, n * WIDE : (n + 1) * WIDE].astype(BF)


def span_of(h2):
    return slice(h2 * 256, (h2 + 1) * 256)


def flat(ref, h2):
    return ref[h2].reshape(256, ref.shape[-1])


def spatial_norm(lat, mod, normed):
    shift, scale = mod[0, 0:1, :], mod[1, 0:1, :]
    for h2 in range(2):
        for lo in (0, 8):
            xhat, _ = standardise(lat[h2, lo : lo + 8].reshape(128, D).astype(F32))
            rows = slice(h2 * 256 + lo * 16, h2 * 256 + lo * 16 + 128)
            normed[rows, :] = (xhat * (1.0 + scale) + shift).astype(BF)


def project(normed, wq, qkv, spans):
    for h2 in spans:
        qkv[span_of(h2), :] = mm(normed[span_of(h2), :], wq[...], NT).astype(BF)


def spatial_heads(pair, qkv, probs, sb, turn):
    heads = [(pair * 2 + i, i) for i in range(2)]
    for h, i in heads:
        sb[i] = mm(qkv[:, cols_of(1, h)], qkv[:, cols_of(0, h)], NT)
    for h, i in heads:
        probs[h] = softmax(sb[i]).astype(BF)
    for h, i in heads:
        turn[rows_of(h), :] = mm(qkv[:, cols_of(2, h)], probs[h], TN).astype(BF)


def block_result(h2, x, mod, block, wo, att):
    gate = mod[2, block : block + 1, :]
    return (x + gate * mm(att, wo[...])).astype(BF)


def spatial_back_open(h2, mod, wo, dmid, dproj, datt):
    rows = span_of(h2)
    dpr = (flat(dmid, h2).astype(F32) * mod[2, 0:1, :]).astype(BF)
    dproj[rows, :] = dpr
    datt[rows, :] = mm(dpr, wo[...], NT).astype(BF)


def spatial_back_values(qkv, probs, datt, dqkv):
    for h in range(HEADS):
        dqkv[:, cols_of(2, h)] = mm(probs[h], datt[:, cols_of(0, h)]).astype(BF)


def spatial_back_heads(pair, qkv, probs, datt, dqkv, sb, ds, turn):
    heads = [(pair * 2 + i, i) for i in range(2)]
    for h, i in heads:
        sb[i] = mm(qkv[:, cols_of(2, h)], datt[:, cols_of(0, h)], NT)
    for h, i in heads:
        ds[i] = score_backward(probs[h], sb[i])
    for h, i in heads:
        dqkv[:, cols_of(1, h)] = (mm(ds[i], qkv[:, cols_of(0, h)]) * SCALE).astype(BF)
    for h, i in heads:
        turn[rows_of(h), :] = (mm(qkv[:, cols_of(1, h)], ds[i], TN) * SCALE).astype(BF)


def block_gradient(h2, x, mod, block, wq, dy, dqkv):
    dnormed = mm(dqkv[span_of(h2), :], wq[...])
    dx = norm_backward(x.astype(F32), dnormed, mod[1, block : block + 1, :])
    return (dx + dy.astype(F32)).astype(BF).reshape(FRAMES, 16, D)


def temporal_open(h2, cot, mod, wo, dproj, datt):
    rows = span_of(h2)
    dpr = (flat(cot, h2).astype(F32) * mod[2, 1:2, :]).astype(BF)
    dproj[rows, :] = dpr
    datt[rows, :] = mm(dpr, wo[...], NT).astype(BF)


def temporal_norm(h2, mod, mid, normed):
    xhat, _ = standardise(flat(mid, h2).astype(F32))
    normed[span_of(h2), :] = (xhat * (1.0 + mod[1, 1:2, :]) + mod[0, 1:2, :]).astype(BF)


def pair_of(part, pair):
    return slice(part * HD + pair * 2 * HEAD, part * HD + (pair + 1) * 2 * HEAD)


def split_pair(x):
    first = lax.broadcasted_iota(jnp.int32, x.shape, 1) < HEAD
    zero = jnp.zeros_like(x)
    return jnp.concatenate([jnp.where(first, x, zero), jnp.where(first, zero, x)], 0)


def pair_tile(pair):
    return pair // 2, slice(pair % 2 * 256, pair % 2 * 256 + 256), slice(0, 512)


def temporal_heads(h2, qkv, datt, dqkv, sb, pt, ds, turn):
    rows = span_of(h2)
    row_id = lax.broadcasted_iota(jnp.int32, (256, 512), 0)
    col_id = lax.broadcasted_iota(jnp.int32, (256, 512), 1)
    mask = (row_id & 15) == (col_id & 15)
    pairs = [(n, pair_tile(n)) for n in range(HEADS // 2)]
    for n, at in pairs:
        sb[at] = mm(qkv[rows, pair_of(1, n)], split_pair(qkv[rows, pair_of(0, n)]), NT)
    for n, at in pairs:
        pt[at] = softmax(sb[at], mask).astype(BF)
    for n, at in pairs:
        sb[at] = mm(qkv[rows, pair_of(2, n)], split_pair(datt[rows, pair_of(0, n)]), NT)
    for n, at in pairs:
        ds[at] = score_backward(pt[at], sb[at])
    for n, at in pairs:
        dqkv[rows, pair_of(2, n)] = mm(pt[at], split_pair(datt[rows, pair_of(0, n)])).astype(BF)
    for n, at in pairs:
        dqkv[rows, pair_of(1, n)] = (mm(ds[at], split_pair(qkv[rows, pair_of(0, n)])) * SCALE).astype(BF)
    for n, at in pairs:
        both = mm(qkv[rows, pair_of(1, n)], ds[at], TN) * SCALE
        turn[rows_of(2 * n), rows] = both[:HEAD, :256].astype(BF)
        turn[rows_of(2 * n + 1), rows] = both[HEAD:, 256:].astype(BF)
    dqkv[rows, 0:HD] = turn[:, rows].T


def temporal_attended(h2, qkv, pt, turn, att):
    rows = span_of(h2)
    for n in range(HEADS // 2):
        both = mm(qkv[rows, pair_of(2, n)], pt[pair_tile(n)], TN)
        turn[rows_of(2 * n), rows] = both[:HEAD, :256].astype(BF)
        turn[rows_of(2 * n + 1), rows] = both[HEAD:, 256:].astype(BF)
    att[rows, :] = turn[:, rows].T


class Exchange:
    def __init__(self, me, n, src_of, dst_of, send, recv, local):
        self.me, self.n, self.src_of, self.dst_of = me, n, src_of, dst_of
        self.send, self.recv, self.local = send, recv, local

    def copy(self, t, slot):
        return pltpu.make_async_remote_copy(
            src_ref=self.src_of(t),
            dst_ref=self.dst_of(slot),
            send_sem=self.send.at[self.n, t],
            recv_sem=self.recv.at[self.n, slot],
            device_id={"seq": t},
            device_id_type=MESH,
        )

    def own(self):
        return pltpu.make_async_copy(self.src_of(self.me), self.dst_of(self.me), self.local.at[self.n])

    def others(self, step):
        @pl.loop(1, FRAMES)
        def _(i):
            step(lax.rem(self.me + i, FRAMES))

    def start(self):
        y, x, c = lax.div(self.me, 8), lax.rem(lax.div(self.me, 2), 4), lax.rem(self.me, 2)
        for dc in range(2):
            for dy, dx in ((0, 1), (0, 3), (1, 0), (1, 1), (1, 3), (0, 2), (1, 2), (0, 0))[: 7 + dc]:
                t = lax.rem(y + dy, 2) * 8 + lax.rem(x + dx, 4) * 2 + lax.rem(c + dc, 2)
                self.copy(t, self.me).start()
        self.own().start()

    def arrive(self):
        self.others(lambda t: self.copy(t, t).wait_recv())
        self.own().wait()

    def drain(self):
        self.others(lambda t: self.copy(t, t).wait_send())


def spot(z, y, x, c):
    return {
        "dp": z * 2 + lax.div(y, 2),
        "seq": lax.rem(y, 2) * 8 + x * 2 + c,
    }


class Place:
    def __init__(self):
        dp, seq = lax.axis_index("dp"), lax.axis_index("seq")
        self.z = lax.div(dp, 2)
        self.y = lax.rem(dp, 2) * 2 + lax.div(seq, 8)
        self.x = lax.rem(lax.div(seq, 2), 4)
        self.c = lax.rem(seq, 2)
        self.at = (self.z, self.y, self.x)

    def moved(self, axis, j):
        return spot(*[j if i == axis else v for i, v in enumerate(self.at)], self.c)

    def partner(self):
        return spot(*self.at, 1 - self.c)


ORDERS = ((0, 1, 2), (1, 2, 0), (2, 0, 1))
CHUNK = 288
HALF = 144
BLOCK = 72
SLOT = 80


def odd_even(j):
    return j + 1 - 2 * lax.rem(j, 2)


def send_to(src, dst, send_sem, recv_sem, device):
    return pltpu.make_async_remote_copy(
        src_ref=src, dst_ref=dst, send_sem=send_sem, recv_sem=recv_sem, device_id=device, device_id_type=MESH
    )


class Reducer:
    def __init__(self, place, m, g, out, buf, sem):
        self.p, self.m, self.g, self.out, self.b, self.s = place, m, g, out, buf, sem

    def go0(self, k):
        return send_to(
            self.g.at[(1 - self.p.c) * 3 + k], self.b["r0"].at[self.m, k],
            self.s["s0"].at[self.m, k], self.s["v0"].at[self.m, k], self.p.partner(),
        )

    def chunk(self, j, half):
        return pl.ds(pl.multiple_of(j * CHUNK + half * HALF, 16), HALF)

    def ring(self, k, half):
        axis = ORDERS[k][0]
        j = self.p.at[axis]
        pair = (odd_even(j), 3 - j)
        return axis, j, pair[half], pair[1 - half]

    def go1(self, k, half, slot):
        axis, j, first, second = self.ring(k, half)
        other = 3 - first if half == 0 else odd_even(first)
        rows = self.chunk(first if slot == 0 else other, half)
        return send_to(
            self.b["r0"].at[self.m, k, rows], self.b["ra"].at[self.m, k, half, slot],
            self.s["sa"].at[self.m, k, half, slot], self.s["va"].at[self.m, k, half, slot],
            self.p.moved(axis, first),
        )

    def go2(self, k, half):
        axis, j, first, second = self.ring(k, half)
        return send_to(
            self.b["tb"].at[self.m, k, half], self.b["rb"].at[self.m, k, half],
            self.s["sb"].at[self.m, k, half], self.s["vb"].at[self.m, k, half],
            self.p.moved(axis, second),
        )

    def go3(self, k, to, slot):
        axis = ORDERS[k][1]
        return send_to(
            self.b["t2"].at[self.m, k, to], self.b["r2"].at[self.m, k, slot],
            self.s["s2"].at[self.m, k, to], self.s["v2"].at[self.m, k, slot],
            self.p.moved(axis, to),
        )

    def go4(self, k, x, c, s, e):
        a, b, _ = ORDERS[k]
        return send_to(
            self.b["t3"].at[self.m, k, x, c], self.b["r3"].at[self.m, k, s, e],
            self.s["s3"].at[self.m, k, x, c], self.s["v3"].at[self.m, k, s, e],
            spot(self.p.at[a], self.p.at[b], x, c),
        )

    def own4(self, k, x, c):
        s = self.p.at[ORDERS[k][2]]
        return pltpu.make_async_copy(
            self.b["t3"].at[self.m, k, x, c], self.b["r3"].at[self.m, k, s, self.p.c],
            self.s["v3"].at[self.m, k, s, self.p.c],
        )

    def to_self(self, k, x, c):
        p = self.p
        a, b, _ = ORDERS[k]
        return (p.at[a] == p.z) & (p.at[b] == p.y) & (x == p.x) & (c == p.c)


    def phase0(self, k):
        self.go0(k).start()

    def sent0(self):
        for k in range(3):
            self.go0(k).wait_send()

    def phase1(self, k):
        self.go0(k).wait_recv()
        r0 = self.b["r0"]
        n = self.p.c * 3 + k

        @pl.loop(0, D // HALF)
        def _(i):
            rows = pl.ds(pl.multiple_of(i * HALF, 16), HALF)
            r0[self.m, k, rows] = (
                r0[self.m, k, rows].astype(F32) + self.g[n, rows].astype(F32)
            ).astype(BF)

        for slot in (1, 0):
            for half in range(2):
                self.go1(k, half, slot).start()

    def phase2(self, k):
        for half in range(2):
            axis, j, first, second = self.ring(k, half)
            self.go1(k, half, 1).wait_recv()
            rows = self.chunk(second, half)
            self.b["tb"][self.m, k, half] = (
                self.b["r0"][self.m, k, rows].astype(F32) + self.b["ra"][self.m, k, half, 1].astype(F32)
            ).astype(BF)
            self.go2(k, half).start()

    def phase3(self, k):
        axis = ORDERS[k][1]
        me = self.p.at[axis]
        for half in range(2):
            _, j, _, _ = self.ring(k, half)
            self.go1(k, half, 0).wait_recv()
            self.go2(k, half).wait_recv()
            rows = self.chunk(j, half)
            total = (
                self.b["r0"][self.m, k, rows].astype(F32)
                + self.b["ra"][self.m, k, half, 0].astype(F32)
                + self.b["rb"][self.m, k, half].astype(F32)
            )
            for i in range(2):
                self.b["t2"][self.m, k, 2 * half + i, :BLOCK] = total[i * BLOCK : (i + 1) * BLOCK].astype(BF)
                self.b["t2"][self.m, k, 2 * half + i, BLOCK:] = jnp.zeros((SLOT - BLOCK, WIDE), BF)

        @pl.loop(1, 4)
        def _(i):
            self.go3(k, lax.rem(me + i, 4), me).start()

    def phase4(self, k):
        axis = ORDERS[k][1]
        me = self.p.at[axis]
        total = self.b["t2"][self.m, k, me].astype(F32)
        for i in range(1, 4):
            t = lax.rem(me + i, 4)
            self.go3(k, t, t).wait_recv()
            total = total + self.b["r2"][self.m, k, t].astype(F32)
        row = lax.broadcasted_iota(jnp.int32, (128, SLOT), 0)
        col = lax.broadcasted_iota(jnp.int32, (128, SLOT), 1)
        pick = ((row & 15) < 9) & (col == lax.shift_right_logical(row, 4) * 9 + (row & 15))
        spread = mm(jnp.where(pick, 1.0, 0.0).astype(BF), total.astype(BF)).astype(BF)
        for x in range(4):
            for c in range(2):
                lo = (x * 2 + c) * 16
                self.b["t3"][self.m, k, x, c] = spread[lo : lo + 16]
        s = self.p.at[ORDERS[k][2]]

        @pl.loop(0, 8)
        def _(i):
            x, c = lax.div(i, 2), lax.rem(i, 2)
            mine = self.to_self(k, x, c)

            @pl.when(mine)
            def _():
                self.own4(k, x, c).start()

            @pl.when(jnp.logical_not(mine))
            def _():
                self.go4(k, x, c, s, self.p.c).start()

    def phase5(self, k):
        p = self.p
        own = self.to_self(k, p.x, p.c)
        own_s = p.at[ORDERS[k][2]]

        @pl.loop(0, 8)
        def _(i):
            s, e = lax.div(i, 2), lax.rem(i, 2)
            mine = own & (s == own_s) & (e == p.c)

            @pl.when(mine)
            def _():
                self.own4(k, p.x, p.c).wait()

            @pl.when(jnp.logical_not(mine))
            def _():
                self.go4(k, s, e, s, e).wait_recv()

        for e in range(2):
            total = self.b["r3"][self.m, k, 0, e].astype(F32)
            for s in range(1, 4):
                total = total + self.b["r3"][self.m, k, s, e].astype(F32)
            n = SLOTS.index(e * 3 + k)
            if n < 4:
                self.out[0][:, n * WIDE : (n + 1) * WIDE] = total[:9]
            elif n == 4:
                self.out[0][:, n * WIDE :] = total[:9, :192]
                self.out[1][:, :192] = total[:9, 192:]
            else:
                self.out[1][:, 192:] = total[:9]

    def drain(self):
        for k in range(3):
            me = self.p.at[ORDERS[k][1]]
            for half in range(2):
                self.go1(k, half, 0).wait_send()
                self.go1(k, half, 1).wait_send()
                self.go2(k, half).wait_send()

            @pl.loop(1, 4)
            def _(i):
                t = lax.rem(me + i, 4)
                self.go3(k, t, t).wait_send()

            @pl.loop(0, 8)
            def _(i):
                x, c = lax.div(i, 2), lax.rem(i, 2)

                @pl.when(jnp.logical_not(self.to_self(k, x, c)))
                def _():
                    self.go4(k, x, c, 0, 0).wait_send()


def greet(p, me):
    barrier = pltpu.get_barrier_semaphore()

    def hail(device):
        pl.semaphore_signal(barrier, inc=1, device_id=device, device_id_type=MESH)

    @pl.loop(1, FRAMES)
    def _(i):
        hail({"seq": lax.rem(me + i, FRAMES)})

    hail(p.partner())
    for axis in range(3):
        for i in range(1, 4):
            hail(p.moved(axis, lax.rem(p.at[axis] + i, 4)))
    selves = 0
    for k in range(3):
        a, b, c = ORDERS[k]

        @pl.loop(0, 8)
        def _(i):
            s, e = lax.div(i, 2), lax.rem(i, 2)
            where = [None] * 3
            where[a], where[b], where[c] = p.z, p.y, s
            same = (where[0] == p.z) & (where[1] == p.y) & (where[2] == p.x) & (e == p.c)

            @pl.when(jnp.logical_not(same))
            def _():
                hail(spot(*where, e))

        own = (p.at[a] == p.z) & (p.at[b] == p.y)
        selves = selves + jnp.where(own & (p.at[c] == p.x), 1, 0)
    return FRAMES - 1 + 10 + 24 - selves


def reduce_buffers(count):
    dma = pltpu.SemaphoreType.DMA
    bufs = dict(
        r0=pltpu.VMEM((count, 3, D, WIDE), BF),
        ra=pltpu.VMEM((count, 3, 2, 2, HALF, WIDE), BF),
        tb=pltpu.VMEM((count, 3, 2, HALF, WIDE), BF),
        rb=pltpu.VMEM((count, 3, 2, HALF, WIDE), BF),
        t2=pltpu.VMEM((count, 3, 4, SLOT, WIDE), BF),
        r2=pltpu.VMEM((count, 3, 4, SLOT, WIDE), BF),
        t3=pltpu.VMEM((count, 3, 4, 2, 16, WIDE), BF),
        r3=pltpu.VMEM((count, 3, 4, 2, 16, WIDE), BF),
    )
    sems = {}
    for end in "sv":
        sems[end + "0"] = dma((count, 3))
        sems[end + "a"] = dma((count, 3, 2, 2))
        sems[end + "b"] = dma((count, 3, 2))
        sems[end + "2"] = dma((count, 3, 4))
        sems[end + "3"] = dma((count, 3, 4, 2))
    return bufs, sems


def kernel(ins, outs, v, sem, buf, rsem):
    me = lax.axis_index("seq")
    p = Place()
    mod = ins["mod"]
    lat, cot, mid, dmid, g = v["lat"], v["cot"], v["mid"], v["dmid"], v["g"]

    def load(src, dst, n):
        return pltpu.make_async_copy(src, dst, sem["load"].at[n])

    loads = {}
    for n, (k, h2) in enumerate((("lat", 0), ("lat", 1), ("cot", 0), ("cot", 1))):
        loads[k, h2] = load(ins[k].at[:, h2], v[k].at[h2], n)
    for n, k in enumerate(("wq_s", "wo_s", "wo_t", "wq_t")):
        loads[k] = load(ins[k], v[k], 4 + n)
    order = (("lat", 0), ("lat", 1), "wq_s", "wo_s", ("cot", 0), ("cot", 1), "wo_t", "wq_t")
    for k in order:
        loads[k].start()
    expected = greet(p, me)

    def exchange(n, src_of, dst_of):
        return Exchange(me, n, src_of, dst_of, sem["send"], sem["recv"], sem["local"])

    def frame_rows(t):
        return pl.ds(pl.multiple_of(t * 16, 16), 16)

    lat_x = exchange(0, lambda t: lat.at[0, t], lambda s: v["lat_in"].at[s])
    att_x = exchange(1, lambda t: v["att_s"].at[frame_rows(t)], lambda s: v["att_in"].at[s])
    mid_x = exchange(2, lambda t: v["mid_s"].at[frame_rows(t)], lambda s: mid.at[1, s])
    dmid_x = [
        exchange(3 + h2, lambda t, h2=h2: v["dmid_t"].at[h2, t], lambda s, h2=h2: dmid.at[h2, s])
        for h2 in range(2)
    ]
    red_t = Reducer(p, 0, g, (outs["qkv_t"], outs["out_t"]), buf, rsem)
    red_s = Reducer(p, 1, g, (outs["qkv_s"], outs["out_s"]), buf, rsem)

    def reduce_step(red, name, ks=(1, 0, 2)):
        for k in ks:
            getattr(red, name)(k)

    def wave(red, name, late):
        c = 1 - p.c if name == "phase0" else p.c
        for core in range(2):
            ks = [(0,), (1, 2)][core ^ late]

            @pl.when(c == core)
            def _(ks=ks):
                reduce_step(red, name, ks)

    loads["lat", 0].wait()
    loads["lat", 1].wait()
    spatial_norm(lat, mod, v["normed_s"])
    pl.semaphore_wait(pltpu.get_barrier_semaphore(), expected)
    lat_x.start()
    loads["wq_s"].wait()
    project(v["normed_s"], v["wq_s"], v["qkv_s"], (0, 1))
    for pair in range(4):
        spatial_heads(pair, v["qkv_s"], v["probs"], v["sb"], v["turn"])
    v["att_s"][...] = v["turn"][...].T
    att_x.start()
    loads["wo_s"].wait()
    v["mid_s"][...] = block_result(1, flat(lat, 1).astype(F32), mod, 0, v["wo_s"], v["att_s"][256:, :])
    mid_x.start()

    for k in order[4:]:
        loads[k].wait()
    for h2 in range(2):
        temporal_open(h2, cot, mod, v["wo_t"], v["dproj"], v["datt"])
    for h2 in range(2):
        if h2 == 0:
            lat_x.arrive()
            att_x.arrive()
            x = v["lat_in"][...].reshape(256, D).astype(F32)
            att_in = v["att_in"][...].reshape(256, HD)
            mid[0] = block_result(0, x, mod, 0, v["wo_s"], att_in).reshape(FRAMES, 16, D)
        else:
            mid_x.arrive()
        temporal_norm(h2, mod, mid, v["normed_t"])
        project(v["normed_t"], v["wq_t"], v["qkv_t"], (h2,))
        temporal_heads(h2, v["qkv_t"], v["datt"], v["dqkv"], v["sb"], v["pt"], v["ds"], v["turn"])
        v["dmid_t"][h2] = block_gradient(h2, flat(mid, h2), mod, 1, v["wq_t"], flat(cot, h2), v["dqkv"])
        dmid_x[h2].start()
        temporal_attended(h2, v["qkv_t"], v["pt"], v["turn"], v["att_t"])
    for first in (True, False):
        weight_grads(first, v["normed_t"], v["dqkv"], v["dproj"], v["att_t"], g)
        wave(red_t, "phase0", not first)
    store_out = []
    for h2 in range(2):
        y = block_result(h2, flat(mid, h2).astype(F32), mod, 1, v["wo_t"], v["att_t"][span_of(h2), :])
        v["block_out"][h2] = y.reshape(FRAMES, 16, D)
        store_out.append(pltpu.make_async_copy(v["block_out"].at[h2], outs["block_out"].at[:, h2], sem["store"].at[h2]))
        store_out[h2].start()

    for h2 in range(2):
        dmid_x[h2].arrive()
        spatial_back_open(h2, mod, v["wo_s"], dmid, v["dproj"], v["datt"])
    spatial_back_values(v["qkv_s"], v["probs"], v["datt"], v["dqkv"])
    reduce_step(red_t, "phase1")
    red_t.sent0()
    weight_grads(True, v["normed_s"], v["dqkv"], v["dproj"], v["att_s"], g)
    wave(red_s, "phase0", 0)
    for pair in range(4):
        if pair == 3:
            reduce_step(red_t, "phase2")
        spatial_back_heads(pair, v["qkv_s"], v["probs"], v["datt"], v["dqkv"], v["sb"], v["ds"], v["turn"])
    v["dqkv"][:, 0:HD] = v["turn"][...].T
    weight_grads(False, v["normed_s"], v["dqkv"], v["dproj"], v["att_s"], g)
    wave(red_s, "phase0", 1)
    wave(red_s, "phase1", 0)
    reduce_step(red_t, "phase3")
    lat_grad = mid
    store_grad = []
    for h2 in range(2):
        lat_grad[h2] = block_gradient(h2, flat(lat, h2), mod, 0, v["wq_s"], flat(dmid, h2), v["dqkv"])
        store_grad.append(pltpu.make_async_copy(lat_grad.at[h2], outs["lat_grad"].at[:, h2], sem["store"].at[2 + h2]))
        store_grad[h2].start()

    wave(red_s, "phase1", 1)
    reduce_step(red_t, "phase4")
    wave(red_s, "phase2", 0)
    wave(red_s, "phase2", 1)
    wave(red_s, "phase3", 0)
    reduce_step(red_t, "phase5")
    wave(red_s, "phase3", 1)
    wave(red_s, "phase4", 0)
    wave(red_s, "phase4", 1)
    for c in store_out + store_grad:
        c.wait()
    for x in [lat_x, att_x, mid_x] + dmid_x:
        x.drain()
    red_s.sent0()
    red_t.drain()
    reduce_step(red_s, "phase5")
    red_s.drain()


def shape(dims, kind=BF):
    return jax.ShapeDtypeStruct(dims, kind)


def params(collective_id=None):
    if collective_id is None:
        return pltpu.CompilerParams(vmem_limit_bytes=VMEM_LIMIT)
    return pltpu.CompilerParams(
        vmem_limit_bytes=VMEM_LIMIT, collective_id=collective_id, has_side_effects=True
    )


VMEM_LIMIT = 62 * 1024 * 1024
INPUTS = ("lat", "mod", "wq_s", "wo_s", "wq_t", "wo_t", "cot")
OUTPUTS = {
    "block_out": shape((FRAMES, 2, 16, D)),
    "lat_grad": shape((FRAMES, 2, 16, D)),
    "qkv_s": shape((9, QKV), F32),
    "out_s": shape((9, HD), F32),
    "qkv_t": shape((9, QKV), F32),
    "out_t": shape((9, HD), F32),
}
HALVES = (2, FRAMES, 16, D)
VALUES = {
    "lat": HALVES, "cot": HALVES,
    "wq_s": (QKV, D), "wo_s": (HD, D), "wq_t": (QKV, D), "wo_t": (HD, D),
    "normed_s": (TOK, D), "qkv_s": (TOK, QKV), "probs": (HEADS, TOK, TOK), "att_s": (TOK, HD),
    "mid_s": (256, D), "lat_in": HALVES[1:], "att_in": (FRAMES, 16, HD),
    "mid": HALVES, "normed_t": (TOK, D), "qkv_t": (TOK, QKV), "att_t": (TOK, HD),
    "dproj": (TOK, D), "datt": (TOK, HD), "dqkv": (TOK, QKV),
    "sb": (2, TOK, TOK), "pt": (2, TOK, TOK), "ds": (2, TOK, TOK), "turn": (HD, TOK),
    "dmid_t": HALVES, "dmid": HALVES, "block_out": HALVES,
    "g": (PIECES, D, WIDE),
}
KINDS = {"sb": F32}


def run(*args):
    dma = pltpu.SemaphoreType.DMA
    bufs, rsems = reduce_buffers(2)
    sems = {
        "load": dma((8,)), "store": dma((4,)),
        "send": dma((5, FRAMES)), "recv": dma((5, FRAMES)), "local": dma((5,)),
    }
    values = {k: pltpu.VMEM(d, KINDS.get(k, BF)) for k, d in VALUES.items()}
    groups = (values, sems, bufs, rsems)

    def unpack(*refs):
        refs = list(refs)

        def take(names):
            got = dict(zip(names, refs))
            del refs[: len(got)]
            return got

        kernel(take(INPUTS), take(OUTPUTS), *[take(g) for g in groups])

    return pl.pallas_call(
        unpack,
        out_shape=tuple(OUTPUTS.values()),
        in_specs=[vmem_spec() if k == "mod" else any_spec() for k in INPUTS],
        out_specs=[any_spec()] * 2 + [vmem_spec()] * 4,
        scratch_shapes=[x for g in groups for x in g.values()],
        compiler_params=params(0),
        name="attention_blocks",
    )(*args)


def hand_over(*refs):
    n = (len(refs) - 2) // 3
    sems = refs[-2:]
    ins = [pltpu.make_async_copy(refs[i], refs[2 * n + i], sems[0].at[i]) for i in range(n)]
    outs = [pltpu.make_async_copy(refs[2 * n + i], refs[n + i], sems[1].at[i]) for i in range(n)]
    for c in ins:
        c.start()
    for i in range(n):
        ins[i].wait()
        outs[i].start()
    for c in outs:
        c.wait()


def body(latents, modulation, spatial_qkv, spatial_out, temporal_qkv, temporal_out, cotangent):
    halves = (FRAMES, 2, 16, D)
    results = run(
        latents.reshape(halves), modulation[0].transpose(1, 0, 2), spatial_qkv.T, spatial_out,
        temporal_qkv.T, temporal_out, cotangent.reshape(halves),
    )
    block_out, lat_grad, qkv_s, out_s, qkv_t, out_t = pl.pallas_call(
        hand_over,
        out_shape=tuple(OUTPUTS.values()),
        in_specs=[any_spec()] * 6,
        out_specs=[any_spec()] * 6,
        scratch_shapes=[pltpu.VMEM(x.shape, x.dtype) for x in OUTPUTS.values()]
        + [pltpu.SemaphoreType.DMA((6,))] * 2,
        compiler_params=params(),
        name="hand_over",
    )(*results)
    return (
        block_out.reshape(1, FRAMES, SPAN, D), lat_grad.reshape(1, 1, TOK, D),
        qkv_s, out_s.T, qkv_t, out_t.T,
    )


def solution(mesh):
    return jax.shard_map(
        body,
        mesh=mesh,
        in_specs=(
            P("dp", "seq", None, None),
            P("dp", None, None, None),
            P(),
            P(),
            P(),
            P(),
            P("dp", None, "seq", None),
        ),
        out_specs=(
            P("dp", None, "seq", None),
            P("dp", "seq", None, None),
            P(("dp", "seq"), None),
            P(None, ("dp", "seq")),
            P(("dp", "seq"), None),
            P(None, ("dp", "seq")),
        ),
        check_vma=False,
    )
```

```python
import functools
import math

import jax
import jax.numpy as jnp
from jax import lax
from jax.experimental import pallas as pl
from jax.experimental.pallas import tpu as pltpu
from jax.sharding import PartitionSpec as P

D = 1152
HEADS = 8
HEAD = 72
HD = 576
QKV = 3 * HD
FRAMES = 16
POS = 512
SPAN = 32
TOK = 512
SCALE = HEAD ** (-0.5)
EXP2 = SCALE / math.log(2.0)
MESH = pl.DeviceIdType.MESH
BF = jnp.bfloat16
F32 = jnp.float32
PIECES = 6
WIDE = 384

NN = (((1,), (0,)), ((), ()))
NT = (((1,), (1,)), ((), ()))
TN = (((0,), (0,)), ((), ()))


def mm(a, b, form=NN):
    return lax.dot_general(a, b, form, preferred_element_type=F32)


def vmem_spec():
    return pl.BlockSpec(memory_space=pltpu.VMEM)


def any_spec():
    return pl.BlockSpec(memory_space=pl.ANY)


def standardise(x):
    centre = jnp.mean(x, -1, keepdims=True)
    centred = x - centre
    spread = jnp.mean(centred * centred, -1, keepdims=True)
    rstd = lax.rsqrt(spread + 1e-06)
    return centred * rstd, rstd


def norm_backward(x, dnormed, scale):
    xhat, rstd = standardise(x)
    dxhat = dnormed * (1.0 + scale)
    first = jnp.mean(dxhat, -1, keepdims=True)
    second = jnp.mean(dxhat * xhat, -1, keepdims=True)
    return rstd * (dxhat - first - xhat * second)


def softmax(scores, mask=None):
    if mask is not None:
        scores = jnp.where(mask, scores, -1e30)
    largest = jnp.max(scores, 0, keepdims=True)
    expo = jnp.exp2((scores - largest) * EXP2)
    return expo * (1.0 / jnp.sum(expo, 0, keepdims=True))


def cols_of(part, h):
    return slice(part * HD + h * HEAD, part * HD + (h + 1) * HEAD)


def rows_of(h):
    return slice(h * HEAD, (h + 1) * HEAD)


def score_backward(p, dp):
    wide = p.astype(F32)
    return (wide * (dp - jnp.sum(dp * wide, 0, keepdims=True))).astype(BF)


SLOTS = (3, 1, 2, 0, 4, 5)


def weight_grads(first, normed, dqkv, dproj, att, g):
    for lo in range(0, D, 384):
        rows = slice(lo, lo + 384)
        left = normed[:, rows]
        if first:
            vals = mm(left, dqkv[:, 2 * HD :], TN)
            outs = mm(dproj[:, rows], att[...], TN)
            g[SLOTS[3], rows, :] = vals[:, :WIDE].astype(BF)
            g[SLOTS[4], rows, :192] = vals[:, WIDE:].astype(BF)
            g[SLOTS[4], rows, 192:] = outs[:, :192].astype(BF)
            g[SLOTS[5], rows, :] = outs[:, 192:].astype(BF)
        else:
            both = mm(left, dqkv[:, : 2 * HD], TN)
            for n in range(3):
                g[SLOTS[n], rows, :] = both[:, n * WIDE : (n + 1) * WIDE].astype(BF)


def span_of(h2):
    return slice(h2 * 256, (h2 + 1) * 256)


def flat(ref, h2):
    return ref[h2].reshape(256, ref.shape[-1])


def spatial_norm(lat, mod, normed):
    shift, scale = mod[0, 0:1, :], mod[1, 0:1, :]
    for h2 in range(2):
        for lo in (0, 8):
            xhat, _ = standardise(lat[h2, lo : lo + 8].reshape(128, D).astype(F32))
            rows = slice(h2 * 256 + lo * 16, h2 * 256 + lo * 16 + 128)
            normed[rows, :] = (xhat * (1.0 + scale) + shift).astype(BF)


def project(normed, wq, qkv, spans):
    for h2 in spans:
        qkv[span_of(h2), :] = mm(normed[span_of(h2), :], wq[...], NT).astype(BF)


def spatial_heads(pair, qkv, probs, sb, turn):
    heads = [(pair * 2 + i, i) for i in range(2)]
    for h, i in heads:
        sb[i] = mm(qkv[:, cols_of(1, h)], qkv[:, cols_of(0, h)], NT)
    for h, i in heads:
        probs[h] = softmax(sb[i]).astype(BF)
    for h, i in heads:
        turn[rows_of(h), :] = mm(qkv[:, cols_of(2, h)], probs[h], TN).astype(BF)


def block_result(h2, x, mod, block, wo, att):
    gate = mod[2, block : block + 1, :]
    return (x + gate * mm(att, wo[...])).astype(BF)


def spatial_back_open(h2, mod, wo, dmid, dproj, datt):
    rows = span_of(h2)
    dpr = (flat(dmid, h2).astype(F32) * mod[2, 0:1, :]).astype(BF)
    dproj[rows, :] = dpr
    datt[rows, :] = mm(dpr, wo[...], NT).astype(BF)


def spatial_back_values(qkv, probs, datt, dqkv):
    for h in range(HEADS):
        dqkv[:, cols_of(2, h)] = mm(probs[h], datt[:, cols_of(0, h)]).astype(BF)


def spatial_back_heads(pair, qkv, probs, datt, dqkv, sb, ds, turn):
    heads = [(pair * 2 + i, i) for i in range(2)]
    for h, i in heads:
        sb[i] = mm(qkv[:, cols_of(2, h)], datt[:, cols_of(0, h)], NT)
    for h, i in heads:
        ds[i] = score_backward(probs[h], sb[i])
    for h, i in heads:
        dqkv[:, cols_of(1, h)] = (mm(ds[i], qkv[:, cols_of(0, h)]) * SCALE).astype(BF)
    for h, i in heads:
        turn[rows_of(h), :] = (mm(qkv[:, cols_of(1, h)], ds[i], TN) * SCALE).astype(BF)


def block_gradient(h2, x, mod, block, wq, dy, dqkv):
    dnormed = mm(dqkv[span_of(h2), :], wq[...])
    dx = norm_backward(x.astype(F32), dnormed, mod[1, block : block + 1, :])
    return (dx + dy.astype(F32)).astype(BF).reshape(FRAMES, 16, D)


def temporal_open(h2, cot, mod, wo, dproj, datt):
    rows = span_of(h2)
    dpr = (flat(cot, h2).astype(F32) * mod[2, 1:2, :]).astype(BF)
    dproj[rows, :] = dpr
    datt[rows, :] = mm(dpr, wo[...], NT).astype(BF)


def temporal_norm(h2, mod, mid, normed):
    xhat, _ = standardise(flat(mid, h2).astype(F32))
    normed[span_of(h2), :] = (xhat * (1.0 + mod[1, 1:2, :]) + mod[0, 1:2, :]).astype(BF)


def pair_of(part, pair):
    return slice(part * HD + pair * 2 * HEAD, part * HD + (pair + 1) * 2 * HEAD)


def split_pair(x):
    first = lax.broadcasted_iota(jnp.int32, x.shape, 1) < HEAD
    zero = jnp.zeros_like(x)
    return jnp.concatenate([jnp.where(first, x, zero), jnp.where(first, zero, x)], 0)


def pair_tile(pair):
    return pair // 2, slice(pair % 2 * 256, pair % 2 * 256 + 256), slice(0, 512)


def temporal_heads(h2, qkv, datt, dqkv, sb, pt, ds, turn):
    rows = span_of(h2)
    row_id = lax.broadcasted_iota(jnp.int32, (256, 512), 0)
    col_id = lax.broadcasted_iota(jnp.int32, (256, 512), 1)
    mask = (row_id & 15) == (col_id & 15)
    pairs = [(n, pair_tile(n)) for n in range(HEADS // 2)]
    for n, at in pairs:
        sb[at] = mm(qkv[rows, pair_of(1, n)], split_pair(qkv[rows, pair_of(0, n)]), NT)
    for n, at in pairs:
        pt[at] = softmax(sb[at], mask).astype(BF)
    for n, at in pairs:
        sb[at] = mm(qkv[rows, pair_of(2, n)], split_pair(datt[rows, pair_of(0, n)]), NT)
    for n, at in pairs:
        ds[at] = score_backward(pt[at], sb[at])
    for n, at in pairs:
        dqkv[rows, pair_of(2, n)] = mm(pt[at], split_pair(datt[rows, pair_of(0, n)])).astype(BF)
    for n, at in pairs:
        dqkv[rows, pair_of(1, n)] = (mm(ds[at], split_pair(qkv[rows, pair_of(0, n)])) * SCALE).astype(BF)
    for n, at in pairs:
        both = mm(qkv[rows, pair_of(1, n)], ds[at], TN) * SCALE
        turn[rows_of(2 * n), rows] = both[:HEAD, :256].astype(BF)
        turn[rows_of(2 * n + 1), rows] = both[HEAD:, 256:].astype(BF)
    dqkv[rows, 0:HD] = turn[:, rows].T


def temporal_attended(h2, qkv, pt, turn, att):
    rows = span_of(h2)
    for n in range(HEADS // 2):
        both = mm(qkv[rows, pair_of(2, n)], pt[pair_tile(n)], TN)
        turn[rows_of(2 * n), rows] = both[:HEAD, :256].astype(BF)
        turn[rows_of(2 * n + 1), rows] = both[HEAD:, 256:].astype(BF)
    att[rows, :] = turn[:, rows].T


def wait_bytes(view, sem):
    pltpu.make_async_copy(view, view, sem).wait()


class Exchange:
    def __init__(self, n, me, src_of, whole, send, recv):
        self.me, self.src_of, self.whole = me, src_of, whole
        self.send, self.recv = send.at[n], recv.at[n]

    def copy(self, t):
        return pltpu.make_async_remote_copy(
            src_ref=self.src_of(t),
            dst_ref=self.whole.at[self.me],
            send_sem=self.send,
            recv_sem=self.recv,
            device_id={"seq": t},
            device_id_type=MESH,
        )

    def start(self):
        y, x, c = lax.div(self.me, 8), lax.rem(lax.div(self.me, 2), 4), lax.rem(self.me, 2)
        for dc in range(2):
            for dy, dx in ((0, 1), (0, 3), (1, 0), (1, 1), (1, 3), (0, 2), (1, 2), (0, 0))[: 7 + dc]:
                t = lax.rem(y + dy, 2) * 8 + lax.rem(x + dx, 4) * 2 + lax.rem(c + dc, 2)
                self.copy(t).start()
        pltpu.make_async_copy(self.src_of(self.me), self.whole.at[self.me], self.recv).start()

    def arrive(self):
        wait_bytes(self.whole, self.recv)

    def drain(self):
        wait_bytes(self.whole.at[pl.ds(0, FRAMES - 1)], self.send)


def spot(z, y, x, c):
    return {
        "dp": z * 2 + lax.div(y, 2),
        "seq": lax.rem(y, 2) * 8 + x * 2 + c,
    }


class Place:
    def __init__(self):
        dp, seq = lax.axis_index("dp"), lax.axis_index("seq")
        self.z = lax.div(dp, 2)
        self.y = lax.rem(dp, 2) * 2 + lax.div(seq, 8)
        self.x = lax.rem(lax.div(seq, 2), 4)
        self.c = lax.rem(seq, 2)
        self.at = (self.z, self.y, self.x)

    def moved(self, axis, j):
        return spot(*[j if i == axis else v for i, v in enumerate(self.at)], self.c)

    def partner(self):
        return spot(*self.at, 1 - self.c)


ORDERS = ((0, 1, 2), (1, 2, 0), (2, 0, 1))
CHUNK = 288
HALF = 144
BLOCK = 72
SLOT = 80


def odd_even(j):
    return j + 1 - 2 * lax.rem(j, 2)


def send_to(src, dst, send_sem, recv_sem, device):
    return pltpu.make_async_remote_copy(
        src_ref=src, dst_ref=dst, send_sem=send_sem, recv_sem=recv_sem, device_id=device, device_id_type=MESH
    )


class Reducer:
    def __init__(self, place, m, g, out, buf, sem):
        self.p, self.m, self.g, self.out, self.b, self.s = place, m, g, out, buf, sem

    def go0(self, k):
        return send_to(
            self.g.at[(1 - self.p.c) * 3 + k], self.b["r0"].at[self.m, k],
            self.s["s0"].at[self.m], self.s["v0"].at[self.m, k], self.p.partner(),
        )

    def chunk(self, j, half):
        return pl.ds(pl.multiple_of(j * CHUNK + half * HALF, 16), HALF)

    def ring(self, k, half):
        axis = ORDERS[k][0]
        j = self.p.at[axis]
        pair = (odd_even(j), 3 - j)
        return axis, j, pair[half], pair[1 - half]

    def go1(self, k, half, slot):
        axis, j, first, second = self.ring(k, half)
        other = 3 - first if half == 0 else odd_even(first)
        rows = self.chunk(first if slot == 0 else other, half)
        return send_to(
            self.b["r0"].at[self.m, k, rows], self.b["ra"].at[self.m, k, half, slot],
            self.s["sa"].at[self.m, k], self.s["va"].at[self.m, k, half, slot],
            self.p.moved(axis, first),
        )

    def go2(self, k, half):
        axis, j, first, second = self.ring(k, half)
        return send_to(
            self.b["tb"].at[self.m, k, half], self.b["rb"].at[self.m, k, half],
            self.s["sb"].at[self.m, k], self.s["vb"].at[self.m, k, half],
            self.p.moved(axis, second),
        )

    def go3(self, k, to, slot):
        axis = ORDERS[k][1]
        return send_to(
            self.b["t2"].at[self.m, k, to], self.b["r2"].at[self.m, k, slot],
            self.s["s2"].at[self.m, k], self.s["v2"].at[self.m, k],
            self.p.moved(axis, to),
        )

    def go4(self, k, i):
        a, b, c = ORDERS[k]
        return send_to(
            self.b["t3"].at[self.m, k, i], self.b["r3"].at[self.m, k, self.p.at[c] * 2 + self.p.c],
            self.s["s3"].at[self.m, k], self.s["v3"].at[self.m, k],
            spot(self.p.at[a], self.p.at[b], lax.div(i, 2), lax.rem(i, 2)),
        )

    def own4(self, k, i):
        return pltpu.make_async_copy(
            self.b["t3"].at[self.m, k, i],
            self.b["r3"].at[self.m, k, self.p.at[ORDERS[k][2]] * 2 + self.p.c],
            self.s["v3"].at[self.m, k],
        )

    def own_rows(self, k):
        a, b, _ = ORDERS[k]
        return (self.p.at[a] == self.p.z) & (self.p.at[b] == self.p.y)


    def phase0(self, k):
        self.go0(k).start()

    def sent0(self):
        wait_bytes(self.b["r0"].at[self.m], self.s["s0"].at[self.m])

    def phase1(self, k):
        self.go0(k).wait_recv()
        r0 = self.b["r0"]
        n = self.p.c * 3 + k

        @pl.loop(0, D // HALF)
        def _(i):
            rows = pl.ds(pl.multiple_of(i * HALF, 16), HALF)
            r0[self.m, k, rows] = (
                r0[self.m, k, rows].astype(F32) + self.g[n, rows].astype(F32)
            ).astype(BF)

        for slot in (1, 0):
            for half in range(2):
                self.go1(k, half, slot).start()

    def phase2(self, k):
        for half in range(2):
            axis, j, first, second = self.ring(k, half)
            self.go1(k, half, 1).wait_recv()
            rows = self.chunk(second, half)
            self.b["tb"][self.m, k, half] = (
                self.b["r0"][self.m, k, rows].astype(F32) + self.b["ra"][self.m, k, half, 1].astype(F32)
            ).astype(BF)
            self.go2(k, half).start()

    def phase3(self, k):
        axis = ORDERS[k][1]
        me = self.p.at[axis]
        for half in range(2):
            _, j, _, _ = self.ring(k, half)
            self.go1(k, half, 0).wait_recv()
            self.go2(k, half).wait_recv()
            rows = self.chunk(j, half)
            total = (
                self.b["r0"][self.m, k, rows].astype(F32)
                + self.b["ra"][self.m, k, half, 0].astype(F32)
                + self.b["rb"][self.m, k, half].astype(F32)
            )
            for i in range(2):
                self.b["t2"][self.m, k, 2 * half + i, :BLOCK] = total[i * BLOCK : (i + 1) * BLOCK].astype(BF)
                self.b["t2"][self.m, k, 2 * half + i, BLOCK:] = jnp.zeros((SLOT - BLOCK, WIDE), BF)

        @pl.loop(1, 4)
        def _(i):
            self.go3(k, lax.rem(me + i, 4), me).start()

    def phase4(self, k):
        axis = ORDERS[k][1]
        me = self.p.at[axis]
        total = self.b["t2"][self.m, k, me].astype(F32)
        wait_bytes(self.b["r2"].at[self.m, k, pl.ds(0, 3)], self.s["v2"].at[self.m, k])
        for i in range(1, 4):
            t = lax.rem(me + i, 4)
            total = total + self.b["r2"][self.m, k, t].astype(F32)
        row = lax.broadcasted_iota(jnp.int32, (128, SLOT), 0)
        col = lax.broadcasted_iota(jnp.int32, (128, SLOT), 1)
        pick = ((row & 15) < 9) & (col == lax.shift_right_logical(row, 4) * 9 + (row & 15))
        spread = mm(jnp.where(pick, 1.0, 0.0).astype(BF), total.astype(BF)).astype(BF)
        for i in range(8):
            self.b["t3"][self.m, k, i] = spread[i * 16 : i * 16 + 16]
        own = self.own_rows(k)
        mine = self.p.x * 2 + self.p.c

        @pl.loop(0, 8)
        def _(i):
            @pl.when(own & (i == mine))
            def _():
                self.own4(k, i).start()

            @pl.when(jnp.logical_not(own & (i == mine)))
            def _():
                self.go4(k, i).start()

    def phase5(self, k):
        wait_bytes(self.b["r3"].at[self.m, k], self.s["v3"].at[self.m, k])
        for e in range(2):
            total = self.b["r3"][self.m, k, e].astype(F32)
            for s in range(1, 4):
                total = total + self.b["r3"][self.m, k, 2 * s + e].astype(F32)
            n = SLOTS.index(e * 3 + k)
            if n < 4:
                self.out[0][:, n * WIDE : (n + 1) * WIDE] = total[:9]
            elif n == 4:
                self.out[0][:, n * WIDE :] = total[:9, :192]
                self.out[1][:, :192] = total[:9, 192:]
            else:
                self.out[1][:, 192:] = total[:9]

    def drain(self, k):
        wait_bytes(self.b["ra"].at[self.m, k], self.s["sa"].at[self.m, k])
        wait_bytes(self.b["tb"].at[self.m, k], self.s["sb"].at[self.m, k])
        wait_bytes(self.b["t2"].at[self.m, k, pl.ds(0, 3)], self.s["s2"].at[self.m, k])

    def drain3(self, k):
        own = self.own_rows(k)
        for count in (7, 8):
            @pl.when(own if count == 7 else jnp.logical_not(own))
            def _(count=count):
                wait_bytes(self.b["t3"].at[self.m, k, pl.ds(0, count)], self.s["s3"].at[self.m, k])


def greet(p, me):
    barrier = pltpu.get_barrier_semaphore()

    def hail(device):
        pl.semaphore_signal(barrier, inc=1, device_id=device, device_id_type=MESH)

    @pl.loop(1, FRAMES)
    def _(i):
        hail({"seq": lax.rem(me + i, FRAMES)})

    hail(p.partner())
    for axis in range(3):
        for i in range(1, 4):
            hail(p.moved(axis, lax.rem(p.at[axis] + i, 4)))
    selves = 0
    for k in range(3):
        a, b, c = ORDERS[k]

        @pl.loop(0, 8)
        def _(i):
            s, e = lax.div(i, 2), lax.rem(i, 2)
            where = [None] * 3
            where[a], where[b], where[c] = p.z, p.y, s
            same = (where[0] == p.z) & (where[1] == p.y) & (where[2] == p.x) & (e == p.c)

            @pl.when(jnp.logical_not(same))
            def _():
                hail(spot(*where, e))

        own = (p.at[a] == p.z) & (p.at[b] == p.y)
        selves = selves + jnp.where(own & (p.at[c] == p.x), 1, 0)
    return FRAMES - 1 + 10 + 24 - selves


def reduce_buffers(count):
    dma = pltpu.SemaphoreType.DMA
    bufs = dict(
        r0=pltpu.VMEM((count, 3, D, WIDE), BF),
        ra=pltpu.VMEM((count, 3, 2, 2, HALF, WIDE), BF),
        tb=pltpu.VMEM((count, 3, 2, HALF, WIDE), BF),
        rb=pltpu.VMEM((count, 3, 2, HALF, WIDE), BF),
        t2=pltpu.VMEM((count, 3, 4, SLOT, WIDE), BF),
        r2=pltpu.VMEM((count, 3, 4, SLOT, WIDE), BF),
        t3=pltpu.VMEM((count, 3, 8, 16, WIDE), BF),
        r3=pltpu.VMEM((count, 3, 8, 16, WIDE), BF),
    )
    sems = dict(
        s0=dma((count,)), sa=dma((count, 3)), sb=dma((count, 3)), s2=dma((count, 3)), s3=dma((count, 3)),
        v0=dma((count, 3)), va=dma((count, 3, 2, 2)), vb=dma((count, 3, 2)), v2=dma((count, 3)), v3=dma((count, 3)),
    )
    return bufs, sems


def kernel(ins, outs, v, sem, buf, rsem):
    me = lax.axis_index("seq")
    p = Place()
    mod = ins["mod"]
    lat, cot, mid, dmid, g = v["lat"], v["cot"], v["mid"], v["dmid"], v["g"]

    def load(src, dst, n):
        return pltpu.make_async_copy(src, dst, sem["load"].at[n])

    loads = {}
    for n, (k, h2) in enumerate((("lat", 0), ("lat", 1), ("cot", 0), ("cot", 1))):
        loads[k, h2] = load(ins[k].at[:, h2], v[k].at[h2], n)
    for n, k in enumerate(("wq_s", "wo_s", "wo_t", "wq_t")):
        loads[k] = load(ins[k], v[k], 4 + n)
    order = (("lat", 0), ("lat", 1), "wq_s", "wo_s", ("cot", 0), ("cot", 1), "wo_t", "wq_t")
    for k in order:
        loads[k].start()
    expected = greet(p, me)

    def exchange(n, src_of, whole):
        return Exchange(n, me, src_of, whole, sem["send"], sem["recv"])

    def frame_rows(t):
        return pl.ds(pl.multiple_of(t * 16, 16), 16)

    lat_x = exchange(0, lambda t: lat.at[0, t], v["lat_in"])
    att_x = exchange(1, lambda t: v["att_s"].at[frame_rows(t)], v["att_in"])
    mid_x = exchange(2, lambda t: v["mid_s"].at[frame_rows(t)], mid.at[1])
    dmid_x = [
        exchange(3 + h2, lambda t, h2=h2: v["dmid_t"].at[h2, t], dmid.at[h2])
        for h2 in range(2)
    ]
    red_t = Reducer(p, 0, g, (outs["qkv_t"], outs["out_t"]), buf, rsem)
    red_s = Reducer(p, 1, g, (outs["qkv_s"], outs["out_s"]), buf, rsem)

    def reduce_step(red, name, ks=(1, 0, 2)):
        for k in ks:
            getattr(red, name)(k)

    def wave(red, name, late):
        c = 1 - p.c if name == "phase0" else p.c
        for core in range(2):
            ks = [(0,), (1, 2)][core ^ late]

            @pl.when(c == core)
            def _(ks=ks):
                reduce_step(red, name, ks)

    loads["lat", 0].wait()
    loads["lat", 1].wait()
    spatial_norm(lat, mod, v["normed_s"])
    pl.semaphore_wait(pltpu.get_barrier_semaphore(), expected)
    lat_x.start()
    loads["wq_s"].wait()
    project(v["normed_s"], v["wq_s"], v["qkv_s"], (0, 1))
    for pair in range(4):
        spatial_heads(pair, v["qkv_s"], v["probs"], v["sb"], v["turn"])
    v["att_s"][...] = v["turn"][...].T
    att_x.start()
    loads["wo_s"].wait()
    v["mid_s"][...] = block_result(1, flat(lat, 1).astype(F32), mod, 0, v["wo_s"], v["att_s"][256:, :])
    mid_x.start()

    for k in order[4:]:
        loads[k].wait()
    for h2 in range(2):
        temporal_open(h2, cot, mod, v["wo_t"], v["dproj"], v["datt"])
    for h2 in range(2):
        if h2 == 0:
            lat_x.arrive()
            att_x.arrive()
            x = v["lat_in"][...].reshape(256, D).astype(F32)
            att_in = v["att_in"][...].reshape(256, HD)
            mid[0] = block_result(0, x, mod, 0, v["wo_s"], att_in).reshape(FRAMES, 16, D)
        else:
            mid_x.arrive()
        temporal_norm(h2, mod, mid, v["normed_t"])
        project(v["normed_t"], v["wq_t"], v["qkv_t"], (h2,))
        temporal_heads(h2, v["qkv_t"], v["datt"], v["dqkv"], v["sb"], v["pt"], v["ds"], v["turn"])
        v["dmid_t"][h2] = block_gradient(h2, flat(mid, h2), mod, 1, v["wq_t"], flat(cot, h2), v["dqkv"])
        dmid_x[h2].start()
        temporal_attended(h2, v["qkv_t"], v["pt"], v["turn"], v["att_t"])
    for first in (True, False):
        weight_grads(first, v["normed_t"], v["dqkv"], v["dproj"], v["att_t"], g)
        wave(red_t, "phase0", not first)
    store_out = []
    for h2 in range(2):
        y = block_result(h2, flat(mid, h2).astype(F32), mod, 1, v["wo_t"], v["att_t"][span_of(h2), :])
        v["block_out"][h2] = y.reshape(FRAMES, 16, D)
        store_out.append(pltpu.make_async_copy(v["block_out"].at[h2], outs["block_out"].at[:, h2], sem["store"].at[h2]))
        store_out[h2].start()

    for x in (lat_x, att_x, mid_x):
        x.drain()

    for h2 in range(2):
        dmid_x[h2].arrive()
        spatial_back_open(h2, mod, v["wo_s"], dmid, v["dproj"], v["datt"])
    spatial_back_values(v["qkv_s"], v["probs"], v["datt"], v["dqkv"])
    reduce_step(red_t, "phase1")
    red_t.sent0()
    weight_grads(True, v["normed_s"], v["dqkv"], v["dproj"], v["att_s"], g)
    wave(red_s, "phase0", 0)
    for pair in range(4):
        if pair == 3:
            reduce_step(red_t, "phase2")
        spatial_back_heads(pair, v["qkv_s"], v["probs"], v["datt"], v["dqkv"], v["sb"], v["ds"], v["turn"])
    v["dqkv"][:, 0:HD] = v["turn"][...].T
    weight_grads(False, v["normed_s"], v["dqkv"], v["dproj"], v["att_s"], g)
    wave(red_s, "phase0", 1)
    wave(red_s, "phase1", 0)
    reduce_step(red_t, "phase3")
    lat_grad = mid
    store_grad = []
    for h2 in range(2):
        lat_grad[h2] = block_gradient(h2, flat(lat, h2), mod, 0, v["wq_s"], flat(dmid, h2), v["dqkv"])
        store_grad.append(pltpu.make_async_copy(lat_grad.at[h2], outs["lat_grad"].at[:, h2], sem["store"].at[2 + h2]))
        store_grad[h2].start()

    wave(red_s, "phase1", 1)
    wave(red_s, "phase2", 0)
    reduce_step(red_t, "phase4")
    for x in dmid_x:
        x.drain()
    wave(red_s, "phase2", 1)
    wave(red_s, "phase3", 0)
    for c in store_out + store_grad:
        c.wait()
    wave(red_s, "phase3", 1)
    wave(red_s, "phase4", 0)
    reduce_step(red_t, "phase5")
    wave(red_s, "phase4", 1)
    reduce_step(red_t, "drain")
    reduce_step(red_t, "drain3")
    red_s.sent0()
    reduce_step(red_s, "drain")
    reduce_step(red_s, "phase5")
    reduce_step(red_s, "drain3")


def shape(dims, kind=BF):
    return jax.ShapeDtypeStruct(dims, kind)


def params(collective_id=None):
    if collective_id is None:
        return pltpu.CompilerParams(vmem_limit_bytes=VMEM_LIMIT)
    return pltpu.CompilerParams(
        vmem_limit_bytes=VMEM_LIMIT, collective_id=collective_id, has_side_effects=True
    )


VMEM_LIMIT = 62 * 1024 * 1024
INPUTS = ("lat", "mod", "wq_s", "wo_s", "wq_t", "wo_t", "cot")
OUTPUTS = {
    "block_out": shape((FRAMES, 2, 16, D)),
    "lat_grad": shape((FRAMES, 2, 16, D)),
    "qkv_s": shape((9, QKV), F32),
    "out_s": shape((9, HD), F32),
    "qkv_t": shape((9, QKV), F32),
    "out_t": shape((9, HD), F32),
}
HALVES = (2, FRAMES, 16, D)
VALUES = {
    "lat": HALVES, "cot": HALVES,
    "wq_s": (QKV, D), "wo_s": (HD, D), "wq_t": (QKV, D), "wo_t": (HD, D),
    "normed_s": (TOK, D), "qkv_s": (TOK, QKV), "probs": (HEADS, TOK, TOK), "att_s": (TOK, HD),
    "mid_s": (256, D), "lat_in": HALVES[1:], "att_in": (FRAMES, 16, HD),
    "mid": HALVES, "normed_t": (TOK, D), "qkv_t": (TOK, QKV), "att_t": (TOK, HD),
    "dproj": (TOK, D), "datt": (TOK, HD), "dqkv": (TOK, QKV),
    "sb": (2, TOK, TOK), "pt": (2, TOK, TOK), "ds": (2, TOK, TOK), "turn": (HD, TOK),
    "dmid_t": HALVES, "dmid": HALVES, "block_out": HALVES,
    "g": (PIECES, D, WIDE),
}
KINDS = {"sb": F32}


def run(*args):
    dma = pltpu.SemaphoreType.DMA
    bufs, rsems = reduce_buffers(2)
    sems = {
        "load": dma((8,)), "store": dma((4,)),
        "send": dma((5,)), "recv": dma((5,)),
    }
    values = {k: pltpu.VMEM(d, KINDS.get(k, BF)) for k, d in VALUES.items()}
    groups = (values, sems, bufs, rsems)

    def unpack(*refs):
        refs = list(refs)

        def take(names):
            got = dict(zip(names, refs))
            del refs[: len(got)]
            return got

        kernel(take(INPUTS), take(OUTPUTS), *[take(g) for g in groups])

    return pl.pallas_call(
        unpack,
        out_shape=tuple(OUTPUTS.values()),
        in_specs=[vmem_spec() if k == "mod" else any_spec() for k in INPUTS],
        out_specs=[any_spec()] * 2 + [vmem_spec()] * 4,
        scratch_shapes=[x for g in groups for x in g.values()],
        compiler_params=params(0),
        name="attention_blocks",
    )(*args)


def hand_over(*refs):
    n = (len(refs) - 2) // 3
    sems = refs[-2:]
    ins = [pltpu.make_async_copy(refs[i], refs[2 * n + i], sems[0].at[i]) for i in range(n)]
    outs = [pltpu.make_async_copy(refs[2 * n + i], refs[n + i], sems[1].at[i]) for i in range(n)]
    for c in ins:
        c.start()
    for i in range(n):
        ins[i].wait()
        outs[i].start()
    for c in outs:
        c.wait()


def body(latents, modulation, spatial_qkv, spatial_out, temporal_qkv, temporal_out, cotangent):
    halves = (FRAMES, 2, 16, D)
    results = run(
        latents.reshape(halves), modulation[0].transpose(1, 0, 2), spatial_qkv.T, spatial_out,
        temporal_qkv.T, temporal_out, cotangent.reshape(halves),
    )
    block_out, lat_grad, qkv_s, out_s, qkv_t, out_t = pl.pallas_call(
        hand_over,
        out_shape=tuple(OUTPUTS.values()),
        in_specs=[any_spec()] * 6,
        out_specs=[any_spec()] * 6,
        scratch_shapes=[pltpu.VMEM(x.shape, x.dtype) for x in OUTPUTS.values()]
        + [pltpu.SemaphoreType.DMA((6,))] * 2,
        compiler_params=params(),
        name="hand_over",
    )(*results)
    return (
        block_out.reshape(1, FRAMES, SPAN, D), lat_grad.reshape(1, 1, TOK, D),
        qkv_s, out_s.T, qkv_t, out_t.T,
    )


def solution(mesh):
    return jax.shard_map(
        body,
        mesh=mesh,
        in_specs=(
            P("dp", "seq", None, None),
            P("dp", None, None, None),
            P(),
            P(),
            P(),
            P(),
            P("dp", None, "seq", None),
        ),
        out_specs=(
            P("dp", None, "seq", None),
            P("dp", "seq", None, None),
            P(("dp", "seq"), None),
            P(None, ("dp", "seq")),
            P(("dp", "seq"), None),
            P(None, ("dp", "seq")),
        ),
        check_vma=False,
    )
```

```python
import functools
import math

import jax
import jax.numpy as jnp
from jax import lax
from jax.experimental import pallas as pl
from jax.experimental.pallas import tpu as pltpu
from jax.sharding import PartitionSpec as P

D = 1152
HEADS = 8
HEAD = 72
HD = 576
QKV = 3 * HD
FRAMES = 16
POS = 512
SPAN = 32
TOK = 512
SCALE = HEAD ** (-0.5)
EXP2 = SCALE / math.log(2.0)
MESH = pl.DeviceIdType.MESH
BF = jnp.bfloat16
F32 = jnp.float32
PIECES = 6
WIDE = 384

NN = (((1,), (0,)), ((), ()))
NT = (((1,), (1,)), ((), ()))
TN = (((0,), (0,)), ((), ()))


def mm(a, b, form=NN):
    return lax.dot_general(a, b, form, preferred_element_type=F32)


def vmem_spec():
    return pl.BlockSpec(memory_space=pltpu.VMEM)


def any_spec():
    return pl.BlockSpec(memory_space=pl.ANY)


def standardise(x):
    centre = jnp.mean(x, -1, keepdims=True)
    centred = x - centre
    spread = jnp.mean(centred * centred, -1, keepdims=True)
    rstd = lax.rsqrt(spread + 1e-06)
    return centred * rstd, rstd


def norm_backward(x, dnormed, scale):
    xhat, rstd = standardise(x)
    dxhat = dnormed * (1.0 + scale)
    first = jnp.mean(dxhat, -1, keepdims=True)
    second = jnp.mean(dxhat * xhat, -1, keepdims=True)
    return rstd * (dxhat - first - xhat * second)


def softmax(scores, mask=None):
    if mask is not None:
        scores = jnp.where(mask, scores, -1e30)
    largest = jnp.max(scores, 0, keepdims=True)
    expo = jnp.exp2((scores - largest) * EXP2)
    return expo * (1.0 / jnp.sum(expo, 0, keepdims=True))


def cols_of(part, h):
    return slice(part * HD + h * HEAD, part * HD + (h + 1) * HEAD)


def rows_of(h):
    return slice(h * HEAD, (h + 1) * HEAD)


def score_backward(p, dp):
    wide = p.astype(F32)
    return (wide * (dp - jnp.sum(dp * wide, 0, keepdims=True))).astype(BF)


SLOTS = (3, 1, 2, 0, 4, 5)


def weight_grads(first, normed, dqkv, dproj, att, g):
    for lo in range(0, D, 384):
        rows = slice(lo, lo + 384)
        left = normed[:, rows]
        if first:
            vals = mm(left, dqkv[:, 2 * HD :], TN)
            outs = mm(dproj[:, rows], att[...], TN)
            g[SLOTS[3], rows, :] = vals[:, :WIDE].astype(BF)
            g[SLOTS[4], rows, :192] = vals[:, WIDE:].astype(BF)
            g[SLOTS[4], rows, 192:] = outs[:, :192].astype(BF)
            g[SLOTS[5], rows, :] = outs[:, 192:].astype(BF)
        else:
            both = mm(left, dqkv[:, : 2 * HD], TN)
            for n in range(3):
                g[SLOTS[n], rows, :] = both[:, n * WIDE : (n + 1) * WIDE].astype(BF)


def span_of(h2):
    return slice(h2 * 256, (h2 + 1) * 256)


def flat(ref, h2):
    return ref[h2].reshape(256, ref.shape[-1])


def spatial_norm(lat, mod, normed):
    shift, scale = mod[0, 0:1, :], mod[1, 0:1, :]
    for h2 in range(2):
        for lo in (0, 8):
            xhat, _ = standardise(lat[h2, lo : lo + 8].reshape(128, D).astype(F32))
            rows = slice(h2 * 256 + lo * 16, h2 * 256 + lo * 16 + 128)
            normed[rows, :] = (xhat * (1.0 + scale) + shift).astype(BF)


def project(normed, wq, qkv, spans):
    for h2 in spans:
        qkv[span_of(h2), :] = mm(normed[span_of(h2), :], wq[...], NT).astype(BF)


def spatial_heads(pair, qkv, probs, sb, turn):
    heads = [(pair * 2 + i, i) for i in range(2)]
    for h, i in heads:
        sb[i] = mm(qkv[:, cols_of(1, h)], qkv[:, cols_of(0, h)], NT)
    for h, i in heads:
        probs[h] = softmax(sb[i]).astype(BF)
    for h, i in heads:
        turn[rows_of(h), :] = mm(qkv[:, cols_of(2, h)], probs[h], TN).astype(BF)


def block_result(h2, x, mod, block, wo, att):
    gate = mod[2, block : block + 1, :]
    return (x + gate * mm(att, wo[...])).astype(BF)


def spatial_back_open(h2, mod, wo, dmid, dproj, datt):
    rows = span_of(h2)
    dpr = (flat(dmid, h2).astype(F32) * mod[2, 0:1, :]).astype(BF)
    dproj[rows, :] = dpr
    datt[rows, :] = mm(dpr, wo[...], NT).astype(BF)


def spatial_back_values(qkv, probs, datt, dqkv):
    for h in range(HEADS):
        dqkv[:, cols_of(2, h)] = mm(probs[h], datt[:, cols_of(0, h)]).astype(BF)


def spatial_back_heads(pair, qkv, probs, datt, dqkv, sb, ds, turn):
    heads = [(pair * 2 + i, i) for i in range(2)]
    for h, i in heads:
        sb[i] = mm(qkv[:, cols_of(2, h)], datt[:, cols_of(0, h)], NT)
    for h, i in heads:
        ds[i] = score_backward(probs[h], sb[i])
    for h, i in heads:
        dqkv[:, cols_of(1, h)] = (mm(ds[i], qkv[:, cols_of(0, h)]) * SCALE).astype(BF)
    for h, i in heads:
        turn[rows_of(h), :] = (mm(qkv[:, cols_of(1, h)], ds[i], TN) * SCALE).astype(BF)


def block_gradient(h2, x, mod, block, wq, dy, dqkv):
    dnormed = mm(dqkv[span_of(h2), :], wq[...])
    dx = norm_backward(x.astype(F32), dnormed, mod[1, block : block + 1, :])
    return (dx + dy.astype(F32)).astype(BF).reshape(FRAMES, 16, D)


def temporal_open(h2, cot, mod, wo, dproj, datt):
    rows = span_of(h2)
    dpr = (flat(cot, h2).astype(F32) * mod[2, 1:2, :]).astype(BF)
    dproj[rows, :] = dpr
    datt[rows, :] = mm(dpr, wo[...], NT).astype(BF)


def temporal_norm(h2, mod, mid, normed):
    xhat, _ = standardise(flat(mid, h2).astype(F32))
    normed[span_of(h2), :] = (xhat * (1.0 + mod[1, 1:2, :]) + mod[0, 1:2, :]).astype(BF)


def pair_of(part, pair):
    return slice(part * HD + pair * 2 * HEAD, part * HD + (pair + 1) * 2 * HEAD)


def split_pair(x):
    first = lax.broadcasted_iota(jnp.int32, x.shape, 1) < HEAD
    zero = jnp.zeros_like(x)
    return jnp.concatenate([jnp.where(first, x, zero), jnp.where(first, zero, x)], 0)


def pair_tile(pair):
    return pair // 2, slice(pair % 2 * 256, pair % 2 * 256 + 256), slice(0, 512)


def temporal_heads(h2, qkv, datt, dqkv, sb, pt, ds, turn):
    rows = span_of(h2)
    row_id = lax.broadcasted_iota(jnp.int32, (256, 512), 0)
    col_id = lax.broadcasted_iota(jnp.int32, (256, 512), 1)
    mask = (row_id & 15) == (col_id & 15)
    pairs = [(n, pair_tile(n)) for n in range(HEADS // 2)]
    for n, at in pairs:
        sb[at] = mm(qkv[rows, pair_of(1, n)], split_pair(qkv[rows, pair_of(0, n)]), NT)
    for n, at in pairs:
        pt[at] = softmax(sb[at], mask).astype(BF)
    for n, at in pairs:
        sb[at] = mm(qkv[rows, pair_of(2, n)], split_pair(datt[rows, pair_of(0, n)]), NT)
    for n, at in pairs:
        ds[at] = score_backward(pt[at], sb[at])
    for n, at in pairs:
        dqkv[rows, pair_of(2, n)] = mm(pt[at], split_pair(datt[rows, pair_of(0, n)])).astype(BF)
    for n, at in pairs:
        dqkv[rows, pair_of(1, n)] = (mm(ds[at], split_pair(qkv[rows, pair_of(0, n)])) * SCALE).astype(BF)
    for n, at in pairs:
        both = mm(qkv[rows, pair_of(1, n)], ds[at], TN) * SCALE
        turn[rows_of(2 * n), rows] = both[:HEAD, :256].astype(BF)
        turn[rows_of(2 * n + 1), rows] = both[HEAD:, 256:].astype(BF)
    dqkv[rows, 0:HD] = turn[:, rows].T


def temporal_attended(h2, qkv, pt, turn, att):
    rows = span_of(h2)
    for n in range(HEADS // 2):
        both = mm(qkv[rows, pair_of(2, n)], pt[pair_tile(n)], TN)
        turn[rows_of(2 * n), rows] = both[:HEAD, :256].astype(BF)
        turn[rows_of(2 * n + 1), rows] = both[HEAD:, 256:].astype(BF)
    att[rows, :] = turn[:, rows].T


def wait_bytes(view, sem):
    pltpu.make_async_copy(view, view, sem).wait()


class Exchange:
    def __init__(self, n, me, src_of, whole, send, recv):
        self.me, self.src_of, self.whole = me, src_of, whole
        self.send, self.recv = send.at[n], recv.at[n]

    def copy(self, t):
        return pltpu.make_async_remote_copy(
            src_ref=self.src_of(t),
            dst_ref=self.whole.at[self.me],
            send_sem=self.send,
            recv_sem=self.recv,
            device_id={"seq": t},
            device_id_type=MESH,
        )

    def start(self):
        y, x, c = lax.div(self.me, 8), lax.rem(lax.div(self.me, 2), 4), lax.rem(self.me, 2)
        for dc in range(2):
            for dy, dx in ((0, 1), (0, 3), (1, 0), (1, 1), (1, 3), (0, 2), (1, 2), (0, 0))[: 7 + dc]:
                t = lax.rem(y + dy, 2) * 8 + lax.rem(x + dx, 4) * 2 + lax.rem(c + dc, 2)
                self.copy(t).start()
        pltpu.make_async_copy(self.src_of(self.me), self.whole.at[self.me], self.recv).start()

    def arrive(self):
        wait_bytes(self.whole, self.recv)

    def drain(self):
        wait_bytes(self.whole.at[pl.ds(0, FRAMES - 1)], self.send)


def spot(z, y, x, c):
    return {
        "dp": z * 2 + lax.div(y, 2),
        "seq": lax.rem(y, 2) * 8 + x * 2 + c,
    }


class Place:
    def __init__(self):
        dp, seq = lax.axis_index("dp"), lax.axis_index("seq")
        self.z = lax.div(dp, 2)
        self.y = lax.rem(dp, 2) * 2 + lax.div(seq, 8)
        self.x = lax.rem(lax.div(seq, 2), 4)
        self.c = lax.rem(seq, 2)
        self.at = (self.z, self.y, self.x)

    def moved(self, axis, j):
        return spot(*[j if i == axis else v for i, v in enumerate(self.at)], self.c)

    def partner(self):
        return spot(*self.at, 1 - self.c)


ORDERS = ((0, 1, 2), (1, 2, 0), (2, 0, 1))
CHUNK = 288
HALF = 144
BLOCK = 72
SLOT = 80


def odd_even(j):
    return j + 1 - 2 * lax.rem(j, 2)


def send_to(src, dst, send_sem, recv_sem, device):
    return pltpu.make_async_remote_copy(
        src_ref=src, dst_ref=dst, send_sem=send_sem, recv_sem=recv_sem, device_id=device, device_id_type=MESH
    )


class Reducer:
    def __init__(self, place, m, g, out, buf, sem):
        self.p, self.m, self.g, self.out, self.b, self.s = place, m, g, out, buf, sem

    def go0(self, k):
        return send_to(
            self.g.at[(1 - self.p.c) * 3 + k], self.b["r0"].at[self.m, k],
            self.s["s0"].at[self.m], self.s["v0"].at[self.m, k], self.p.partner(),
        )

    def chunk(self, j, half):
        return pl.ds(pl.multiple_of(j * CHUNK + half * HALF, 16), HALF)

    def ring(self, k, half):
        axis = ORDERS[k][0]
        j = self.p.at[axis]
        pair = (odd_even(j), 3 - j)
        return axis, j, pair[half], pair[1 - half]

    def go1(self, k, half, slot):
        axis, j, first, second = self.ring(k, half)
        other = 3 - first if half == 0 else odd_even(first)
        rows = self.chunk(first if slot == 0 else other, half)
        return send_to(
            self.b["r0"].at[self.m, k, rows], self.b["ra"].at[self.m, k, half, slot],
            self.s["sa"].at[self.m, k], self.s["va"].at[self.m, k, half, slot],
            self.p.moved(axis, first),
        )

    def go2(self, k, half):
        axis, j, first, second = self.ring(k, half)
        return send_to(
            self.b["tb"].at[self.m, k, half], self.b["rb"].at[self.m, k, half],
            self.s["sb"].at[self.m, k], self.s["vb"].at[self.m, k, half],
            self.p.moved(axis, second),
        )

    def go3(self, k, to, slot):
        axis = ORDERS[k][1]
        return send_to(
            self.b["t2"].at[self.m, k, to], self.b["r2"].at[self.m, k, slot],
            self.s["s2"].at[self.m, k], self.s["v2"].at[self.m, k],
            self.p.moved(axis, to),
        )

    def go4(self, k, i):
        a, b, c = ORDERS[k]
        return send_to(
            self.b["t3"].at[self.m, k, i], self.b["r3"].at[self.m, k, self.p.at[c] * 2 + self.p.c],
            self.s["s3"].at[self.m, k], self.s["v3"].at[self.m, k],
            spot(self.p.at[a], self.p.at[b], lax.div(i, 2), lax.rem(i, 2)),
        )

    def own4(self, k, i):
        return pltpu.make_async_copy(
            self.b["t3"].at[self.m, k, i],
            self.b["r3"].at[self.m, k, self.p.at[ORDERS[k][2]] * 2 + self.p.c],
            self.s["v3"].at[self.m, k],
        )

    def own_rows(self, k):
        a, b, _ = ORDERS[k]
        return (self.p.at[a] == self.p.z) & (self.p.at[b] == self.p.y)


    def phase0(self, k):
        self.go0(k).start()

    def sent0(self):
        wait_bytes(self.b["r0"].at[self.m], self.s["s0"].at[self.m])

    def phase1(self, k):
        self.go0(k).wait_recv()
        r0 = self.b["r0"]
        n = self.p.c * 3 + k

        @pl.loop(0, D // HALF)
        def _(i):
            rows = pl.ds(pl.multiple_of(i * HALF, 16), HALF)
            r0[self.m, k, rows] = (
                r0[self.m, k, rows].astype(F32) + self.g[n, rows].astype(F32)
            ).astype(BF)

        for slot in (1, 0):
            for half in range(2):
                self.go1(k, half, slot).start()

    def phase2(self, k):
        for half in range(2):
            axis, j, first, second = self.ring(k, half)
            self.go1(k, half, 1).wait_recv()
            rows = self.chunk(second, half)
            self.b["tb"][self.m, k, half] = (
                self.b["r0"][self.m, k, rows].astype(F32) + self.b["ra"][self.m, k, half, 1].astype(F32)
            ).astype(BF)
            self.go2(k, half).start()

    def phase3(self, k):
        axis = ORDERS[k][1]
        me = self.p.at[axis]
        for half in range(2):
            _, j, _, _ = self.ring(k, half)
            self.go1(k, half, 0).wait_recv()
            self.go2(k, half).wait_recv()
            rows = self.chunk(j, half)
            total = (
                self.b["r0"][self.m, k, rows].astype(F32)
                + self.b["ra"][self.m, k, half, 0].astype(F32)
                + self.b["rb"][self.m, k, half].astype(F32)
            )
            for i in range(2):
                self.b["t2"][self.m, k, 2 * half + i, :BLOCK] = total[i * BLOCK : (i + 1) * BLOCK].astype(BF)
                self.b["t2"][self.m, k, 2 * half + i, BLOCK:] = jnp.zeros((SLOT - BLOCK, WIDE), BF)

        @pl.loop(1, 4)
        def _(i):
            self.go3(k, lax.rem(me + i, 4), me).start()

    def phase4(self, k):
        axis = ORDERS[k][1]
        me = self.p.at[axis]
        total = self.b["t2"][self.m, k, me].astype(F32)
        wait_bytes(self.b["r2"].at[self.m, k, pl.ds(0, 3)], self.s["v2"].at[self.m, k])
        for i in range(1, 4):
            t = lax.rem(me + i, 4)
            total = total + self.b["r2"][self.m, k, t].astype(F32)
        row = lax.broadcasted_iota(jnp.int32, (128, SLOT), 0)
        col = lax.broadcasted_iota(jnp.int32, (128, SLOT), 1)
        pick = ((row & 15) < 9) & (col == lax.shift_right_logical(row, 4) * 9 + (row & 15))
        spread = mm(jnp.where(pick, 1.0, 0.0).astype(BF), total.astype(BF)).astype(BF)
        for i in range(8):
            self.b["t3"][self.m, k, i] = spread[i * 16 : i * 16 + 16]
        own = self.own_rows(k)
        mine = self.p.x * 2 + self.p.c

        @pl.loop(0, 8)
        def _(i):
            @pl.when(own & (i == mine))
            def _():
                self.own4(k, i).start()

            @pl.when(jnp.logical_not(own & (i == mine)))
            def _():
                self.go4(k, i).start()

    def phase5(self, k):
        wait_bytes(self.b["r3"].at[self.m, k], self.s["v3"].at[self.m, k])
        for e in range(2):
            total = self.b["r3"][self.m, k, e].astype(F32)
            for s in range(1, 4):
                total = total + self.b["r3"][self.m, k, 2 * s + e].astype(F32)
            n = SLOTS.index(e * 3 + k)
            if n < 4:
                self.out[0][:, n * WIDE : (n + 1) * WIDE] = total[:9]
            elif n == 4:
                self.out[0][:, n * WIDE :] = total[:9, :192]
                self.out[1][:, :192] = total[:9, 192:]
            else:
                self.out[1][:, 192:] = total[:9]

    def drain(self, k):
        wait_bytes(self.b["ra"].at[self.m, k], self.s["sa"].at[self.m, k])
        wait_bytes(self.b["tb"].at[self.m, k], self.s["sb"].at[self.m, k])
        wait_bytes(self.b["t2"].at[self.m, k, pl.ds(0, 3)], self.s["s2"].at[self.m, k])

    def drain3(self, k):
        own = self.own_rows(k)
        for count in (7, 8):
            @pl.when(own if count == 7 else jnp.logical_not(own))
            def _(count=count):
                wait_bytes(self.b["t3"].at[self.m, k, pl.ds(0, count)], self.s["s3"].at[self.m, k])


def greet(p, me):
    barrier = pltpu.get_barrier_semaphore()

    def hail(device):
        pl.semaphore_signal(barrier, inc=1, device_id=device, device_id_type=MESH)

    @pl.loop(1, FRAMES)
    def _(i):
        hail({"seq": lax.rem(me + i, FRAMES)})

    hail(p.partner())
    for axis in range(3):
        for i in range(1, 4):
            hail(p.moved(axis, lax.rem(p.at[axis] + i, 4)))
    selves = 0
    for k in range(3):
        a, b, c = ORDERS[k]

        @pl.loop(0, 8)
        def _(i):
            s, e = lax.div(i, 2), lax.rem(i, 2)
            where = [None] * 3
            where[a], where[b], where[c] = p.z, p.y, s
            same = (where[0] == p.z) & (where[1] == p.y) & (where[2] == p.x) & (e == p.c)

            @pl.when(jnp.logical_not(same))
            def _():
                hail(spot(*where, e))

        own = (p.at[a] == p.z) & (p.at[b] == p.y)
        selves = selves + jnp.where(own & (p.at[c] == p.x), 1, 0)
    return FRAMES - 1 + 10 + 24 - selves


def reduce_buffers(count):
    dma = pltpu.SemaphoreType.DMA
    bufs = dict(
        r0=pltpu.VMEM((count, 3, D, WIDE), BF),
        ra=pltpu.VMEM((count, 3, 2, 2, HALF, WIDE), BF),
        tb=pltpu.VMEM((count, 3, 2, HALF, WIDE), BF),
        rb=pltpu.VMEM((count, 3, 2, HALF, WIDE), BF),
        t2=pltpu.VMEM((count, 3, 4, SLOT, WIDE), BF),
        r2=pltpu.VMEM((count, 3, 4, SLOT, WIDE), BF),
        t3=pltpu.VMEM((count, 3, 8, 16, WIDE), BF),
        r3=pltpu.VMEM((count, 3, 8, 16, WIDE), BF),
    )
    sems = dict(
        s0=dma((count,)), sa=dma((count, 3)), sb=dma((count, 3)), s2=dma((count, 3)), s3=dma((count, 3)),
        v0=dma((count, 3)), va=dma((count, 3, 2, 2)), vb=dma((count, 3, 2)), v2=dma((count, 3)), v3=dma((count, 3)),
    )
    return bufs, sems


def kernel(ins, outs, v, sem, buf, rsem):
    me = lax.axis_index("seq")
    p = Place()
    mod = ins["mod"]
    lat, cot, mid, dmid, g = v["lat"], v["cot"], v["mid"], v["dmid"], v["g"]

    def load(src, dst, n):
        return pltpu.make_async_copy(src, dst, sem["load"].at[n])

    loads = {}
    for n, (k, h2) in enumerate((("lat", 0), ("lat", 1), ("cot", 0), ("cot", 1))):
        loads[k, h2] = load(ins[k].at[:, h2], v[k].at[h2], n)
    for n, k in enumerate(("wq_s", "wo_s", "wo_t", "wq_t")):
        loads[k] = load(ins[k], v[k], 4 + n)
    order = (("lat", 0), ("lat", 1), "wq_s", "wo_s", ("cot", 0), ("cot", 1), "wo_t", "wq_t")
    for k in order:
        loads[k].start()
    expected = greet(p, me)

    def exchange(n, src_of, whole):
        return Exchange(n, me, src_of, whole, sem["send"], sem["recv"])

    def frame_rows(t):
        return pl.ds(pl.multiple_of(t * 16, 16), 16)

    lat_x = exchange(0, lambda t: lat.at[0, t], v["lat_in"])
    att_x = exchange(1, lambda t: v["att_s"].at[frame_rows(t)], v["att_in"])
    mid_x = exchange(2, lambda t: v["mid_s"].at[frame_rows(t)], mid.at[1])
    dmid_x = [
        exchange(3 + h2, lambda t, h2=h2: v["dmid_t"].at[h2, t], dmid.at[h2])
        for h2 in range(2)
    ]
    red_t = Reducer(p, 0, g, (outs["qkv_t"], outs["out_t"]), buf, rsem)
    red_s = Reducer(p, 1, g, (outs["qkv_s"], outs["out_s"]), buf, rsem)

    def reduce_step(red, name, ks=(1, 0, 2)):
        for k in ks:
            getattr(red, name)(k)

    def wave(red, name, late):
        c = 1 - p.c if name == "phase0" else p.c
        for core in range(2):
            ks = [(0,), (1, 2)][core ^ late]

            @pl.when(c == core)
            def _(ks=ks):
                reduce_step(red, name, ks)

    loads["lat", 0].wait()
    loads["lat", 1].wait()
    spatial_norm(lat, mod, v["n_s"])
    pl.semaphore_wait(pltpu.get_barrier_semaphore(), expected)
    lat_x.start()
    loads["wq_s"].wait()
    project(v["n_s"], v["wq_s"], v["qkv_s"], (0, 1))
    for pair in range(4):
        spatial_heads(pair, v["qkv_s"], v["probs"], v["sb"], v["turn"])
    v["att_s"][...] = v["turn"][...].T
    att_x.start()
    loads["wo_s"].wait()
    v["mid_s"][...] = block_result(1, flat(lat, 1).astype(F32), mod, 0, v["wo_s"], v["att_s"][256:, :])
    mid_x.start()

    for k in order[4:]:
        loads[k].wait()
    for h2 in range(2):
        temporal_open(h2, cot, mod, v["wo_t"], v["dproj"], v["datt"])
    for h2 in range(2):
        if h2 == 0:
            lat_x.arrive()
            att_x.arrive()
            x = v["lat_in"][...].reshape(256, D).astype(F32)
            att_in = v["att_in"][...].reshape(256, HD)
            mid[0] = block_result(0, x, mod, 0, v["wo_s"], att_in).reshape(FRAMES, 16, D)
        else:
            mid_x.arrive()
        temporal_norm(h2, mod, mid, v["n_t"])
        project(v["n_t"], v["wq_t"], v["qkv_t"], (h2,))
        temporal_heads(h2, v["qkv_t"], v["datt"], v["dqkv"], v["sb"], v["pt"], v["ds"], v["turn"])
        v["dmid_t"][h2] = block_gradient(h2, flat(mid, h2), mod, 1, v["wq_t"], flat(cot, h2), v["dqkv"])
        dmid_x[h2].start()
        temporal_attended(h2, v["qkv_t"], v["pt"], v["turn"], v["att_t"])
    for first in (True, False):
        weight_grads(first, v["n_t"], v["dqkv"], v["dproj"], v["att_t"], g)
        wave(red_t, "phase0", not first)
    store_out = []
    for h2 in range(2):
        y = block_result(h2, flat(mid, h2).astype(F32), mod, 1, v["wo_t"], v["att_t"][span_of(h2), :])
        v["y"][h2] = y.reshape(FRAMES, 16, D)
        store_out.append(pltpu.make_async_copy(v["y"].at[h2], outs["y"].at[:, h2], sem["store"].at[h2]))
        store_out[h2].start()

    for x in (lat_x, att_x, mid_x):
        x.drain()

    for h2 in range(2):
        dmid_x[h2].arrive()
        spatial_back_open(h2, mod, v["wo_s"], dmid, v["dproj"], v["datt"])
    spatial_back_values(v["qkv_s"], v["probs"], v["datt"], v["dqkv"])
    reduce_step(red_t, "phase1")
    red_t.sent0()
    weight_grads(True, v["n_s"], v["dqkv"], v["dproj"], v["att_s"], g)
    wave(red_s, "phase0", 0)
    for pair in range(4):
        if pair == 3:
            reduce_step(red_t, "phase2")
        spatial_back_heads(pair, v["qkv_s"], v["probs"], v["datt"], v["dqkv"], v["sb"], v["ds"], v["turn"])
    v["dqkv"][:, 0:HD] = v["turn"][...].T
    weight_grads(False, v["n_s"], v["dqkv"], v["dproj"], v["att_s"], g)
    wave(red_s, "phase0", 1)
    wave(red_s, "phase1", 0)
    reduce_step(red_t, "phase3")
    lat_grad = mid
    store_grad = []
    for h2 in range(2):
        lat_grad[h2] = block_gradient(h2, flat(lat, h2), mod, 0, v["wq_s"], flat(dmid, h2), v["dqkv"])
        store_grad.append(pltpu.make_async_copy(lat_grad.at[h2], outs["dx"].at[:, h2], sem["store"].at[2 + h2]))
        store_grad[h2].start()

    wave(red_s, "phase1", 1)
    wave(red_s, "phase2", 0)
    reduce_step(red_t, "phase4")
    for x in dmid_x:
        x.drain()
    wave(red_s, "phase2", 1)
    wave(red_s, "phase3", 0)
    for c in store_out + store_grad:
        c.wait()
    wave(red_s, "phase3", 1)
    wave(red_s, "phase4", 0)
    reduce_step(red_t, "phase5")
    wave(red_s, "phase4", 1)
    reduce_step(red_t, "drain")
    reduce_step(red_t, "drain3")
    red_s.sent0()
    reduce_step(red_s, "drain")
    reduce_step(red_s, "phase5")
    reduce_step(red_s, "drain3")


def shape(dims, kind=BF):
    return jax.ShapeDtypeStruct(dims, kind)


def params(collective_id=None):
    if collective_id is None:
        return pltpu.CompilerParams(vmem_limit_bytes=VMEM_LIMIT)
    return pltpu.CompilerParams(
        vmem_limit_bytes=VMEM_LIMIT, collective_id=collective_id, has_side_effects=True
    )


VMEM_LIMIT = 62 * 1024 * 1024
INPUTS = ("lat", "mod", "wq_s", "wo_s", "wq_t", "wo_t", "cot")
OUTPUTS = {
    "y": shape((FRAMES, 2, 16, D)),
    "dx": shape((FRAMES, 2, 16, D)),
    "qkv_s": shape((9, QKV), F32),
    "out_s": shape((9, HD), F32),
    "qkv_t": shape((9, QKV), F32),
    "out_t": shape((9, HD), F32),
}
HALVES = (2, FRAMES, 16, D)
VALUES = {
    "lat": HALVES, "cot": HALVES,
    "wq_s": (QKV, D), "wo_s": (HD, D), "wq_t": (QKV, D), "wo_t": (HD, D),
    "n_s": (TOK, D), "qkv_s": (TOK, QKV), "probs": (HEADS, TOK, TOK), "att_s": (TOK, HD),
    "mid_s": (256, D), "lat_in": HALVES[1:], "att_in": (FRAMES, 16, HD),
    "mid": HALVES, "n_t": (TOK, D), "qkv_t": (TOK, QKV), "att_t": (TOK, HD),
    "dproj": (TOK, D), "datt": (TOK, HD), "dqkv": (TOK, QKV),
    "sb": (2, TOK, TOK), "pt": (2, TOK, TOK), "ds": (2, TOK, TOK), "turn": (HD, TOK),
    "dmid_t": HALVES, "dmid": HALVES, "y": HALVES,
    "g": (PIECES, D, WIDE),
}
KINDS = {"sb": F32}


def run(*args):
    dma = pltpu.SemaphoreType.DMA
    bufs, rsems = reduce_buffers(2)
    sems = {
        "load": dma((8,)), "store": dma((4,)),
        "send": dma((5,)), "recv": dma((5,)),
    }
    values = {k: pltpu.VMEM(d, KINDS.get(k, BF)) for k, d in VALUES.items()}
    groups = (values, sems, bufs, rsems)

    def unpack(*refs):
        refs = list(refs)

        def take(names):
            got = dict(zip(names, refs))
            del refs[: len(got)]
            return got

        kernel(take(INPUTS), take(OUTPUTS), *[take(g) for g in groups])

    return pl.pallas_call(
        unpack,
        out_shape=tuple(OUTPUTS.values()),
        in_specs=[vmem_spec() if k == "mod" else any_spec() for k in INPUTS],
        out_specs=[any_spec()] * 2 + [vmem_spec()] * 4,
        scratch_shapes=[x for g in groups for x in g.values()],
        compiler_params=params(0),
        name="attention_blocks",
    )(*args)


def hand_over(*refs):
    n = (len(refs) - 2) // 3
    sems = refs[-2:]
    ins = [pltpu.make_async_copy(refs[i], refs[2 * n + i], sems[0].at[i]) for i in range(n)]
    outs = [pltpu.make_async_copy(refs[2 * n + i], refs[n + i], sems[1].at[i]) for i in range(n)]
    for c in ins:
        c.start()
    for i in range(n):
        ins[i].wait()
        outs[i].start()
    for c in outs:
        c.wait()


def body(latents, modulation, spatial_qkv, spatial_out, temporal_qkv, temporal_out, cotangent):
    halves = (FRAMES, 2, 16, D)
    results = run(
        latents.reshape(halves), modulation[0].transpose(1, 0, 2), spatial_qkv.T, spatial_out,
        temporal_qkv.T, temporal_out, cotangent.reshape(halves),
    )
    block_out, lat_grad, qkv_s, out_s, qkv_t, out_t = pl.pallas_call(
        hand_over,
        out_shape=tuple(OUTPUTS.values()),
        in_specs=[any_spec()] * 6,
        out_specs=[any_spec()] * 6,
        scratch_shapes=[pltpu.VMEM(x.shape, x.dtype) for x in OUTPUTS.values()]
        + [pltpu.SemaphoreType.DMA((6,))] * 2,
        compiler_params=params(),
        name="hand_over",
    )(*results)
    return (
        block_out.reshape(1, FRAMES, SPAN, D), lat_grad.reshape(1, 1, TOK, D),
        qkv_s, out_s.T, qkv_t, out_t.T,
    )


def solution(mesh):
    return jax.shard_map(
        body,
        mesh=mesh,
        in_specs=(
            P("dp", "seq", None, None),
            P("dp", None, None, None),
            P(),
            P(),
            P(),
            P(),
            P("dp", None, "seq", None),
        ),
        out_specs=(
            P("dp", None, "seq", None),
            P("dp", "seq", None, None),
            P(("dp", "seq"), None),
            P(None, ("dp", "seq")),
            P(("dp", "seq"), None),
            P(None, ("dp", "seq")),
        ),
        check_vma=False,
    )
```
